32 devices in a mesh: dp: 4 (over z), fsdp: 8 (over y, x, core).
Axes of the slice: x: 2, y: 2, z: 4, core: 2. Of those that a mesh axis runs over, the one named last changes fastest.
Arguments:
- layer_input: bfloat16 [4, 2048, 2048], P('dp', 'fsdp'), may hold values from -6 to 6
- doc_starts: int32 [4, 6], P('dp'), may hold values from 0 to 2047, as said below
- norm1_gain: bfloat16 [2048], P(('dp', 'fsdp')), may hold values from 0.099609375 to 1.8984375
- w_query: bfloat16 [2048, 256], P(('dp', 'fsdp')), may hold values from -0.125 to 0.125
- w_key: bfloat16 [2048, 256], P(('dp', 'fsdp')), may hold values from -0.125 to 0.125
- w_value: bfloat16 [2048, 2048], P(('dp', 'fsdp')), may hold values from -0.125 to 0.125
- w_out: bfloat16 [2048, 2048], P(('dp', 'fsdp')), may hold values from -1 to 1
- norm2_gain: bfloat16 [2048], P(('dp', 'fsdp')), may hold values from 0.099609375 to 1.8984375
- w_gate: bfloat16 [2048, 5504], P(('dp', 'fsdp')), may hold values from -0.125 to 0.125
- w_up: bfloat16 [2048, 5504], P(('dp', 'fsdp')), may hold values from -0.125 to 0.125
- w_down: bfloat16 [5504, 2048], P(None, ('dp', 'fsdp')), may hold values from -0.078125 to 0.078125
- cotangent: bfloat16 [4, 2048, 2048], P('dp', 'fsdp'), may hold values from -6 to 6
Outputs:
- out_act: bfloat16 [4, 2048, 2048], P('dp', 'fsdp')
- grad_input: float32 [4, 2048, 2048], P('dp', 'fsdp')
- grad_norm1: float32 [2048], P(('dp', 'fsdp'))
- grad_query: float32 [2048, 256], P(('dp', 'fsdp'))
- grad_key: float32 [2048, 256], P(('dp', 'fsdp'))
- grad_value: float32 [2048, 2048], P(('dp', 'fsdp'))
- grad_out: float32 [2048, 2048], P(('dp', 'fsdp'))
- grad_norm2: float32 [2048], P(('dp', 'fsdp'))
- grad_gate: float32 [2048, 5504], P(('dp', 'fsdp'))
- grad_up: float32 [2048, 5504], P(('dp', 'fsdp'))
- grad_down: float32 [5504, 2048], P(None, ('dp', 'fsdp'))
The draws below stay inside these ranges and needn't reach their ends.
Inputs may be any that keep to these rules, and one draw needn't show every extreme that they name: `doc_starts`: in each row the six starts rise strictly from 0; the second and third are below 256, the last three are 1793 or more, so that one document runs from the row's first device to its last.
All inputs are finite; a program needn't handle non-finite values.
Results may differ from the reference program's by a relative error of at most 0.012.
Values may be sent and summed in bfloat16 or wider, within the bound.
A program may use at most 312 MiB of HBM per device.

```python
import math
import jax
import jax.numpy as jnp
from jax import lax

D = 2048
HEADS = 16
FEAT = 16
FF = 5504
TOK_DEV = 256
LEN = 2048
ROWS = 4


def draw_doc_starts(key, part):
    key = jax.random.fold_in(key, 7)

    def one_row(row_key):
        early_key, late_key = jax.random.split(row_key)
        early = jnp.sort(jax.random.permutation(early_key, TOK_DEV - 1)[:2] + 1)
        late = jnp.sort(jax.random.permutation(late_key, TOK_DEV - 1)[:3] + LEN - TOK_DEV + 1)
        return jnp.concatenate([jnp.zeros((1,), jnp.int32), early.astype(jnp.int32), late.astype(jnp.int32)])
    return jax.vmap(one_row)(jax.random.split(key, ROWS))


def block_levels(own_key, dims, pieces, low, high):
    factor_of = 1.0
    for position, shards_of in pieces:
        heights = jax.random.uniform(jax.random.fold_in(jax.random.fold_in(own_key, 6), position), (shards_of,), jnp.float32, low / len(pieces), high / len(pieces))
        factor_of = factor_of * jnp.repeat(jnp.exp(heights), dims[position] // shards_of).reshape((-1,) + (1,) * (len(dims) - 1 - position))
    return factor_of


def bell_draw(key, shape, spread, bound, shards=(), kind=jnp.bfloat16):
    values = spread * jax.random.normal(key, shape, jnp.float32)
    if shards:
        values = values * block_levels(key, shape, shards, -0.22, 0.18)
    return jnp.clip(values, -bound, bound).astype(kind)


def setup_inputs(seed: int = 0) -> dict:
    streams_of = jax.random.split(jax.random.key(seed), 13)
    return {
        "layer_input": bell_draw(streams_of[0], (ROWS, LEN, D), 1.0, 6.0, ((0, 4), (1, 8))),
        "doc_starts": draw_doc_starts(jax.random.fold_in(streams_of[12], 71), 0),
        "norm1_gain": jnp.clip(1.0 + 0.18 * jax.random.normal(streams_of[2], (D,), jnp.float32), 0.099609375, 1.8984375).astype(jnp.bfloat16),
        "w_query": bell_draw(streams_of[3], (D, HEADS * FEAT), D ** -0.5, 0.125, ((0, 32),)),
        "w_key": bell_draw(streams_of[4], (D, HEADS * FEAT), D ** -0.5, 0.125, ((0, 32),)),
        "w_value": bell_draw(streams_of[5], (D, D), D ** -0.5, 0.125, ((0, 32),)),
        "w_out": bell_draw(streams_of[6], (D, D), (D // 64) ** -0.5, 1.0, ((0, 32),)),
        "norm2_gain": jnp.clip(1.0 + 0.18 * jax.random.normal(streams_of[7], (D,), jnp.float32), 0.099609375, 1.8984375).astype(jnp.bfloat16),
        "w_gate": bell_draw(streams_of[8], (D, FF), D ** -0.5, 0.125, ((0, 32),)),
        "w_up": bell_draw(streams_of[9], (D, FF), D ** -0.5, 0.125, ((0, 32),)),
        "w_down": bell_draw(streams_of[10], (FF, D), FF ** -0.5, 0.078125, ((1, 32),)),
        "cotangent": bell_draw(streams_of[11], (ROWS, LEN, D), 1.0, 6.0, ((0, 4), (1, 8))),
    }


EPS = 1e-05
HI = lax.Precision.HIGHEST

@jax.custom_vjp
def low(v):
    return lax.optimization_barrier(v.astype(jnp.bfloat16)).astype(jnp.float32)

@jax.custom_vjp
def low_back(v):
    return v

def low_keep(v):
    return (low(v), None)

def low_pass(kept, grad):
    return (grad,)

def back_keep(v):
    return (v, None)

def back_low(kept, grad):
    return (low(grad),)
low.defvjp(low_keep, low_pass)
low_back.defvjp(back_keep, back_low)

def taylor(vector):
    feat = vector.shape[-1]
    linear = vector / feat ** 0.25
    square = (vector[..., :, None] * vector[..., None, :]).reshape(vector.shape[:-1] + (feat * feat,))
    square = square / math.sqrt(2.0 * feat)
    ones = jnp.ones(vector.shape[:-1] + (1,), vector.dtype)
    return jnp.concatenate([ones, linear, square], -1)

def rms_norm(values, gain):
    return values * lax.rsqrt(lax.optimization_barrier(jnp.mean(values * values, -1, keepdims=True)) + EPS) * gain

def head_attend(item):
    feat_query, feat_key, head_values, segment = item
    length = segment.shape[0]
    places = jnp.arange(length, dtype=jnp.int32)
    masking = ((segment[:, None] == segment[None, :]) & (places[None, :] <= places[:, None])).astype(feat_query.dtype)
    weights = jnp.dot(feat_query, feat_key.T, precision=HI) * masking
    numer = jnp.dot(weights, head_values, precision=HI)
    denom = lax.optimization_barrier(jnp.sum(weights, 1))
    return numer / denom[:, None]

def project(left, right):
    return jnp.einsum('rtd,de->rte', left, right, precision=HI)

def forward(inputs, segments, gain_one, query_w, key_w, value_w, out_w, gain_two, gate_w, up_w, down_w):
    rows, length, width = inputs.shape
    head_width = width // HEADS
    act_one = low(rms_norm(inputs, gain_one))
    queries = low_back(project(act_one, query_w))
    keys = low_back(project(act_one, key_w))
    feat_query = low(taylor(queries.reshape(rows, length, HEADS, FEAT)))
    feat_key = low(taylor(keys.reshape(rows, length, HEADS, FEAT)))
    values = low(low_back(project(act_one, value_w))).reshape(rows, length, HEADS, head_width)

    def by_head(tensor):
        return jnp.transpose(tensor, (0, 2, 1, 3)).reshape(rows * HEADS, length, tensor.shape[-1])
    seg_heads = jnp.repeat(segments, HEADS, axis=0)
    attended = lax.map(jax.checkpoint(head_attend), (by_head(feat_query), by_head(feat_key), by_head(values), seg_heads))
    attended = jnp.transpose(attended.reshape(rows, HEADS, length, head_width), (0, 2, 1, 3)).reshape(rows, length, width)
    attended = low(low_back(attended))
    resid = inputs + low_back(project(attended, out_w))
    act_two = low(rms_norm(resid, gain_two))
    gate_pre = low_back(project(act_two, gate_w))
    upward = low_back(project(act_two, up_w))
    hidden = low(jax.nn.silu(gate_pre) * upward)
    return resid + project(hidden, down_w)

def reference(layer_input, doc_starts, norm1_gain, w_query, w_key, w_value, w_out, norm2_gain, w_gate, w_up, w_down, cotangent):
    length = layer_input.shape[1]
    places = jnp.arange(length, dtype=jnp.int32)
    segments = lax.optimization_barrier(jnp.sum((doc_starts[:, None, :] <= places[None, :, None]).astype(jnp.int32), -1)).astype(jnp.int32)
    floats = [t.astype(jnp.float32) for t in (layer_input, norm1_gain, w_query, w_key, w_value, w_out, norm2_gain, w_gate, w_up, w_down)]

    def whole(*params):
        return forward(params[0], segments, *params[1:])
    result, pullback = jax.vjp(whole, *floats)
    grads = pullback(cotangent.astype(jnp.float32))
    return (result.astype(jnp.bfloat16), grads[0], grads[1], grads[2], grads[3], grads[4], grads[5], grads[6], grads[7], grads[8], grads[9])
```

```python
import functools

import jax
import jax.numpy as jnp
from jax import lax
from jax.experimental import pallas as pl
from jax.experimental.pallas import tpu as pltpu
from jax.sharding import PartitionSpec as P

FEAT = 16
EPS = 1e-05
BLK = 256
F32 = jnp.float32
BF16 = jnp.bfloat16
NT = (((1,), (1,)), ((), ()))
TN = (((0,), (0,)), ((), ()))
VMEM = pltpu.VMEM
ALL = ("dp", "fsdp")


def dot(a, b):
    return jnp.dot(a, b, preferred_element_type=F32)


def dot_nt(a, b):
    return lax.dot_general(a, b, NT, preferred_element_type=F32)


def dot_tn(a, b):
    return lax.dot_general(a, b, TN, preferred_element_type=F32)


def rms_apply(values, gain):
    factor = lax.rsqrt(jnp.mean(values * values, -1, keepdims=True) + EPS)
    return values * factor * gain, factor


def rms_back(grad, values, factor, gain):
    normed = values * factor
    grad_gain = jnp.sum(grad * normed, 0)
    inner = grad * gain
    grad_in = factor * (inner - normed * jnp.mean(inner * normed, -1, keepdims=True))
    return grad_in, grad_gain


def pair_mask(seg_rows, seg_cols, block, other):
    rows = lax.broadcasted_iota(jnp.int32, (BLK, BLK), 0) + block * BLK
    cols = lax.broadcasted_iota(jnp.int32, (BLK, BLK), 1) + other * BLK
    return (seg_rows == seg_cols) & (cols <= rows)


def attend_kernel(heads, wide, q_ref, k_ref, v_ref, sc_ref, sr_ref, att_ref, full_ref, den_ref):
    block = pl.program_id(0)
    seg_rows = sc_ref[...]
    for h in range(heads):
        feat = slice(h * FEAT, (h + 1) * FEAT)
        entry = slice(h * wide, (h + 1) * wide)
        q = q_ref[:, feat]

        def step(c, carry):
            num, den = carry
            here = pl.ds(pl.multiple_of(c * BLK, BLK), BLK)
            x = dot_nt(q, k_ref[here, feat]) * 0.25
            w = jnp.where(pair_mask(seg_rows, sr_ref[c], block, c), 1.0 + x + 0.5 * x * x, 0.0)
            num = num + dot(w.astype(BF16), v_ref[here, entry])
            return num, den + jnp.sum(w, 1, keepdims=True)

        num, den = lax.fori_loop(
            0, block + 1, step, (jnp.zeros((BLK, wide), F32), jnp.zeros((BLK, 1), F32))
        )
        att = num / den
        att_ref[:, entry] = att.astype(BF16)
        full_ref[:, entry] = att
        den_ref[:, h : h + 1] = den


def attend_back_kernel(
    heads, wide, blocks, q_ref, k_ref, v_ref, sc_ref, sr_ref, da_ref, full_ref, den_ref,
    dq_ref, dk_ref, dv_ref, dk_acc, dv_acc,
):
    block = pl.program_id(0)
    seg_rows = sc_ref[...]

    @pl.when(block == 0)
    def _():
        dk_acc[...] = jnp.zeros_like(dk_acc)
        dv_acc[...] = jnp.zeros_like(dv_acc)

    for h in range(heads):
        feat = slice(h * FEAT, (h + 1) * FEAT)
        entry = slice(h * wide, (h + 1) * wide)
        q = q_ref[:, feat]
        inv = 1.0 / den_ref[:, h : h + 1]
        da = da_ref[:, entry].astype(F32)
        dn = (da * inv).astype(BF16)
        dd = -jnp.sum(da * full_ref[:, entry], 1, keepdims=True) * inv

        def step(c, dq):
            here = pl.ds(pl.multiple_of(c * BLK, BLK), BLK)
            k = k_ref[here, feat]
            x = dot_nt(q, k) * 0.25
            mask = pair_mask(seg_rows, sr_ref[c], block, c)
            slope = 1.0 + x
            w = jnp.where(mask, slope + 0.5 * x * x, 0.0).astype(BF16)
            dw = dot_nt(dn, v_ref[here, entry]) + dd
            ds = jnp.where(mask, dw * slope * 0.25, 0.0).astype(BF16)
            dv_acc[here, entry] += dot_tn(w, dn)
            dk_acc[here, feat] += dot_tn(ds, q)
            return dq + dot(ds, k)

        dq_ref[:, feat] = lax.fori_loop(
            0, block + 1, step, jnp.zeros((BLK, FEAT), F32)
        ).astype(BF16)

    @pl.when(block == blocks - 1)
    def _():
        dk_ref[...] = dk_acc[...].astype(BF16)
        dv_ref[...] = dv_acc[...].astype(BF16)


def per_block(lanes):
    return pl.BlockSpec((BLK, lanes), lambda b: (b, 0))


def attend(q, k, v, seg):
    length, width = v.shape
    heads = q.shape[1] // FEAT
    blocks = length // BLK
    sc = seg[:, None]
    sr = seg.reshape(blocks, 1, BLK)
    whole = pl.BlockSpec(memory_space=VMEM)
    return pl.pallas_call(
        functools.partial(attend_kernel, heads, width // heads),
        grid=(blocks,),
        out_shape=(
            jax.ShapeDtypeStruct((length, width), BF16),
            jax.ShapeDtypeStruct((length, width), F32),
            jax.ShapeDtypeStruct((length, heads), F32),
        ),
        in_specs=[per_block(heads * FEAT), whole, whole, per_block(1), whole],
        out_specs=(per_block(width), per_block(width), per_block(heads)),
        compiler_params=pltpu.CompilerParams(vmem_limit_bytes=32 << 20),
        cost_estimate=pl.CostEstimate(
            flops=heads * length * length * 300, bytes_accessed=length * width * 8, transcendentals=0
        ),
    )(q, k, v, sc, sr)


def attend_back(q, k, v, seg, da, full, den):
    length, width = v.shape
    heads = q.shape[1] // FEAT
    blocks = length // BLK
    sc = seg[:, None]
    sr = seg.reshape(blocks, 1, BLK)
    whole = pl.BlockSpec(memory_space=VMEM)
    return pl.pallas_call(
        functools.partial(attend_back_kernel, heads, width // heads, blocks),
        grid=(blocks,),
        out_shape=(
            jax.ShapeDtypeStruct((length, heads * FEAT), BF16),
            jax.ShapeDtypeStruct((length, heads * FEAT), BF16),
            jax.ShapeDtypeStruct((length, width), BF16),
        ),
        in_specs=[per_block(heads * FEAT), whole, whole, per_block(1), whole, per_block(width),
                  per_block(width), per_block(heads)],
        out_specs=(per_block(heads * FEAT), whole, whole),
        scratch_shapes=[VMEM((length, heads * FEAT), F32), VMEM((length, width), F32)],
        compiler_params=pltpu.CompilerParams(vmem_limit_bytes=40 << 20),
        cost_estimate=pl.CostEstimate(
            flops=heads * length * length * 700, bytes_accessed=length * width * 14, transcendentals=0
        ),
    )(q, k, v, sc, sr, da, full, den)


def swap(parts, axis="fsdp"):
    return lax.all_to_all(parts, axis, 1, 0, tiled=True)


def group_columns(arrays, groups):
    return jnp.concatenate([a.reshape(a.shape[0], groups, -1) for a in arrays], -1).reshape(
        arrays[0].shape[0], -1
    )


def split_groups(array, groups, widths):
    parts = array.reshape(array.shape[0], groups, -1)
    out, at = [], 0
    for w in widths:
        out.append(parts[:, :, at : at + w].reshape(array.shape[0], groups * w))
        at += w
    return out


def on_device(
    layer_input, doc_starts, norm1_gain, w_query, w_key, w_value, w_out, norm2_gain,
    w_gate, w_up, w_down, cotangent,
):
    n_f, n_d = lax.axis_size("fsdp"), lax.axis_size("dp")
    x = layer_input[0].astype(F32)
    cot = cotangent[0]
    tokens, width = x.shape
    length = tokens * n_f
    kv = w_query.shape[1]
    rows = w_query.shape[0]
    ff = w_gate.shape[1]
    ff_own = ff // n_f
    qk_own, v_own = kv // n_f, width // n_f

    gains = jnp.stack([norm1_gain, norm2_gain], 1)
    pad = jnp.zeros((rows, 126), BF16)
    mats = lax.all_gather(
        jnp.concatenate([w_query, w_key, w_value, gains, pad], 1), ALL, axis=0, tiled=True
    )
    out_full = lax.all_gather(w_out, ALL, axis=0, tiled=True)
    w_qkv = mats[:, : 2 * kv + width]
    gain_one = mats[:, 2 * kv + width].astype(F32)
    gain_two = mats[:, 2 * kv + width + 1].astype(F32)
    ffn = lax.all_gather(swap(group_columns([w_gate, w_up, w_down.T], n_f)), "dp", axis=0, tiled=True)
    w_gu, w_dt = ffn[:, : 2 * ff_own], ffn[:, 2 * ff_own :]
    cot_all = lax.all_gather(cot, "fsdp", axis=0, tiled=True)

    places = jnp.arange(length, dtype=jnp.int32)
    seg = jnp.sum((doc_starts[0][None, :] <= places[:, None]).astype(jnp.int32), 1)

    normed_one, factor_one = rms_apply(x, gain_one)
    act_one = normed_one.astype(BF16)
    qkv = dot(act_one, w_qkv).astype(BF16)
    q, k, v = qkv[:, :kv], qkv[:, kv : 2 * kv], qkv[:, 2 * kv :]
    own = swap(group_columns([q, k, v], n_f))
    q_own, k_own, val_own = own[:, :qk_own], own[:, qk_own : 2 * qk_own], own[:, 2 * qk_own :]
    att_own, full_own, den_own = attend(q_own, k_own, val_own, seg)
    mixed = lax.all_to_all(att_own, "fsdp", 0, 1, tiled=True)
    resid = x + dot(mixed, out_full)
    normed_two, factor_two = rms_apply(resid, gain_two)
    act_two = lax.all_gather(normed_two.astype(BF16), "fsdp", axis=0, tiled=True)

    gate_up = dot(act_two, w_gu)
    gate, up = gate_up[:, :ff_own], gate_up[:, ff_own:]
    sigma = jax.nn.sigmoid(gate)
    swish = gate * sigma
    hidden = (swish * up).astype(BF16)
    out_part = dot_nt(hidden, w_dt).astype(BF16)
    out_sum = lax.psum_scatter(out_part, "fsdp", scatter_dimension=0, tiled=True)
    output = (resid + out_sum.astype(F32)).astype(BF16)[None]

    d_hidden = dot(cot_all, w_dt)
    d_gate = (d_hidden * up * sigma * (1.0 + gate * (1.0 - sigma))).astype(BF16)
    d_up = (d_hidden * swish).astype(BF16)
    d_gu = jnp.concatenate([d_gate, d_up], 1)
    d_act_two_part = dot_nt(d_gu, w_gu).astype(BF16)
    d_act_two = lax.psum_scatter(d_act_two_part, "fsdp", scatter_dimension=0, tiled=True).astype(F32)
    g_ffn = jnp.concatenate([dot_tn(act_two, d_gu).astype(BF16), dot_tn(cot_all, hidden).astype(BF16)], 1)
    g_ffn = lax.psum_scatter(g_ffn, "dp", scatter_dimension=0, tiled=True)
    g_ffn = lax.all_to_all(g_ffn, "fsdp", 0, 1, tiled=True)
    grad_gate, grad_up, grad_dt = [
        g.astype(F32) for g in split_groups(g_ffn, n_f, [ff_own] * 3)
    ]

    d_norm, gain_two_term = rms_back(d_act_two, resid, factor_two, gain_two)
    d_resid = cot.astype(F32) + d_norm
    d_proj = d_resid.astype(BF16)
    out_term = dot_tn(mixed, d_proj).astype(BF16)
    grad_out = lax.psum_scatter(out_term, ALL, scatter_dimension=0, tiled=True).astype(F32)
    d_att = swap(dot_nt(d_proj, out_full).astype(BF16))
    dq, dk, dv = attend_back(q_own, k_own, val_own, seg, d_att, full_own, den_own)
    back = lax.all_to_all(jnp.concatenate([dq, dk, dv], 1), "fsdp", 0, 1, tiled=True)
    d_qkv = jnp.concatenate(split_groups(back, n_f, [qk_own, qk_own, v_own]), 1)
    d_act_one = dot_nt(d_qkv, w_qkv)
    d_norm, gain_one_term = rms_back(d_act_one, x, factor_one, gain_one)
    grad_input = (d_resid + d_norm)[None]
    terms = jnp.concatenate(
        [
            dot_tn(act_one, d_qkv).astype(BF16),
            gain_one_term[:, None].astype(BF16),
            gain_two_term[:, None].astype(BF16),
            jnp.zeros((width, 126), BF16),
        ],
        1,
    )
    grads = lax.psum_scatter(terms, ALL, scatter_dimension=0, tiled=True).astype(F32)
    return (
        output,
        grad_input,
        grads[:, 2 * kv + width],
        grads[:, :kv],
        grads[:, kv : 2 * kv],
        grads[:, 2 * kv : 2 * kv + width],
        grad_out,
        grads[:, 2 * kv + width + 1],
        grad_gate,
        grad_up,
        grad_dt.T,
    )


def solution(mesh):
    rows, cols = P(ALL, None), P(None, ALL)
    toks = P("dp", "fsdp", None)
    return jax.shard_map(
        on_device,
        mesh=mesh,
        in_specs=(toks, P("dp", None), P(ALL), rows, rows, rows, rows, P(ALL), rows, rows, cols, toks),
        out_specs=(toks, toks, P(ALL), rows, rows, rows, rows, P(ALL), rows, rows, cols),
        check_vma=False,
    )
```

```python
import functools

import jax
import jax.numpy as jnp
from jax import lax
from jax.experimental import pallas as pl
from jax.experimental.pallas import tpu as pltpu
from jax.sharding import PartitionSpec as P

FEAT = 16
EPS = 1e-05
BLK = 256
F32 = jnp.float32
BF16 = jnp.bfloat16
NT = (((1,), (1,)), ((), ()))
TN = (((0,), (0,)), ((), ()))
VMEM = pltpu.VMEM
ALL = ("dp", "fsdp")
MESH = pl.DeviceIdType.MESH


def dot(a, b):
    return jnp.dot(a, b, preferred_element_type=F32)


def dot_nt(a, b):
    return lax.dot_general(a, b, NT, preferred_element_type=F32)


def dot_tn(a, b):
    return lax.dot_general(a, b, TN, preferred_element_type=F32)


def rms_apply(values, gain):
    factor = lax.rsqrt(jnp.mean(values * values, -1, keepdims=True) + EPS)
    return values * factor * gain, factor


def rms_back(grad, values, factor, gain):
    normed = values * factor
    grad_gain = jnp.sum(grad * normed, 0)
    inner = grad * gain
    grad_in = factor * (inner - normed * jnp.mean(inner * normed, -1, keepdims=True))
    return grad_in, grad_gain


def neighbours():
    me = lax.axis_index("fsdp")
    core, side, line = lax.rem(me, 2), lax.rem(me // 2, 2), me // 4

    def at(y, x, c):
        return 4 * y + 2 * x + c

    return (
        me,
        at(line, side, 1 - core),
        at(line, 1 - side, core),
        at(1 - line, side, core),
        at(1 - line, 1 - side, core),
        1 - 2 * core,
    )


def greet(others):
    barrier = pltpu.get_barrier_semaphore()
    for other in others:
        pl.semaphore_signal(barrier, inc=1, device_id={"fsdp": other}, device_id_type=MESH)
    pl.semaphore_wait(barrier, len(others))


def push(src, dst, send, recv, to):
    return pltpu.make_async_remote_copy(
        src_ref=src, dst_ref=dst, send_sem=send, recv_sem=recv,
        device_id={"fsdp": to}, device_id_type=MESH,
    )


class Gather:
    COPIES = 13

    def __init__(self, x_ref, o_ref, send, recv, local):
        me, sib, xn, yn, dg, _ = neighbours()
        half = x_ref.shape[0] // 2
        lo, hi = pl.ds(0, half), pl.ds(half, half)

        def own(part, to, k):
            return push(x_ref.at[part], o_ref.at[me, part], send.at[k], recv.at[k], to)

        def on(who, part, to, k):
            spot = o_ref.at[who, part]
            return push(spot, spot, send.at[k], recv.at[k], to)

        self.keep = pltpu.make_async_copy(x_ref, o_ref.at[me], local)
        self.x_hi, self.y_lo = own(hi, xn, 0), own(lo, yn, 1)
        self.x_lo, self.y_hi = own(lo, xn, 2), own(hi, yn, 3)
        self.whole = push(x_ref, o_ref.at[me], send.at[4], recv.at[4], sib)
        self.over_x, self.over_y = on(yn, lo, xn, 5), on(xn, hi, yn, 7)
        self.core = [
            on(yn, lo, sib, 6), on(xn, hi, sib, 8), on(xn, lo, sib, 9),
            on(yn, hi, sib, 10), on(dg, lo, sib, 11), on(dg, hi, sib, 12),
        ]

    def start(self):
        self.keep.start()
        for copy in (self.x_hi, self.y_lo, self.x_lo, self.y_hi, self.whole):
            copy.start()

    def turn(self):
        self.y_lo.wait_recv()
        self.over_x.start()
        self.core[0].start()
        self.x_hi.wait_recv()
        self.over_y.start()
        self.core[1].start()

    def rest(self):
        self.x_lo.wait_recv()
        self.core[2].start()
        self.y_hi.wait_recv()
        self.core[3].start()

    def across(self):
        self.over_x.wait_recv()
        self.core[4].start()
        self.over_y.wait_recv()
        self.core[5].start()

    def finish(self):
        self.whole.wait_recv()
        for copy in self.core:
            copy.wait_recv()
        self.close()

    def close(self):
        for copy in [self.x_hi, self.y_lo, self.x_lo, self.y_hi, self.whole, self.over_x, self.over_y] + self.core:
            copy.wait_send()
        self.keep.wait()


def gather_scratch():
    dma = pltpu.SemaphoreType.DMA
    return [dma((Gather.COPIES,)), dma((Gather.COPIES,)), dma(())]


def gather_kernel(x_ref, o_ref, send, recv, local):
    _, sib, xn, yn, _, _ = neighbours()
    greet([sib, xn, yn])
    g = Gather(x_ref, o_ref, send, recv, local)
    g.start()
    g.turn()
    g.rest()
    g.across()
    g.finish()


ANY = pl.BlockSpec(memory_space=pl.ANY)
LINKED = pl.CostEstimate(flops=45 * 10**9, bytes_accessed=10**8, transcendentals=0)
WHOLE = pl.BlockSpec(memory_space=VMEM)


def row_gather(x, cid):
    rows, cols = x.shape
    return pl.pallas_call(
        gather_kernel,
        out_shape=jax.ShapeDtypeStruct((8, rows, cols), x.dtype),
        in_specs=[ANY],
        out_specs=ANY,
        scratch_shapes=gather_scratch(),
        compiler_params=pltpu.CompilerParams(collective_id=cid, has_side_effects=True),
        cost_estimate=LINKED,
        name="row_gather",
    )(x).reshape(8 * rows, cols)


class Sum:
    COPIES = 10

    def __init__(self, mine, got, away, ex, ey, fx, fy, total, send, recv):
        me, sib, xn, yn, dg, self.flip = neighbours()
        half = fx.shape[0] // 2
        self.lo, self.hi = lo, hi = pl.ds(0, half), pl.ds(half, half)
        self.order = [dg, xn, yn, me]
        self.mine, self.got, self.ex, self.ey, self.fx, self.fy, self.total = mine, got, ex, ey, fx, fy, total
        self.swaps = [push(away(k), got.at[k], send.at[k], recv.at[k], sib) for k in range(4)]
        self.a = push(mine.at[0, lo], ey, send.at[4], recv.at[4], yn)
        self.b = push(mine.at[0, hi], ex, send.at[5], recv.at[5], xn)
        self.c = push(mine.at[1, hi], fx.at[hi], send.at[6], recv.at[6], xn)
        self.d = push(mine.at[2, lo], fy.at[lo], send.at[7], recv.at[7], yn)
        self.e = push(mine.at[1, lo], fx.at[lo], send.at[8], recv.at[8], xn)
        self.f = push(mine.at[2, hi], fy.at[hi], send.at[9], recv.at[9], yn)

    def add(self, k, part, more=None):
        value = self.mine[k, part].astype(F32) + self.got[k, part].astype(F32)
        if more is not None:
            value = value + more[...].astype(F32)
        self.mine[k, part] = value.astype(BF16)

    def over(self):
        self.swaps[0].wait_recv()
        self.add(0, self.lo)
        self.a.start()
        self.add(0, self.hi)
        self.b.start()

    def along_x(self):
        self.swaps[1].wait_recv()
        self.add(1, self.hi)
        self.c.start()

    def along_y(self):
        self.swaps[2].wait_recv()
        self.add(2, self.lo)
        self.d.start()

    def second(self):
        self.a.wait_recv()
        self.add(1, self.lo, self.ey)
        self.e.start()
        self.b.wait_recv()
        self.add(2, self.hi, self.ex)
        self.f.start()

    def own(self):
        self.swaps[3].wait_recv()
        self.total[...] = self.mine[3].astype(F32) + self.got[3].astype(F32)

    def finish(self):
        for copy in (self.c, self.d, self.e, self.f):
            copy.wait_recv()
        self.total[...] += self.fx[...].astype(F32) + self.fy[...].astype(F32)
        for copy in self.swaps + [self.a, self.b, self.c, self.d, self.e, self.f]:
            copy.wait_send()


def sum_scratch(rows, cols):
    dma = pltpu.SemaphoreType.DMA
    return [
        VMEM((4, rows, cols), BF16), VMEM((4, rows, cols), BF16), VMEM((rows // 2, cols), BF16),
        VMEM((rows // 2, cols), BF16), VMEM((rows, cols), BF16), VMEM((rows, cols), BF16),
        dma((Sum.COPIES,)), dma((Sum.COPIES,)),
    ]


def product_sum_kernel(turned, l_ref, r_ref, o_ref, out, mine, got, ex, ey, fx, fy, send, recv):
    _, sib, xn, yn, _, _ = neighbours()
    rows, cols = o_ref.shape
    greet([sib, xn, yn])
    s = Sum(mine, got, out.at.__getitem__, ex, ey, fx, fy, o_ref, send, recv)

    def block(q, to):
        left = l_ref[pl.ds(pl.multiple_of(q * rows, rows), rows), :]

        @pl.loop(0, cols // 256)
        def _(n):
            here = pl.ds(pl.multiple_of(n * 256, 256), 256)
            part = dot_nt(left, r_ref[here, :]) if turned else dot(left, r_ref[:, here])
            to[:, here] = part.astype(BF16)

    def away(k):
        block(s.order[k] + s.flip, out.at[k])
        s.swaps[k].start()

    def home(k):
        block(s.order[k], mine.at[k])

    away(0)
    home(0)
    away(1)
    s.over()
    home(1)
    s.along_x()
    away(2)
    home(2)
    s.along_y()
    away(3)
    s.second()
    home(3)
    s.own()
    s.finish()


def product_sum(left, right, turned, cid):
    if lax.axis_size("fsdp") != 8:
        part = (dot_nt(left, right) if turned else dot(left, right)).astype(BF16)
        return lax.psum_scatter(part, "fsdp", scatter_dimension=0, tiled=True).astype(F32)
    rows, cols = left.shape[0] // 8, right.shape[0 if turned else 1]
    return pl.pallas_call(
        functools.partial(product_sum_kernel, turned),
        out_shape=jax.ShapeDtypeStruct((rows, cols), F32),
        in_specs=[WHOLE, WHOLE],
        out_specs=WHOLE,
        scratch_shapes=[VMEM((4, rows, cols), BF16)] + sum_scratch(rows, cols),
        compiler_params=pltpu.CompilerParams(
            collective_id=cid, has_side_effects=True, vmem_limit_bytes=56 << 20
        ),
        cost_estimate=LINKED,
        name="product_sum",
    )(left, right)


def start_kernel(x_ref, a_ref, ox_ref, oa_ref, send, recv, local, a_send, a_recv, keep):
    me = lax.axis_index("fsdp")
    others = [lax.rem(me + r, 8) for r in range(1, 8)]
    greet(others)
    g = Gather(x_ref, ox_ref, send, recv, local)
    g.start()
    moves = []
    for r, to in enumerate(others):
        moves.append(push(a_ref.at[to], oa_ref.at[me], a_send.at[r], a_recv.at[r], to))
    stay = [pltpu.make_async_copy(a_ref.at[me], oa_ref.at[me], keep)]
    for copy in moves + stay:
        copy.start()
    g.turn()
    g.rest()
    g.across()
    g.finish()
    for copy in moves + stay:
        copy.wait()


def start_exchange(x, a, cid):
    if lax.axis_size("fsdp") != 8:
        return (
            lax.all_gather(x, "fsdp", axis=0, tiled=True),
            lax.all_to_all(a, "fsdp", 0, 0, tiled=True),
        )
    dma = pltpu.SemaphoreType.DMA
    x_all, a = pl.pallas_call(
        start_kernel,
        out_shape=(
            jax.ShapeDtypeStruct((8,) + x.shape, x.dtype),
            jax.ShapeDtypeStruct(a.shape, a.dtype),
        ),
        in_specs=[ANY] * 2,
        out_specs=(ANY,) * 2,
        scratch_shapes=gather_scratch() + [dma((7,))] * 2 + [dma(())],
        compiler_params=pltpu.CompilerParams(collective_id=cid, has_side_effects=True),
        cost_estimate=LINKED,
        name="start_exchange",
    )(x, a)
    return x_all.reshape(-1, x.shape[1]), a


def same_or_later(seg_rows, seg_cols):
    rows = lax.broadcasted_iota(jnp.int32, (BLK, BLK), 0)
    cols = lax.broadcasted_iota(jnp.int32, (BLK, BLK), 1)
    return (seg_rows == seg_cols) & (cols <= rows)


def spot(b):
    return pl.ds(b * BLK, BLK)


def moving(c):
    return pl.ds(pl.multiple_of(c * BLK, BLK), BLK)


def lanes_of(h, heads):
    lane = lax.broadcasted_iota(jnp.int32, (BLK, 128), 1)
    at = (heads + h) * FEAT
    return (lane >= at) & (lane < at + FEAT)


def lay_out(heads, wide, blocks, qkv_ref, edge_ref, qz, vx):
    first = (lax.broadcasted_iota(jnp.int32, (BLK, wide), 1) == 0).astype(F32)

    @pl.loop(0, blocks)
    def _(b):
        here = moving(b)
        tile = qkv_ref[here, heads * wide :].astype(F32)
        turned = pltpu.roll(tile, heads * FEAT, 1) * 0.25
        edge = edge_ref[here, :]
        for h in range(heads):
            qz[b, h * BLK : (h + 1) * BLK, :] = jnp.where(lanes_of(h, heads), turned, 0.0).astype(BF16)
            vx[h, here, :wide] = (qkv_ref[here, h * wide : (h + 1) * wide].astype(F32) * edge).astype(BF16)
            vx[h, here, wide:] = (first * edge).astype(BF16)


def attend_kernel(heads, wide, blocks, qkv_ref, sc_ref, sr_ref, edge_ref, att_ref, full_ref, den_ref, qz, vx):
    lay_out(heads, wide, blocks, qkv_ref, edge_ref, qz, vx)
    one = (lax.broadcasted_iota(jnp.int32, (BLK, wide), 1) == 0).astype(BF16)
    for b in range(blocks):
        here = spot(b)

        def weigh(c):
            s = dot_nt(qz[b], qkv_ref[c, heads * wide :]) + 1.0
            return s * s + 1.0

        def step(c, sums):
            at = moving(c)
            w = weigh(at).astype(BF16)
            return tuple(
                sums[h] + dot(w[h * BLK : (h + 1) * BLK], vx[h, at, :]) for h in range(heads)
            )

        sums = lax.fori_loop(0, b, step, (jnp.zeros((BLK, 2 * wide), F32),) * heads)
        if b == blocks - 1:
            sums = tuple(s * edge_ref[here, :] for s in sums)
        mask = same_or_later(sc_ref[here, :], sr_ref[b])
        w = weigh(here)
        for h in range(heads):
            entry = slice(h * wide, (h + 1) * wide)
            near = jnp.where(mask, w[h * BLK : (h + 1) * BLK], 0.0).astype(BF16)
            value = jnp.concatenate([qkv_ref[here, entry], one], 1)
            total = sums[h] + dot(near, value)
            den = total[:, wide : wide + 1]
            att = total[:, :wide] / den
            att_ref[here, entry] = att.astype(BF16)
            full_ref[here, entry] = att
            den_ref[here, h : h + 1] = den


def attend_back_kernel(heads, wide, blocks, with_sum, *refs):
    qkv_ref, sc_ref, sr_ref, edge_ref, da_ref, full_ref, den_ref = refs[:7]
    refs = refs[7:]
    if with_sum:
        part_ref, d_ref, o_ref, qz, vx, near_dn, far_dn, qk_acc, v_acc = refs[:9]
        mine, got, ex, ey, fx, fy, send, recv, local = refs[9:]
        _, sib, xn, yn, _, flip = neighbours()
        greet([sib, xn, yn])
        s = Sum(
            mine, got, lambda k: part_ref.at[neighbours()[(4, 2, 3, 0)[k]] + flip], ex, ey, fx, fy, o_ref, send, recv
        )
        loads = [pltpu.make_async_copy(part_ref.at[s.order[k]], mine.at[k], local.at[k]) for k in range(4)]
        for k in range(4):
            s.swaps[k].start()
            loads[k].start()

        def first():
            loads[0].wait()
            s.over()

        def second():
            loads[1].wait()
            s.along_x()
            loads[2].wait()
            s.along_y()

        def fourth():
            loads[3].wait()
            s.own()

        turns = {blocks - 1: first, blocks - 2: second, blocks - 3: s.second, blocks - 4: fourth}
    else:
        d_ref, qz, vx, near_dn, far_dn, qk_acc, v_acc = refs
        turns = {}
    lay_out(heads, wide, blocks, qkv_ref, edge_ref, qz, vx)
    qk_acc[...] = jnp.zeros_like(qk_acc)
    v_acc[...] = jnp.zeros_like(v_acc)
    one = (lax.broadcasted_iota(jnp.int32, (BLK, wide), 1) == 0).astype(F32)
    unit = one.astype(BF16)
    for b in reversed(range(blocks)):
        here = spot(b)
        for h in range(heads):
            entry = slice(h * wide, (h + 1) * wide)
            inv = 1.0 / den_ref[here, h : h + 1]
            da = da_ref[here, entry].astype(F32)
            dn = da * inv
            dd = -jnp.sum(dn * full_ref[here, entry], 1, keepdims=True)
            rows = slice(h * BLK, (h + 1) * BLK)
            near_dn[rows, :wide] = dn.astype(BF16)
            near_dn[rows, wide:] = (dd * one).astype(BF16)
            if b == blocks - 1:
                edge = edge_ref[here, :]
                far_dn[rows, :wide] = (dn * edge).astype(BF16)
                far_dn[rows, wide:] = (dd * edge * one).astype(BF16)

        far = far_dn if b == blocks - 1 else near_dn

        def pair(c, grads, values, mask):
            keys = qkv_ref[c, heads * wide :]
            t = dot_nt(qz[b], keys) + 1.0
            out, parts = [], []
            for h in range(heads):
                rows = slice(h * BLK, (h + 1) * BLK)
                t_h = t[rows]
                w = t_h * t_h + 1.0
                ds = dot_nt(grads[rows, :], values(h)) * t_h
                if mask is not None:
                    w = jnp.where(mask, w, 0.0)
                    ds = jnp.where(mask, ds, 0.0)
                ds = ds.astype(BF16)
                parts.append(ds)
                v_acc[c, h * wide : (h + 1) * wide] += dot_tn(w.astype(BF16), grads[rows, :wide])
                out.append(dot(ds, keys))
            qk_acc[c, :] += dot_tn(jnp.concatenate(parts, 0), qz[b])
            return out

        def step(c, dq):
            at = moving(c)
            return tuple(
                a + g for a, g in zip(dq, pair(at, far, lambda h: vx[h, at, :], None))
            )

        dq = lax.fori_loop(0, b, step, (jnp.zeros((BLK, 128), F32),) * heads)
        if b == 0:
            v_acc[here, :] = v_acc[here, :] * edge_ref[here, :]
        near = pair(
            here, near_dn,
            lambda h: jnp.concatenate([qkv_ref[here, h * wide : (h + 1) * wide], unit], 1),
            same_or_later(sc_ref[here, :], sr_ref[b]),
        )
        total = jnp.zeros((BLK, 128), F32)
        for h in range(heads):
            total = jnp.where(lanes_of(h, heads), dq[h] + near[h], total)
        back = pltpu.roll(total, 128 - heads * FEAT, 1) * 0.5
        d_ref[here, heads * wide :] = back.astype(BF16)
        if b in turns:
            turns[b]()
    for b in range(blocks):
        here = spot(b)
        d_ref[here, : heads * wide] = v_acc[here, :].astype(BF16)
        queries = d_ref[here, heads * wide :].astype(F32)
        d_ref[here, heads * wide :] = (queries + 2.0 * qk_acc[here, :]).astype(BF16)
    if with_sum:
        s.finish()


def marks(seg):
    length = seg.shape[0]
    edge = (seg == seg[BLK - 1]).astype(F32)
    return seg[:, None], seg.reshape(length // BLK, 1, BLK), edge[:, None]


def attend(qkv, seg, heads, wide):
    length = qkv.shape[0]
    blocks = length // BLK
    width = heads * wide
    return pl.pallas_call(
        functools.partial(attend_kernel, heads, wide, blocks),
        out_shape=(
            jax.ShapeDtypeStruct((length, width), BF16),
            jax.ShapeDtypeStruct((length, width), F32),
            jax.ShapeDtypeStruct((length, heads), F32),
        ),
        in_specs=[WHOLE] * 4,
        out_specs=(WHOLE,) * 3,
        scratch_shapes=[VMEM((blocks, heads * BLK, 128), BF16), VMEM((heads, length, 2 * wide), BF16)],
        compiler_params=pltpu.CompilerParams(vmem_limit_bytes=48 << 20),
        cost_estimate=pl.CostEstimate(flops=2 * 10**10, bytes_accessed=4 * 10**7, transcendentals=0),
        name="attend",
    )(qkv, *marks(seg))


def attend_back(qkv, seg, heads, wide, da, full, den, part, cid):
    length, columns = qkv.shape
    blocks = length // BLK
    width = heads * wide
    with_sum = lax.axis_size("fsdp") == 8
    args = [qkv, *marks(seg), da, full, den]
    specs = [WHOLE] * 7
    outs = [jax.ShapeDtypeStruct((length, columns), BF16)]
    scratch = [
        VMEM((blocks, heads * BLK, 128), BF16), VMEM((heads, length, 2 * wide), BF16),
        VMEM((heads * BLK, 2 * wide), BF16), VMEM((heads * BLK, 2 * wide), BF16),
        VMEM((length, 128), F32), VMEM((length, width), F32),
    ]
    if with_sum:
        rows, cols = length // 8, part.shape[1]
        args.append(part.reshape(8, rows, cols))
        specs.append(ANY)
        outs.append(jax.ShapeDtypeStruct((rows, cols), F32))
        scratch += sum_scratch(rows, cols) + [pltpu.SemaphoreType.DMA((4,))]
        params = pltpu.CompilerParams(
            vmem_limit_bytes=60 << 20, collective_id=cid, has_side_effects=True
        )
    else:
        params = pltpu.CompilerParams(vmem_limit_bytes=60 << 20)
    got = pl.pallas_call(
        functools.partial(attend_back_kernel, heads, wide, blocks, with_sum),
        out_shape=outs,
        in_specs=specs,
        out_specs=[WHOLE] * len(outs),
        scratch_shapes=scratch,
        compiler_params=params,
        cost_estimate=LINKED,
        name="attend_back",
    )(*args)
    if with_sum:
        return got
    return got[0], lax.psum_scatter(part, "fsdp", scatter_dimension=0, tiled=True).astype(F32)


def row_all(part, cid):
    if lax.axis_size("fsdp") == 8:
        return row_gather(part, cid)
    return lax.all_gather(part, "fsdp", axis=0, tiled=True)


def group(arrays, groups):
    parts = jnp.concatenate([a.reshape(a.shape[0], groups, -1) for a in arrays], -1)
    return jnp.transpose(parts, (1, 0, 2))


def over_rows(own):
    return lax.all_gather(own.reshape(-1, own.shape[-1]), "dp", axis=0, tiled=True)


def sum_rows(array):
    return lax.psum_scatter(array, "dp", scatter_dimension=0, tiled=True)


def to_owners(part, groups):
    part = part.reshape(groups, part.shape[0] // groups, -1)
    return jnp.transpose(lax.all_to_all(part, "fsdp", 0, 0, tiled=True), (1, 0, 2)).astype(F32)


def columns(array, lo, hi):
    return array[:, :, lo:hi].reshape(array.shape[0], -1)


def after(value, *others):
    return lax.optimization_barrier((value,) + others)[0]


def on_device(
    layer_input, doc_starts, norm1_gain, w_query, w_key, w_value, w_out, norm2_gain,
    w_gate, w_up, w_down, cotangent,
):
    n_f = lax.axis_size("fsdp")
    x = layer_input[0]
    cot = cotangent[0]
    tokens, width = x.shape
    length = tokens * n_f
    kv = w_query.shape[1]
    rows = w_query.shape[0]
    ff = w_gate.shape[1]
    ff_own, qk_own, v_own = ff // n_f, kv // n_f, width // n_f
    heads = qk_own // FEAT
    wide = v_own // heads
    used = v_own + 2 * qk_own
    gain_at = used
    qkv_cols = v_own + 128
    att_cols = qkv_cols + v_own

    def each(vec):
        return jnp.broadcast_to(vec[:, None, None], (rows, n_f, 1))

    attn = group(
        [w_value, w_query, w_key, each(norm1_gain), each(norm2_gain),
         jnp.zeros((rows, n_f, qkv_cols - used - 2), BF16), w_out],
        n_f,
    )
    attn = over_rows(lax.all_to_all(attn, "fsdp", 0, 0, tiled=True))
    x_all, gu_part = start_exchange(x, group([w_gate, w_up], n_f), 0)
    w_gu = over_rows(gu_part)
    dt_part = lax.all_to_all(after(group([w_down.T], n_f), x_all), "fsdp", 0, 0, tiled=True)
    w_dt = over_rows(after(dt_part, w_gu))
    gain_one = attn[:, gain_at].astype(F32)
    gain_two = attn[:, gain_at + 1].astype(F32)
    keep = (jnp.arange(qkv_cols) < used)[None, :]
    w_qkv = jnp.where(keep, attn[:, :qkv_cols], jnp.zeros((), BF16))
    w_o = lax.all_to_all(attn[:, qkv_cols:], "fsdp", 0, 1, tiled=True)

    places = jnp.arange(length, dtype=jnp.int32)
    seg = jnp.sum((doc_starts[0][None, :] <= places[:, None]).astype(jnp.int32), 1)

    normed_one, _ = rms_apply(x_all.astype(F32), gain_one)
    act_one = normed_one.astype(BF16)
    qkv = dot(act_one, w_qkv).astype(BF16)
    mixed, full, den = attend(qkv, seg, heads, wide)
    x_f = x.astype(F32)
    resid = x_f + product_sum(mixed, w_o, False, 2)
    normed_two, factor_two = rms_apply(resid, gain_two)
    act_two = row_all(normed_two.astype(BF16), 3)

    gate_up = dot(act_two, w_gu)
    gate, up = gate_up[:, :ff_own], gate_up[:, ff_own:]
    sigma = jax.nn.sigmoid(gate)
    swish = gate * sigma
    hidden = (swish * up).astype(BF16)
    cot_all = row_all(after(cot, hidden), 1)
    g_dt = dot_tn(cot_all, hidden).astype(BF16)
    d_hidden = dot(cot_all, w_dt)
    d_gate = (d_hidden * up * sigma * (1.0 + gate * (1.0 - sigma))).astype(BF16)
    d_up = (d_hidden * swish).astype(BF16)
    d_gu = jnp.concatenate([d_gate, d_up], 1)
    g_gu = dot_tn(act_two, d_gu).astype(BF16)
    d_act_two = product_sum(after(d_gu, g_gu, g_dt), w_gu, True, 4)
    g_dt = sum_rows(g_dt)
    g_gu = sum_rows(after(g_gu, g_dt))
    d_act_two = after(d_act_two, g_dt)
    out_part = dot_nt(hidden, w_dt).astype(BF16)

    d_norm, _ = rms_back(d_act_two, resid, factor_two, gain_two)
    d_resid = cot.astype(F32) + d_norm
    d_proj = row_all(d_resid.astype(BF16), 5)
    d_att = dot_nt(d_proj, w_o).astype(BF16)
    g_out = dot_tn(mixed, d_proj).astype(BF16)
    d_qkv, out_sum = attend_back(qkv, seg, heads, wide, d_att, full, den, out_part, 7)
    g_qkv = dot_tn(act_one, d_qkv).astype(BF16)
    d_act_one = product_sum(after(d_qkv, g_qkv, g_gu), w_qkv, True, 6)

    g_out = sum_rows(after(lax.all_to_all(g_out, "fsdp", 1, 0, tiled=True), g_gu))
    g_qkv = sum_rows(after(g_qkv, g_out))
    own_rows = lax.axis_index("dp") * (width // lax.axis_size("dp"))

    def gain_grad(weights, grads, gain):
        part = lax.dynamic_slice_in_dim(weights, own_rows, grads.shape[0], 0)
        inner = jnp.sum(part.astype(F32) * grads.astype(F32), 1)
        return inner / lax.dynamic_slice_in_dim(gain, own_rows, grads.shape[0], 0)

    gains = jnp.stack([gain_grad(w_qkv, g_qkv, gain_one), gain_grad(w_gu, g_gu, gain_two)], 1)
    g_qkv = jnp.concatenate([g_qkv[:, :used], gains.astype(BF16)], 1)
    g_dt = to_owners(g_dt, n_f)
    g_gu = to_owners(g_gu, n_f)
    g_out = to_owners(g_out, n_f)
    g_qkv = to_owners(g_qkv, n_f)
    output = (resid + out_sum).astype(BF16)[None]
    factor_one = lax.rsqrt(jnp.mean(x_f * x_f, -1, keepdims=True) + EPS)
    d_norm, _ = rms_back(d_act_one, x_f, factor_one, gain_one)
    grad_input = (d_resid + d_norm)[None]
    return (
        output,
        grad_input,
        jnp.sum(g_qkv[:, :, gain_at], 1),
        columns(g_qkv, v_own, v_own + qk_own),
        columns(g_qkv, v_own + qk_own, used),
        columns(g_qkv, 0, v_own),
        columns(g_out, 0, v_own),
        jnp.sum(g_qkv[:, :, gain_at + 1], 1),
        columns(g_gu, 0, ff_own),
        columns(g_gu, ff_own, 2 * ff_own),
        columns(g_dt, 0, ff_own).T,
    )


def solution(mesh):
    rows, cols = P(ALL, None), P(None, ALL)
    toks = P("dp", "fsdp", None)
    return jax.shard_map(
        on_device,
        mesh=mesh,
        in_specs=(toks, P("dp", None), P(ALL), rows, rows, rows, rows, P(ALL), rows, rows, cols, toks),
        out_specs=(toks, toks, P(ALL), rows, rows, rows, rows, P(ALL), rows, rows, cols),
        check_vma=False,
    )
```

```python
import functools

import jax
import jax.numpy as jnp
from jax import lax
from jax.experimental import pallas as pl
from jax.experimental.pallas import tpu as pltpu
from jax.sharding import PartitionSpec as P

FEAT = 16
EPS = 1e-05
BLK = 256
F32 = jnp.float32
BF16 = jnp.bfloat16
NT = (((1,), (1,)), ((), ()))
TN = (((0,), (0,)), ((), ()))
VMEM = pltpu.VMEM
ALL = ("dp", "fsdp")
MESH = pl.DeviceIdType.MESH


def dot(a, b):
    return jnp.dot(a, b, preferred_element_type=F32)


def dot_nt(a, b):
    return lax.dot_general(a, b, NT, preferred_element_type=F32)


def dot_tn(a, b):
    return lax.dot_general(a, b, TN, preferred_element_type=F32)


def rms_apply(values, gain):
    factor = lax.rsqrt(jnp.mean(values * values, -1, keepdims=True) + EPS)
    return values * factor * gain, factor


def rms_back(grad, values, factor, gain):
    normed = values * factor
    grad_gain = jnp.sum(grad * normed, 0)
    inner = grad * gain
    grad_in = factor * (inner - normed * jnp.mean(inner * normed, -1, keepdims=True))
    return grad_in, grad_gain


def neighbours():
    me = lax.axis_index("fsdp")
    core, side, line = lax.rem(me, 2), lax.rem(me // 2, 2), me // 4

    def at(y, x, c):
        return 4 * y + 2 * x + c

    return (
        me,
        at(line, side, 1 - core),
        at(line, 1 - side, core),
        at(1 - line, side, core),
        at(1 - line, 1 - side, core),
        1 - 2 * core,
    )


def greet(others):
    barrier = pltpu.get_barrier_semaphore()
    for other in others:
        pl.semaphore_signal(barrier, inc=1, device_id={"fsdp": other}, device_id_type=MESH)
    pl.semaphore_wait(barrier, len(others))


def push(src, dst, send, recv, to):
    return pltpu.make_async_remote_copy(
        src_ref=src, dst_ref=dst, send_sem=send, recv_sem=recv,
        device_id={"fsdp": to}, device_id_type=MESH,
    )


class Gather:
    COPIES = 13

    def __init__(self, x_ref, o_ref, send, recv, local):
        me, sib, xn, yn, dg, _ = neighbours()
        half = x_ref.shape[0] // 2
        lo, hi = pl.ds(0, half), pl.ds(half, half)

        def own(part, to, k):
            return push(x_ref.at[part], o_ref.at[me, part], send.at[k], recv.at[k], to)

        def on(who, part, to, k):
            spot = o_ref.at[who, part]
            return push(spot, spot, send.at[k], recv.at[k], to)

        self.keep = pltpu.make_async_copy(x_ref, o_ref.at[me], local)
        self.x_hi, self.y_lo = own(hi, xn, 0), own(lo, yn, 1)
        self.x_lo, self.y_hi = own(lo, xn, 2), own(hi, yn, 3)
        self.whole = push(x_ref, o_ref.at[me], send.at[4], recv.at[4], sib)
        self.over_x, self.over_y = on(yn, lo, xn, 5), on(xn, hi, yn, 7)
        self.core = [
            on(yn, lo, sib, 6), on(xn, hi, sib, 8), on(xn, lo, sib, 9),
            on(yn, hi, sib, 10), on(dg, lo, sib, 11), on(dg, hi, sib, 12),
        ]

    def start(self):
        self.keep.start()
        for copy in (self.x_hi, self.y_lo, self.x_lo, self.y_hi, self.whole):
            copy.start()

    def turn(self):
        self.y_lo.wait_recv()
        self.over_x.start()
        self.core[0].start()
        self.x_hi.wait_recv()
        self.over_y.start()
        self.core[1].start()

    def rest(self):
        self.x_lo.wait_recv()
        self.core[2].start()
        self.y_hi.wait_recv()
        self.core[3].start()

    def across(self):
        self.over_x.wait_recv()
        self.core[4].start()
        self.over_y.wait_recv()
        self.core[5].start()

    def finish(self):
        self.whole.wait_recv()
        for copy in self.core:
            copy.wait_recv()
        self.sent()
        self.keep.wait()

    def sent(self):
        for copy in [self.x_hi, self.y_lo, self.x_lo, self.y_hi, self.whole, self.over_x, self.over_y] + self.core:
            copy.wait_send()


def gather_scratch():
    dma = pltpu.SemaphoreType.DMA
    return [dma((Gather.COPIES,)), dma((Gather.COPIES,)), dma(())]


def gather_kernel(x_ref, o_ref, send, recv, local):
    _, sib, xn, yn, _, _ = neighbours()
    greet([sib, xn, yn])
    g = Gather(x_ref, o_ref, send, recv, local)
    g.start()
    g.turn()
    g.rest()
    g.across()
    g.finish()


ANY = pl.BlockSpec(memory_space=pl.ANY)
LINKED = pl.CostEstimate(flops=45 * 10**9, bytes_accessed=10**8, transcendentals=0)
WHOLE = pl.BlockSpec(memory_space=VMEM)


def row_gather(x, cid):
    rows, cols = x.shape
    return pl.pallas_call(
        gather_kernel,
        out_shape=jax.ShapeDtypeStruct((8, rows, cols), x.dtype),
        in_specs=[ANY],
        out_specs=ANY,
        scratch_shapes=gather_scratch(),
        compiler_params=pltpu.CompilerParams(collective_id=cid, has_side_effects=True),
        cost_estimate=LINKED,
        name="row_gather",
    )(x).reshape(8 * rows, cols)


class Sum:
    COPIES = 10

    def __init__(self, mine, got, away, ex, ey, fx, fy, total, send, recv):
        me, sib, xn, yn, dg, self.flip = neighbours()
        half = fx.shape[0] // 2
        self.lo, self.hi = lo, hi = pl.ds(0, half), pl.ds(half, half)
        self.order = [dg, xn, yn, me]
        self.mine, self.got, self.ex, self.ey, self.fx, self.fy, self.total = mine, got, ex, ey, fx, fy, total
        self.swaps = [push(away(k), got.at[k], send.at[k], recv.at[k], sib) for k in range(4)]
        self.a = push(mine.at[0, lo], ey, send.at[4], recv.at[4], yn)
        self.b = push(mine.at[0, hi], ex, send.at[5], recv.at[5], xn)
        self.c = push(mine.at[1, hi], fx.at[hi], send.at[6], recv.at[6], xn)
        self.d = push(mine.at[2, lo], fy.at[lo], send.at[7], recv.at[7], yn)
        self.e = push(mine.at[1, lo], fx.at[lo], send.at[8], recv.at[8], xn)
        self.f = push(mine.at[2, hi], fy.at[hi], send.at[9], recv.at[9], yn)

    def add(self, k, part, more=None):
        value = self.mine[k, part].astype(F32) + self.got[k, part].astype(F32)
        if more is not None:
            value = value + more[...].astype(F32)
        self.mine[k, part] = value.astype(BF16)

    def over(self):
        self.swaps[0].wait_recv()
        self.add(0, self.lo)
        self.a.start()
        self.add(0, self.hi)
        self.b.start()

    def along_x(self):
        self.swaps[1].wait_recv()
        self.add(1, self.hi)
        self.c.start()

    def along_y(self):
        self.swaps[2].wait_recv()
        self.add(2, self.lo)
        self.d.start()

    def second(self):
        self.a.wait_recv()
        self.add(1, self.lo, self.ey)
        self.e.start()
        self.b.wait_recv()
        self.add(2, self.hi, self.ex)
        self.f.start()

    def own(self):
        self.swaps[3].wait_recv()
        self.total[...] = self.mine[3].astype(F32) + self.got[3].astype(F32)

    def finish(self):
        for copy in (self.c, self.d, self.e, self.f):
            copy.wait_recv()
        self.total[...] += self.fx[...].astype(F32) + self.fy[...].astype(F32)
        for copy in self.swaps + [self.a, self.b, self.c, self.d, self.e, self.f]:
            copy.wait_send()


def sum_scratch(rows, cols):
    dma = pltpu.SemaphoreType.DMA
    return [
        VMEM((4, rows, cols), BF16), VMEM((4, rows, cols), BF16), VMEM((rows // 2, cols), BF16),
        VMEM((rows // 2, cols), BF16), VMEM((rows, cols), BF16), VMEM((rows, cols), BF16),
        dma((Sum.COPIES,)), dma((Sum.COPIES,)),
    ]


def product_sum_kernel(turned, l_ref, r_ref, o_ref, out, mine, got, ex, ey, fx, fy, send, recv):
    _, sib, xn, yn, _, _ = neighbours()
    rows, cols = o_ref.shape
    greet([sib, xn, yn])
    s = Sum(mine, got, out.at.__getitem__, ex, ey, fx, fy, o_ref, send, recv)

    def block(q, to):
        left = l_ref[pl.ds(pl.multiple_of(q * rows, rows), rows), :]

        @pl.loop(0, cols // 256)
        def _(n):
            here = pl.ds(pl.multiple_of(n * 256, 256), 256)
            part = dot_nt(left, r_ref[here, :]) if turned else dot(left, r_ref[:, here])
            to[:, here] = part.astype(BF16)

    def away(k):
        block(s.order[k] + s.flip, out.at[k])
        s.swaps[k].start()

    def home(k):
        block(s.order[k], mine.at[k])

    away(0)
    home(0)
    away(1)
    s.over()
    home(1)
    s.along_x()
    away(2)
    home(2)
    s.along_y()
    away(3)
    s.second()
    home(3)
    s.own()
    s.finish()


def product_sum(left, right, turned, cid):
    if lax.axis_size("fsdp") != 8:
        part = (dot_nt(left, right) if turned else dot(left, right)).astype(BF16)
        return lax.psum_scatter(part, "fsdp", scatter_dimension=0, tiled=True).astype(F32)
    rows, cols = left.shape[0] // 8, right.shape[0 if turned else 1]
    return pl.pallas_call(
        functools.partial(product_sum_kernel, turned),
        out_shape=jax.ShapeDtypeStruct((rows, cols), F32),
        in_specs=[WHOLE, WHOLE],
        out_specs=WHOLE,
        scratch_shapes=[VMEM((4, rows, cols), BF16)] + sum_scratch(rows, cols),
        compiler_params=pltpu.CompilerParams(
            collective_id=cid, has_side_effects=True, vmem_limit_bytes=56 << 20
        ),
        cost_estimate=LINKED,
        name="product_sum",
    )(left, right)


def start_kernel(x_ref, a_ref, ox_ref, oa_ref, send, recv, local, a_send, a_recv, keep):
    me = lax.axis_index("fsdp")
    others = [lax.rem(me + r, 8) for r in range(1, 8)]
    greet(others)
    g = Gather(x_ref, ox_ref, send, recv, local)
    g.start()
    moves = []
    for r, to in enumerate(others):
        moves.append(push(a_ref.at[to], oa_ref.at[me], a_send.at[r], a_recv.at[r], to))
    stay = [pltpu.make_async_copy(a_ref.at[me], oa_ref.at[me], keep)]
    for copy in moves + stay:
        copy.start()
    g.turn()
    g.rest()
    g.across()
    g.finish()
    for copy in moves + stay:
        copy.wait()


def start_exchange(x, a, cid):
    if lax.axis_size("fsdp") != 8:
        return (
            lax.all_gather(x, "fsdp", axis=0, tiled=True),
            lax.all_to_all(a, "fsdp", 0, 0, tiled=True),
        )
    dma = pltpu.SemaphoreType.DMA
    x_all, a = pl.pallas_call(
        start_kernel,
        out_shape=(
            jax.ShapeDtypeStruct((8,) + x.shape, x.dtype),
            jax.ShapeDtypeStruct(a.shape, a.dtype),
        ),
        in_specs=[ANY] * 2,
        out_specs=(ANY,) * 2,
        scratch_shapes=gather_scratch() + [dma((7,))] * 2 + [dma(())],
        compiler_params=pltpu.CompilerParams(collective_id=cid, has_side_effects=True),
        cost_estimate=LINKED,
        name="start_exchange",
    )(x, a)
    return x_all.reshape(-1, x.shape[1]), a


def same_or_later(seg_rows, seg_cols):
    rows = lax.broadcasted_iota(jnp.int32, (BLK, BLK), 0)
    cols = lax.broadcasted_iota(jnp.int32, (BLK, BLK), 1)
    return (seg_rows == seg_cols) & (cols <= rows)


def spot(b):
    return pl.ds(b * BLK, BLK)


def moving(c):
    return pl.ds(pl.multiple_of(c * BLK, BLK), BLK)


def lanes_of(h, heads):
    lane = lax.broadcasted_iota(jnp.int32, (BLK, 128), 1)
    at = (heads + h) * FEAT
    return (lane >= at) & (lane < at + FEAT)


def lay_out(heads, wide, blocks, qkv_ref, edge_ref, qz, vx):
    first = (lax.broadcasted_iota(jnp.int32, (BLK, wide), 1) == 0).astype(F32)

    @pl.loop(0, blocks)
    def _(b):
        here = moving(b)
        tile = qkv_ref[here, heads * wide :].astype(F32)
        turned = pltpu.roll(tile, heads * FEAT, 1) * 0.25
        edge = edge_ref[here, :]
        for h in range(heads):
            qz[b, h * BLK : (h + 1) * BLK, :] = jnp.where(lanes_of(h, heads), turned, 0.0).astype(BF16)
            vx[h, here, :wide] = (qkv_ref[here, h * wide : (h + 1) * wide].astype(F32) * edge).astype(BF16)
            vx[h, here, wide:] = (first * edge).astype(BF16)


def attend_kernel(
    heads, wide, blocks, x_ref, gain_ref, w_ref, sc_ref, sr_ref, edge_ref,
    qkv_ref, att_ref, full_ref, den_ref, xs, act, load, qz, vx,
):
    width = x_ref.shape[1]

    def fetch(b):
        return pltpu.make_async_copy(x_ref.at[moving(b)], xs.at[lax.rem(b, 2)], load.at[lax.rem(b, 2)])

    fetch(0).start()

    @pl.loop(0, blocks)
    def _(b):
        @pl.when(b < blocks - 1)
        def _():
            fetch(b + 1).start()

        fetch(b).wait()

        @pl.loop(0, BLK // 64)
        def _(n):
            some = pl.ds(pl.multiple_of(n * 64, 64), 64)
            x = xs[lax.rem(b, 2), some, :].astype(F32)
            factor = lax.rsqrt(jnp.sum(x * x, 1, keepdims=True) * (1.0 / width) + EPS)
            act[some, :] = (x * factor * gain_ref[...]).astype(BF16)

        qkv_ref[moving(b), :] = dot(act[...], w_ref[...]).astype(BF16)

    lay_out(heads, wide, blocks, qkv_ref, edge_ref, qz, vx)
    one = (lax.broadcasted_iota(jnp.int32, (BLK, wide), 1) == 0).astype(BF16)
    for b in range(blocks):
        here = spot(b)

        def weigh(c):
            s = dot_nt(qz[b], qkv_ref[c, heads * wide :]) + 1.0
            return s * s + 1.0

        def step(c, sums):
            at = moving(c)
            w = weigh(at).astype(BF16)
            return tuple(
                sums[h] + dot(w[h * BLK : (h + 1) * BLK], vx[h, at, :]) for h in range(heads)
            )

        sums = lax.fori_loop(0, b, step, (jnp.zeros((BLK, 2 * wide), F32),) * heads)
        if b == blocks - 1:
            sums = tuple(s * edge_ref[here, :] for s in sums)
        mask = same_or_later(sc_ref[here, :], sr_ref[b])
        w = weigh(here)
        for h in range(heads):
            entry = slice(h * wide, (h + 1) * wide)
            near = jnp.where(mask, w[h * BLK : (h + 1) * BLK], 0.0).astype(BF16)
            value = jnp.concatenate([qkv_ref[here, entry], one], 1)
            total = sums[h] + dot(near, value)
            den = total[:, wide : wide + 1]
            att = total[:, :wide] / den
            att_ref[here, entry] = att.astype(BF16)
            full_ref[here, entry] = att
            den_ref[here, h : h + 1] = den


def attend_back_kernel(heads, wide, blocks, with_sum, *refs):
    qkv_ref, sc_ref, sr_ref, edge_ref, da_ref, full_ref, den_ref = refs[:7]
    refs = refs[7:]
    if with_sum:
        part_ref, d_ref, o_ref, qz, vx, near_dn, far_dn, qk_acc, v_acc = refs[:9]
        mine, got, ex, ey, fx, fy, send, recv, local = refs[9:]
        _, sib, xn, yn, _, flip = neighbours()
        greet([sib, xn, yn])
        s = Sum(
            mine, got, lambda k: part_ref.at[neighbours()[(4, 2, 3, 0)[k]] + flip], ex, ey, fx, fy, o_ref, send, recv
        )
        loads = [pltpu.make_async_copy(part_ref.at[s.order[k]], mine.at[k], local.at[k]) for k in range(4)]
        for k in range(4):
            s.swaps[k].start()
            loads[k].start()

        def first():
            loads[0].wait()
            s.over()

        def second():
            loads[1].wait()
            s.along_x()
            loads[2].wait()
            s.along_y()

        def fourth():
            loads[3].wait()
            s.own()

        turns = {blocks - 1: first, blocks - 2: second, blocks - 3: s.second, blocks - 4: fourth}
    else:
        d_ref, qz, vx, near_dn, far_dn, qk_acc, v_acc = refs
        turns = {}
    lay_out(heads, wide, blocks, qkv_ref, edge_ref, qz, vx)
    qk_acc[...] = jnp.zeros_like(qk_acc)
    v_acc[...] = jnp.zeros_like(v_acc)
    one = (lax.broadcasted_iota(jnp.int32, (BLK, wide), 1) == 0).astype(F32)
    unit = one.astype(BF16)
    for b in reversed(range(blocks)):
        here = spot(b)
        for h in range(heads):
            entry = slice(h * wide, (h + 1) * wide)
            inv = 1.0 / den_ref[here, h : h + 1]
            da = da_ref[here, entry].astype(F32)
            dn = da * inv
            dd = -jnp.sum(dn * full_ref[here, entry], 1, keepdims=True)
            rows = slice(h * BLK, (h + 1) * BLK)
            near_dn[rows, :wide] = dn.astype(BF16)
            near_dn[rows, wide:] = (dd * one).astype(BF16)
            if b == blocks - 1:
                edge = edge_ref[here, :]
                far_dn[rows, :wide] = (dn * edge).astype(BF16)
                far_dn[rows, wide:] = (dd * edge * one).astype(BF16)

        far = far_dn if b == blocks - 1 else near_dn

        def pair(c, grads, values, mask):
            keys = qkv_ref[c, heads * wide :]
            t = dot_nt(qz[b], keys) + 1.0
            out, parts = [], []
            for h in range(heads):
                rows = slice(h * BLK, (h + 1) * BLK)
                t_h = t[rows]
                w = t_h * t_h + 1.0
                ds = dot_nt(grads[rows, :], values(h)) * t_h
                if mask is not None:
                    w = jnp.where(mask, w, 0.0)
                    ds = jnp.where(mask, ds, 0.0)
                ds = ds.astype(BF16)
                parts.append(ds)
                v_acc[c, h * wide : (h + 1) * wide] += dot_tn(w.astype(BF16), grads[rows, :wide])
                out.append(dot(ds, keys))
            qk_acc[c, :] += dot_tn(jnp.concatenate(parts, 0), qz[b])
            return out

        def step(c, dq):
            at = moving(c)
            return tuple(
                a + g for a, g in zip(dq, pair(at, far, lambda h: vx[h, at, :], None))
            )

        dq = lax.fori_loop(0, b, step, (jnp.zeros((BLK, 128), F32),) * heads)
        if b == 0:
            v_acc[here, :] = v_acc[here, :] * edge_ref[here, :]
        near = pair(
            here, near_dn,
            lambda h: jnp.concatenate([qkv_ref[here, h * wide : (h + 1) * wide], unit], 1),
            same_or_later(sc_ref[here, :], sr_ref[b]),
        )
        total = jnp.zeros((BLK, 128), F32)
        for h in range(heads):
            total = jnp.where(lanes_of(h, heads), dq[h] + near[h], total)
        back = pltpu.roll(total, 128 - heads * FEAT, 1) * 0.5
        d_ref[here, heads * wide :] = back.astype(BF16)
        if b in turns:
            turns[b]()
    for b in range(blocks):
        here = spot(b)
        d_ref[here, : heads * wide] = v_acc[here, :].astype(BF16)
        queries = d_ref[here, heads * wide :].astype(F32)
        d_ref[here, heads * wide :] = (queries + 2.0 * qk_acc[here, :]).astype(BF16)
    if with_sum:
        s.finish()


def marks(seg):
    length = seg.shape[0]
    edge = (seg == seg[BLK - 1]).astype(F32)
    return seg[:, None], seg.reshape(length // BLK, 1, BLK), edge[:, None]


def attend(x_all, gain, w_qkv, seg, heads, wide):
    length, columns = x_all.shape[0], w_qkv.shape[1]
    blocks = length // BLK
    width = heads * wide
    return pl.pallas_call(
        functools.partial(attend_kernel, heads, wide, blocks),
        out_shape=(
            jax.ShapeDtypeStruct((length, columns), BF16),
            jax.ShapeDtypeStruct((length, width), BF16),
            jax.ShapeDtypeStruct((length, width), F32),
            jax.ShapeDtypeStruct((length, heads), F32),
        ),
        in_specs=[ANY] + [WHOLE] * 5,
        out_specs=(WHOLE,) * 4,
        scratch_shapes=[VMEM((2, BLK, x_all.shape[1]), BF16), VMEM((BLK, x_all.shape[1]), BF16),
                        pltpu.SemaphoreType.DMA((2,)), VMEM((blocks, heads * BLK, 128), BF16), VMEM((heads, length, 2 * wide), BF16)],
        compiler_params=pltpu.CompilerParams(vmem_limit_bytes=48 << 20),
        cost_estimate=pl.CostEstimate(flops=2 * 10**10, bytes_accessed=4 * 10**7, transcendentals=0),
        name="attend",
    )(x_all, gain[None, :], w_qkv, *marks(seg))


def attend_back(qkv, seg, heads, wide, da, full, den, part, cid):
    length, columns = qkv.shape
    blocks = length // BLK
    width = heads * wide
    with_sum = lax.axis_size("fsdp") == 8
    args = [qkv, *marks(seg), da, full, den]
    specs = [WHOLE] * 7
    outs = [jax.ShapeDtypeStruct((length, columns), BF16)]
    scratch = [
        VMEM((blocks, heads * BLK, 128), BF16), VMEM((heads, length, 2 * wide), BF16),
        VMEM((heads * BLK, 2 * wide), BF16), VMEM((heads * BLK, 2 * wide), BF16),
        VMEM((length, 128), F32), VMEM((length, width), F32),
    ]
    if with_sum:
        rows, cols = length // 8, part.shape[1]
        args.append(part.reshape(8, rows, cols))
        specs.append(ANY)
        outs.append(jax.ShapeDtypeStruct((rows, cols), F32))
        scratch += sum_scratch(rows, cols) + [pltpu.SemaphoreType.DMA((4,))]
        params = pltpu.CompilerParams(
            vmem_limit_bytes=60 << 20, collective_id=cid, has_side_effects=True
        )
    else:
        params = pltpu.CompilerParams(vmem_limit_bytes=60 << 20)
    got = pl.pallas_call(
        functools.partial(attend_back_kernel, heads, wide, blocks, with_sum),
        out_shape=outs,
        in_specs=specs,
        out_specs=[WHOLE] * len(outs),
        scratch_shapes=scratch,
        compiler_params=params,
        cost_estimate=LINKED,
        name="attend_back",
    )(*args)
    if with_sum:
        return got
    return got[0], lax.psum_scatter(part, "fsdp", scatter_dimension=0, tiled=True).astype(F32)


def tiles(cols):
    return [pl.ds(at, min(256, cols - at)) for at in range(0, cols, 256)]


def gated(gate, up):
    return gate * jax.nn.sigmoid(gate) * up


def gated_back(grad, gate, up):
    sigma = jax.nn.sigmoid(gate)
    return grad * up * sigma * (1.0 + gate * (1.0 - sigma)), grad * gate * sigma


def lane_index(rows):
    return lax.broadcasted_iota(jnp.int32, (rows, 128), 1)


def feed_kernel(
    ff, cot_ref, act_ref, w_ref, cot_all_ref, gu_ref, hid_ref, grad_ref,
    acts, gus, hid, cots, acc, load, save_gu, save_hid, save_cot, send, recv, local,
):
    me, sib, xn, yn, dg, flip = neighbours()
    rows = cot_ref.shape[0]
    main = ff // 128 * 128
    tail = ff - main
    greet([sib, xn, yn])
    g = Gather(cot_ref, cots, send, recv, local)
    g.start()

    def at(b):
        return pl.ds(pl.multiple_of(b * rows, rows), rows)

    def fetch(b):
        return pltpu.make_async_copy(act_ref.at[at(b)], acts.at[lax.rem(b, 2)], load.at[lax.rem(b, 2)])

    def keep_gu(b):
        return pltpu.make_async_copy(gus.at[lax.rem(b, 2)], gu_ref.at[at(b)], save_gu.at[lax.rem(b, 2)])

    fetch(0).start()

    def work(lo, hi):
        @pl.loop(lo, hi)
        def _(b):
            slot = lax.rem(b, 2)

            @pl.when(b < 7)
            def _():
                fetch(b + 1).start()

            fetch(b).wait()

            @pl.when(b >= 2)
            def _():
                keep_gu(b - 2).wait()

            gu = gus.at[slot]
            for tile in tiles(w_ref.shape[1]):
                gu[:, tile] = dot(acts[slot], w_ref[:, tile])
            hid[b, :, :main] = gated(gu[:, :main], gu[:, main : 2 * main]).astype(BF16)
            last = gu[:, 2 * main :]
            value = gated(last, pltpu.roll(last, 128 - tail, 1))
            hid[b, :, main:] = jnp.where(lane_index(rows) < tail, value, 0.0).astype(BF16)
            keep_gu(b).start()

    work(0, 5)
    g.turn()
    work(5, 8)
    keep_gu(6).wait()
    keep_gu(7).wait()
    store = pltpu.make_async_copy(hid, hid_ref, save_hid)
    store.start()

    def add(first, second, start):
        @pl.loop(0, acc.shape[0] // 256)
        def _(n):
            here = pl.ds(pl.multiple_of(n * 256, 256), 256)
            value = dot_tn(cots[first, :, here], hid[first]) + dot_tn(cots[second, :, here], hid[second])
            acc[here, :] = value if start else acc[here, :] + value

    g.whole.wait_recv()
    g.keep.wait()
    g.rest()
    add(me, sib, True)
    g.across()
    for k in range(4):
        g.core[k].wait_recv()
    add(xn, xn + flip, False)
    add(yn, yn + flip, False)
    g.core[4].wait_recv()
    g.core[5].wait_recv()
    store_cot = pltpu.make_async_copy(cots, cot_all_ref, save_cot)
    store_cot.start()

    @pl.loop(0, acc.shape[0] // 256)
    def _(n):
        here = pl.ds(pl.multiple_of(n * 256, 256), 256)
        value = dot_tn(cots[dg, :, here], hid[dg]) + dot_tn(cots[dg + flip, :, here], hid[dg + flip])
        grad_ref[here, :] = (acc[here, :] + value).astype(BF16)

    g.sent()
    store.wait()
    store_cot.wait()


def feed(cot, act, w_gu, ff, cid):
    main = ff // 128 * 128
    tail = ff - main
    hid_cols = main + -(-tail // 128) * 128
    if lax.axis_size("fsdp") != 8:
        cot_all = lax.all_gather(cot, "fsdp", axis=0, tiled=True)
        gu = dot(act, w_gu)
        gate = jnp.concatenate([gu[:, :main], gu[:, 2 * main : 2 * main + tail]], 1)
        up = jnp.concatenate([gu[:, main : 2 * main], gu[:, 2 * main + tail : 2 * ff]], 1)
        hidden = jnp.pad(gated(gate, up), ((0, 0), (0, hid_cols - ff))).astype(BF16)
        return cot_all, gu, hidden, dot_tn(cot_all, hidden).astype(BF16)
    rows, width = cot.shape
    gu_cols = w_gu.shape[1]
    dma = pltpu.SemaphoreType.DMA
    cot_all, gu, hidden, grad = pl.pallas_call(
        functools.partial(feed_kernel, ff),
        out_shape=(
            jax.ShapeDtypeStruct((8, rows, width), BF16),
            jax.ShapeDtypeStruct((8 * rows, gu_cols), F32),
            jax.ShapeDtypeStruct((8, rows, hid_cols), BF16),
            jax.ShapeDtypeStruct((width, hid_cols), BF16),
        ),
        in_specs=[ANY, ANY, WHOLE],
        out_specs=(ANY, ANY, ANY, WHOLE),
        scratch_shapes=[
            VMEM((2, rows, width), BF16), VMEM((2, rows, gu_cols), F32), VMEM((8, rows, hid_cols), BF16),
            VMEM((8, rows, width), BF16), VMEM((width, hid_cols), F32),
            dma((2,)), dma((2,)), dma(()), dma(()),
        ] + gather_scratch(),
        compiler_params=pltpu.CompilerParams(
            collective_id=cid, has_side_effects=True, vmem_limit_bytes=56 << 20
        ),
        cost_estimate=LINKED,
        name="feed",
    )(cot, act, w_gu)
    return cot_all.reshape(-1, width), gu, hidden.reshape(-1, hid_cols), grad


def feed_back_kernel(
    ff, cot_ref, gu_ref, act_ref, w_ref, d_ref, o_ref, grad_ref,
    acts, cots, gus, dh, dgu, out, load_act, load_cot, load_gu, mine, got, ex, ey, fx, fy, send, recv,
):
    me, sib, xn, yn, dg, flip = neighbours()
    rows, cols = o_ref.shape
    main = ff // 128 * 128
    tail = ff - main
    order = [dg + flip, dg, xn + flip, xn, yn + flip, yn, me + flip, me]

    def fetch(k):
        q, slot = order[k], k % 2
        return [
            pltpu.make_async_copy(cot_ref.at[q], cots.at[slot], load_cot.at[slot]),
            pltpu.make_async_copy(gu_ref.at[q], gus.at[slot], load_gu.at[slot]),
        ]

    for copy in fetch(0):
        copy.start()
    whole = pltpu.make_async_copy(act_ref, acts, load_act)
    whole.start()
    greet([sib, xn, yn])
    s = Sum(mine, got, out.at.__getitem__, ex, ey, fx, fy, o_ref, send, recv)

    def block(k, to):
        if k < 7:
            for copy in fetch(k + 1):
                copy.start()
        for copy in fetch(k):
            copy.wait()
        slot, q = k % 2, order[k]
        gu = gus.at[slot]
        for tile in tiles(d_ref.shape[1]):
            dh[:, tile] = dot(cots[slot], d_ref[:, tile])
        here = pl.ds(pl.multiple_of(q * rows, rows), rows)
        d_gate, d_up = gated_back(dh[:, :main], gu[:, :main], gu[:, main : 2 * main])
        dgu[here, :main] = d_gate.astype(BF16)
        dgu[here, main : 2 * main] = d_up.astype(BF16)
        last = gu[:, 2 * main :]
        d_gate, d_up = gated_back(dh[:, main:], last, pltpu.roll(last, 128 - tail, 1))
        lane = lane_index(rows)
        both = jnp.where(lane < tail, d_gate, jnp.where(lane < 2 * tail, pltpu.roll(d_up, tail, 1), 0.0))
        dgu[here, 2 * main :] = both.astype(BF16)

        @pl.loop(0, cols // 256)
        def _(n):
            part = pl.ds(pl.multiple_of(n * 256, 256), 256)
            to[:, part] = dot_nt(dgu[here, :], w_ref[part, :]).astype(BF16)

    def away(k):
        block(2 * k, out.at[k])
        s.swaps[k].start()

    def home(k):
        block(2 * k + 1, mine.at[k])

    away(0)
    home(0)
    s.over()
    away(1)
    home(1)
    s.along_x()
    away(2)
    home(2)
    s.along_y()
    s.second()
    away(3)
    home(3)
    s.own()
    whole.wait()

    @pl.loop(0, cols // 256)
    def _(n):
        part = pl.ds(pl.multiple_of(n * 256, 256), 256)
        grad_ref[part, :] = dot_tn(acts[:, part], dgu[...]).astype(BF16)

    s.finish()


def feed_back(cot_all, gu, act, w_gu, w_dt, ff, cid):
    main = ff // 128 * 128
    tail = ff - main
    if lax.axis_size("fsdp") != 8:
        gate = jnp.concatenate([gu[:, :main], gu[:, 2 * main : 2 * main + tail]], 1)
        up = jnp.concatenate([gu[:, main : 2 * main], gu[:, 2 * main + tail : 2 * ff]], 1)
        d_gate, d_up = gated_back(dot(cot_all, w_dt)[:, :ff], gate, up)
        d_gu = jnp.concatenate(
            [d_gate[:, :main], d_up[:, :main], d_gate[:, main:], d_up[:, main:],
             jnp.zeros((gu.shape[0], gu.shape[1] - 2 * ff), F32)], 1
        ).astype(BF16)
        part = lax.psum_scatter(
            dot_nt(d_gu, w_gu).astype(BF16), "fsdp", scatter_dimension=0, tiled=True
        )
        return part.astype(F32), dot_tn(act, d_gu).astype(BF16)
    length, width = act.shape
    rows, gu_cols, hid_cols = length // 8, gu.shape[1], w_dt.shape[1]
    dma = pltpu.SemaphoreType.DMA
    return pl.pallas_call(
        functools.partial(feed_back_kernel, ff),
        out_shape=(
            jax.ShapeDtypeStruct((rows, width), F32),
            jax.ShapeDtypeStruct((width, gu_cols), BF16),
        ),
        in_specs=[ANY, ANY, ANY, WHOLE, WHOLE],
        out_specs=(WHOLE, WHOLE),
        scratch_shapes=[
            VMEM((length, width), BF16), VMEM((2, rows, width), BF16), VMEM((2, rows, gu_cols), F32),
            VMEM((rows, hid_cols), F32), VMEM((length, gu_cols), BF16), VMEM((4, rows, width), BF16),
            dma(()), dma((2,)), dma((2,)),
        ] + sum_scratch(rows, width),
        compiler_params=pltpu.CompilerParams(
            collective_id=cid, has_side_effects=True, vmem_limit_bytes=61 << 20
        ),
        cost_estimate=LINKED,
        name="feed_back",
    )(cot_all.reshape(8, rows, width), gu.reshape(8, rows, gu_cols), act, w_gu, w_dt)


def project_back_kernel(
    p_ref, hid_ref, d_ref, w_ref, mix_ref, att_ref, part_ref, grad_ref,
    rowed, parts, acc, save, send, recv, local,
):
    me, sib, xn, yn, dg, flip = neighbours()
    rows, cols = p_ref.shape
    greet([sib, xn, yn])
    g = Gather(p_ref, rowed, send, recv, local)
    g.start()

    def side(lo, hi):
        @pl.loop(lo, hi)
        def _(b):
            left = hid_ref[pl.ds(pl.multiple_of(b * rows, rows), rows), :]
            for tile in tiles(cols):
                parts[b, :, tile] = dot_nt(left, d_ref[tile, :]).astype(BF16)

    def use(q, start):
        at = pl.ds(pl.multiple_of(q * rows, rows), rows)
        att_ref[at, :] = dot_nt(rowed[q], w_ref[...]).astype(BF16)
        left = mix_ref[at, :]
        for tile in tiles(cols):
            value = dot_tn(left, rowed[q, :, tile])
            acc[:, tile] = value if start else acc[:, tile] + value

    side(0, 5)
    g.turn()
    side(5, 8)
    store = pltpu.make_async_copy(parts, part_ref, save)
    store.start()
    g.keep.wait()
    use(me, True)
    g.whole.wait_recv()
    use(sib, False)
    g.rest()
    use(xn, False)
    use(yn, False)
    g.across()
    use(dg, False)
    for k in range(4):
        g.core[k].wait_recv()
    use(xn + flip, False)
    use(yn + flip, False)
    g.core[4].wait_recv()
    g.core[5].wait_recv()
    use(dg + flip, False)
    grad_ref[...] = acc[...].astype(BF16)
    g.sent()
    store.wait()


def project_back(d_proj, hidden, w_dt, w_o, mixed, cid):
    if lax.axis_size("fsdp") != 8:
        d_proj = lax.all_gather(d_proj, "fsdp", axis=0, tiled=True)
        return (
            dot_nt(d_proj, w_o).astype(BF16),
            dot_nt(hidden, w_dt).astype(BF16),
            dot_tn(mixed, d_proj).astype(BF16),
        )
    rows, width = d_proj.shape
    own = w_o.shape[0]
    att, part, grad = pl.pallas_call(
        project_back_kernel,
        out_shape=(
            jax.ShapeDtypeStruct((8 * rows, own), BF16),
            jax.ShapeDtypeStruct((8, rows, width), BF16),
            jax.ShapeDtypeStruct((own, width), BF16),
        ),
        in_specs=[ANY] + [WHOLE] * 4,
        out_specs=(WHOLE, ANY, WHOLE),
        scratch_shapes=[
            VMEM((8, rows, width), BF16), VMEM((8, rows, width), BF16), VMEM((own, width), F32),
            pltpu.SemaphoreType.DMA(()),
        ] + gather_scratch(),
        compiler_params=pltpu.CompilerParams(
            collective_id=cid, has_side_effects=True, vmem_limit_bytes=50 << 20
        ),
        cost_estimate=LINKED,
        name="project_back",
    )(d_proj, hidden, w_dt, w_o, mixed)
    return att, part.reshape(8 * rows, width), grad


def row_all(part, cid):
    if lax.axis_size("fsdp") == 8:
        return row_gather(part, cid)
    return lax.all_gather(part, "fsdp", axis=0, tiled=True)


def group(arrays, groups):
    parts = jnp.concatenate([a.reshape(a.shape[0], groups, -1) for a in arrays], -1)
    return jnp.transpose(parts, (1, 0, 2))


def over_rows(own):
    return lax.all_gather(own.reshape(-1, own.shape[-1]), "dp", axis=0, tiled=True)


def sum_rows(array):
    return lax.psum_scatter(array, "dp", scatter_dimension=0, tiled=True)


def to_owners(part, groups):
    part = part.reshape(groups, part.shape[0] // groups, -1)
    return jnp.transpose(lax.all_to_all(part, "fsdp", 0, 0, tiled=True), (1, 0, 2)).astype(F32)


def columns(array, lo, hi):
    return array[:, :, lo:hi].reshape(array.shape[0], -1)


def after(value, *others):
    return lax.optimization_barrier((value,) + others)[0]


def on_device(
    layer_input, doc_starts, norm1_gain, w_query, w_key, w_value, w_out, norm2_gain,
    w_gate, w_up, w_down, cotangent,
):
    n_f = lax.axis_size("fsdp")
    x = layer_input[0]
    cot = cotangent[0]
    tokens, width = x.shape
    length = tokens * n_f
    kv = w_query.shape[1]
    rows = w_query.shape[0]
    ff = w_gate.shape[1]
    ff_own, qk_own, v_own = ff // n_f, kv // n_f, width // n_f
    heads = qk_own // FEAT
    wide = v_own // heads
    used = v_own + 2 * qk_own
    gain_at = used
    qkv_cols = v_own + 128
    att_cols = qkv_cols + v_own

    def each(vec):
        return jnp.broadcast_to(vec[:, None, None], (rows, n_f, 1))

    attn = group(
        [w_value, w_query, w_key, each(norm1_gain), each(norm2_gain),
         jnp.zeros((rows, n_f, qkv_cols - used - 2), BF16), w_out],
        n_f,
    )
    attn = over_rows(lax.all_to_all(attn, "fsdp", 0, 0, tiled=True))
    main = ff_own // 128 * 128

    def halves(a):
        a = a.reshape(rows, n_f, ff_own)
        return a[:, :, :main], a[:, :, main:]

    (gate_main, gate_tail), (up_main, up_tail) = halves(w_gate), halves(w_up)
    empty = jnp.zeros((rows, n_f, 128), BF16)
    gu = group(
        [gate_main, up_main, gate_tail, up_tail, empty[:, :, : -(2 * ff_own) % 128]], n_f
    )
    x_all, gu_part = start_exchange(x, gu, 0)
    w_gu = over_rows(gu_part)
    dt = group([w_down.T, empty[:, :, : -ff_own % 128]], n_f)
    w_dt = over_rows(lax.all_to_all(after(dt, x_all), "fsdp", 0, 0, tiled=True))
    gain_one = attn[:, gain_at].astype(F32)
    gain_two = attn[:, gain_at + 1].astype(F32)
    keep = (jnp.arange(qkv_cols) < used)[None, :]
    w_qkv = jnp.where(keep, attn[:, :qkv_cols], jnp.zeros((), BF16))
    w_o = lax.all_to_all(attn[:, qkv_cols:], "fsdp", 0, 1, tiled=True)

    places = jnp.arange(length, dtype=jnp.int32)
    seg = jnp.sum((doc_starts[0][None, :] <= places[:, None]).astype(jnp.int32), 1)

    normed_one, _ = rms_apply(x_all.astype(F32), gain_one)
    act_one = normed_one.astype(BF16)
    qkv, mixed, full, den = attend(x_all, gain_one, w_qkv, seg, heads, wide)
    x_f = x.astype(F32)
    resid = x_f + product_sum(mixed, w_o, False, 2)
    normed_two, factor_two = rms_apply(resid, gain_two)
    act_two = row_all(normed_two.astype(BF16), 3)

    cot_all, gate_up, hidden, g_dt = feed(cot, act_two, w_gu, ff_own, 1)
    d_act_two, g_gu = feed_back(cot_all, gate_up, act_two, w_gu, w_dt, ff_own, 4)
    g_dt = sum_rows(g_dt)
    g_gu = sum_rows(after(g_gu, g_dt))

    d_norm, _ = rms_back(d_act_two, resid, factor_two, gain_two)
    d_resid = cot.astype(F32) + d_norm
    d_att, out_part, g_out = project_back(d_resid.astype(BF16), hidden, w_dt, w_o, mixed, 5)
    d_qkv, out_sum = attend_back(qkv, seg, heads, wide, d_att, full, den, out_part, 7)
    g_qkv = dot_tn(act_one, d_qkv).astype(BF16)
    d_act_one = product_sum(after(d_qkv, g_qkv, g_gu), w_qkv, True, 6)

    g_out = sum_rows(after(lax.all_to_all(g_out, "fsdp", 1, 0, tiled=True), g_gu, d_qkv))
    g_qkv = sum_rows(after(g_qkv, g_out))
    own_rows = lax.axis_index("dp") * (width // lax.axis_size("dp"))

    def gain_grad(weights, grads, gain):
        part = lax.dynamic_slice_in_dim(weights, own_rows, grads.shape[0], 0)
        inner = jnp.sum(part.astype(F32) * grads.astype(F32), 1)
        return inner / lax.dynamic_slice_in_dim(gain, own_rows, grads.shape[0], 0)

    gains = jnp.stack([gain_grad(w_qkv, g_qkv, gain_one), gain_grad(w_gu, g_gu, gain_two)], 1)
    filler = jnp.zeros((g_qkv.shape[0], qkv_cols - used - 2), BF16)
    g_attn = jnp.concatenate([g_qkv[:, :used], gains.astype(BF16), filler, g_out], 1)
    g_dt = to_owners(g_dt, n_f)
    g_gu = to_owners(g_gu, n_f)
    g_attn = to_owners(g_attn, n_f)

    def from_halves(at, tail):
        both = [g_gu[:, :, at : at + main], g_gu[:, :, tail : tail + ff_own - main]]
        return jnp.concatenate(both, 2).reshape(rows, ff)

    output = (resid + out_sum).astype(BF16)[None]
    factor_one = lax.rsqrt(jnp.mean(x_f * x_f, -1, keepdims=True) + EPS)
    d_norm, _ = rms_back(d_act_one, x_f, factor_one, gain_one)
    grad_input = (d_resid + d_norm)[None]
    return (
        output,
        grad_input,
        jnp.sum(g_attn[:, :, gain_at], 1),
        columns(g_attn, v_own, v_own + qk_own),
        columns(g_attn, v_own + qk_own, used),
        columns(g_attn, 0, v_own),
        columns(g_attn, qkv_cols, att_cols),
        jnp.sum(g_attn[:, :, gain_at + 1], 1),
        from_halves(0, 2 * main),
        from_halves(main, main + ff_own),
        columns(g_dt, 0, ff_own).T,
    )


def solution(mesh):
    rows, cols = P(ALL, None), P(None, ALL)
    toks = P("dp", "fsdp", None)
    return jax.shard_map(
        on_device,
        mesh=mesh,
        in_specs=(toks, P("dp", None), P(ALL), rows, rows, rows, rows, P(ALL), rows, rows, cols, toks),
        out_specs=(toks, toks, P(ALL), rows, rows, rows, rows, P(ALL), rows, rows, cols),
        check_vma=False,
    )
```

```python
import functools

import jax
import jax.numpy as jnp
from jax import lax
from jax.experimental import pallas as pl
from jax.experimental.pallas import tpu as pltpu
from jax.sharding import PartitionSpec as P

FEAT = 16
EPS = 1e-05
BLK = 256
F32 = jnp.float32
BF16 = jnp.bfloat16
NT = (((1,), (1,)), ((), ()))
TN = (((0,), (0,)), ((), ()))
VMEM = pltpu.VMEM
ALL = ("dp", "fsdp")
MESH = pl.DeviceIdType.MESH


def dot(a, b):
    return jnp.dot(a, b, preferred_element_type=F32)


def dot_nt(a, b):
    return lax.dot_general(a, b, NT, preferred_element_type=F32)


def dot_tn(a, b):
    return lax.dot_general(a, b, TN, preferred_element_type=F32)


def rms_apply(values, gain):
    factor = lax.rsqrt(jnp.mean(values * values, -1, keepdims=True) + EPS)
    return values * factor * gain, factor


def rms_back(grad, values, factor, gain):
    normed = values * factor
    grad_gain = jnp.sum(grad * normed, 0)
    inner = grad * gain
    grad_in = factor * (inner - normed * jnp.mean(inner * normed, -1, keepdims=True))
    return grad_in, grad_gain


def neighbours():
    me = lax.axis_index("fsdp")
    core, side, line = lax.rem(me, 2), lax.rem(me // 2, 2), me // 4

    def at(y, x, c):
        return 4 * y + 2 * x + c

    return (
        me,
        at(line, side, 1 - core),
        at(line, 1 - side, core),
        at(1 - line, side, core),
        at(1 - line, 1 - side, core),
        1 - 2 * core,
    )


def greet(others):
    barrier = pltpu.get_barrier_semaphore()
    for other in others:
        pl.semaphore_signal(barrier, inc=1, device_id={"fsdp": other}, device_id_type=MESH)
    pl.semaphore_wait(barrier, len(others))


def push(src, dst, send, recv, to):
    return pltpu.make_async_remote_copy(
        src_ref=src, dst_ref=dst, send_sem=send, recv_sem=recv,
        device_id={"fsdp": to}, device_id_type=MESH,
    )


class Gather:
    COPIES = 13

    def __init__(self, x_ref, o_ref, send, recv, local):
        me, sib, xn, yn, dg, _ = neighbours()
        half = x_ref.shape[0] // 2
        lo, hi = pl.ds(0, half), pl.ds(half, half)

        def own(part, to, k):
            return push(x_ref.at[part], o_ref.at[me, part], send.at[k], recv.at[k], to)

        def on(who, part, to, k):
            spot = o_ref.at[who, part]
            return push(spot, spot, send.at[k], recv.at[k], to)

        self.keep = pltpu.make_async_copy(x_ref, o_ref.at[me], local)
        self.x_hi, self.y_lo = own(hi, xn, 0), own(lo, yn, 1)
        self.x_lo, self.y_hi = own(lo, xn, 2), own(hi, yn, 3)
        self.whole = push(x_ref, o_ref.at[me], send.at[4], recv.at[4], sib)
        self.over_x, self.over_y = on(yn, lo, xn, 5), on(xn, hi, yn, 7)
        self.core = [
            on(yn, lo, sib, 6), on(xn, hi, sib, 8), on(xn, lo, sib, 9),
            on(yn, hi, sib, 10), on(dg, lo, sib, 11), on(dg, hi, sib, 12),
        ]

    def start(self):
        self.keep.start()
        for copy in (self.x_hi, self.y_lo, self.x_lo, self.y_hi, self.whole):
            copy.start()

    def turn(self):
        self.y_lo.wait_recv()
        self.over_x.start()
        self.core[0].start()
        self.x_hi.wait_recv()
        self.over_y.start()
        self.core[1].start()

    def rest(self):
        self.x_lo.wait_recv()
        self.core[2].start()
        self.y_hi.wait_recv()
        self.core[3].start()

    def across(self):
        self.over_x.wait_recv()
        self.core[4].start()
        self.over_y.wait_recv()
        self.core[5].start()

    def finish(self):
        self.whole.wait_recv()
        for copy in self.core:
            copy.wait_recv()
        self.sent()
        self.keep.wait()

    def sent(self):
        for copy in [self.x_hi, self.y_lo, self.x_lo, self.y_hi, self.whole, self.over_x, self.over_y] + self.core:
            copy.wait_send()


def gather_scratch():
    dma = pltpu.SemaphoreType.DMA
    return [dma((Gather.COPIES,)), dma((Gather.COPIES,)), dma(())]


ANY = pl.BlockSpec(memory_space=pl.ANY)
LINKED = pl.CostEstimate(flops=45 * 10**9, bytes_accessed=10**8, transcendentals=0)
WHOLE = pl.BlockSpec(memory_space=VMEM)


class Sum:
    COPIES = 10

    def __init__(self, mine, got, away, ex, ey, fx, fy, total, send, recv):
        me, sib, xn, yn, dg, self.flip = neighbours()
        half = fx.shape[0] // 2
        self.lo, self.hi = lo, hi = pl.ds(0, half), pl.ds(half, half)
        self.order = [dg, xn, yn, me]
        self.mine, self.got, self.ex, self.ey, self.fx, self.fy, self.total = mine, got, ex, ey, fx, fy, total
        self.swaps = [push(away(k), got.at[k], send.at[k], recv.at[k], sib) for k in range(4)]
        self.a = push(mine.at[0, lo], ey, send.at[4], recv.at[4], yn)
        self.b = push(mine.at[0, hi], ex, send.at[5], recv.at[5], xn)
        self.c = push(mine.at[1, hi], fx.at[hi], send.at[6], recv.at[6], xn)
        self.d = push(mine.at[2, lo], fy.at[lo], send.at[7], recv.at[7], yn)
        self.e = push(mine.at[1, lo], fx.at[lo], send.at[8], recv.at[8], xn)
        self.f = push(mine.at[2, hi], fy.at[hi], send.at[9], recv.at[9], yn)

    def add(self, k, part, more=None):
        value = self.mine[k, part].astype(F32) + self.got[k, part].astype(F32)
        if more is not None:
            value = value + more[...].astype(F32)
        self.mine[k, part] = value.astype(BF16)

    def over(self):
        self.swaps[0].wait_recv()
        self.add(0, self.lo)
        self.a.start()
        self.add(0, self.hi)
        self.b.start()

    def along_x(self):
        self.swaps[1].wait_recv()
        self.add(1, self.hi)
        self.c.start()

    def along_y(self):
        self.swaps[2].wait_recv()
        self.add(2, self.lo)
        self.d.start()

    def second(self):
        self.a.wait_recv()
        self.add(1, self.lo, self.ey)
        self.e.start()
        self.b.wait_recv()
        self.add(2, self.hi, self.ex)
        self.f.start()

    def own(self):
        self.swaps[3].wait_recv()
        self.total[...] = self.mine[3].astype(F32) + self.got[3].astype(F32)

    def finish(self):
        for copy in (self.c, self.d, self.e, self.f):
            copy.wait_recv()
        self.total[...] += self.fx[...].astype(F32) + self.fy[...].astype(F32)
        for copy in self.swaps + [self.a, self.b, self.c, self.d, self.e, self.f]:
            copy.wait_send()


def sum_scratch(rows, cols):
    dma = pltpu.SemaphoreType.DMA
    return [
        VMEM((4, rows, cols), BF16), VMEM((4, rows, cols), BF16), VMEM((rows // 2, cols), BF16),
        VMEM((rows // 2, cols), BF16), VMEM((rows, cols), BF16), VMEM((rows, cols), BF16),
        dma((Sum.COPIES,)), dma((Sum.COPIES,)),
    ]


def product_sum_kernel(turned, normed, l_ref, r_ref, *refs):
    if normed:
        x_ref, gain_ref, o_ref, act, out, mine, got, ex, ey, fx, fy, send, recv = refs
        _, sib, xn, yn, _, _ = neighbours()
        greet([sib, xn, yn])
    else:
        x_ref, gain_ref, base_ref, e_ref, o_ref, e_out_ref = refs[:6]
        out, mine, got, ex, ey, fx, fy, send, recv = refs[6:15]
        greet(everyone())
        moved = Exchange(e_ref, e_out_ref, *refs[15:])
        moved.start()
    rows, cols = o_ref.shape
    depth = l_ref.shape[1]
    s = Sum(mine, got, out.at.__getitem__, ex, ey, fx, fy, o_ref, send, recv)

    def block(q, to):
        left = l_ref[pl.ds(pl.multiple_of(q * rows, rows), rows), :]

        @pl.loop(0, cols // 256)
        def _(n):
            here = pl.ds(pl.multiple_of(n * 256, 256), 256)
            part = dot_nt(left, r_ref[here, :depth]) if turned else dot(left, r_ref[:, here])
            to[:, here] = part.astype(BF16)

    def away(k):
        block(s.order[k] + s.flip, out.at[k])
        s.swaps[k].start()

    def home(k):
        block(s.order[k], mine.at[k])

    away(0)
    home(0)
    away(1)
    s.over()
    home(1)
    s.along_x()
    away(2)
    home(2)
    s.along_y()
    away(3)
    s.second()
    home(3)
    s.own()
    s.finish()
    if not normed:
        @pl.loop(0, rows // 64)
        def _(n):
            some = pl.ds(pl.multiple_of(n * 64, 64), 64)
            value = x_ref[some, :].astype(F32)
            factor = lax.rsqrt(jnp.sum(value * value, 1, keepdims=True) * (1.0 / cols) + EPS)
            value = value * factor
            inner = o_ref[some, :] * gain_ref[...]
            along = jnp.sum(inner * value, 1, keepdims=True) * (1.0 / cols)
            o_ref[some, :] = base_ref[some, :] + factor * (inner - value * along)

        moved.finish()
    else:
        @pl.loop(0, rows // 64)
        def _(n):
            some = pl.ds(pl.multiple_of(n * 64, 64), 64)
            value = x_ref[some, :].astype(F32) + o_ref[some, :]
            factor = lax.rsqrt(jnp.sum(value * value, 1, keepdims=True) * (1.0 / cols) + EPS)
            o_ref[some, :] = value
            act[some, :] = (value * factor * gain_ref[...]).astype(BF16)


def product_sum(left, right, turned, cid, x, gain, base=None, moved=None):
    depth = left.shape[1]
    if lax.axis_size("fsdp") != 8:
        part = (dot_nt(left, right[:, :depth]) if turned else dot(left, right)).astype(BF16)
        part = lax.psum_scatter(part, "fsdp", scatter_dimension=0, tiled=True).astype(F32)
        if base is not None:
            x = x.astype(F32)
            part, _ = rms_back(part, x, rms_apply(x, gain)[1], gain)
            return base + part, lax.all_to_all(moved, "fsdp", 0, 0, tiled=True)
        part = part + x.astype(F32)
        act = rms_apply(part, gain)[0].astype(BF16)
        return part, act
    rows, cols = left.shape[0] // 8, right.shape[0 if turned else 1]
    args, specs = [left, right, x, gain[None, :]], [WHOLE] * 4
    outs, out_specs = [jax.ShapeDtypeStruct((rows, cols), F32)], [WHOLE]
    scratch = [VMEM((4, rows, cols), BF16)] + sum_scratch(rows, cols)
    if base is None:
        outs.append(jax.ShapeDtypeStruct((rows, cols), BF16))
        out_specs.append(WHOLE)
    else:
        args += [base, moved]
        specs += [WHOLE, ANY]
        outs.append(jax.ShapeDtypeStruct(moved.shape, moved.dtype))
        out_specs.append(ANY)
        scratch += exchange_scratch()
    got = pl.pallas_call(
        functools.partial(product_sum_kernel, turned, base is None),
        out_shape=outs,
        in_specs=specs,
        out_specs=out_specs,
        scratch_shapes=scratch,
        compiler_params=pltpu.CompilerParams(
            collective_id=cid, has_side_effects=True, vmem_limit_bytes=56 << 20
        ),
        cost_estimate=LINKED,
        name="product_sum",
    )(*args)
    return got


def start_kernel(x_ref, a_ref, ox_ref, oa_ref, send, recv, local, a_send, a_recv, keep):
    me = lax.axis_index("fsdp")
    others = [lax.rem(me + r, 8) for r in range(1, 8)]
    greet(others)
    g = Gather(x_ref, ox_ref, send, recv, local)
    g.start()
    moves = []
    for r, to in enumerate(others):
        moves.append(push(a_ref.at[to], oa_ref.at[me], a_send.at[r], a_recv.at[r], to))
    stay = [pltpu.make_async_copy(a_ref.at[me], oa_ref.at[me], keep)]
    for copy in moves + stay:
        copy.start()
    g.turn()
    g.rest()
    g.across()
    g.finish()
    for copy in moves + stay:
        copy.wait()


def start_exchange(x, a, cid):
    if lax.axis_size("fsdp") != 8:
        return (
            lax.all_gather(x, "fsdp", axis=0, tiled=True),
            lax.all_to_all(a, "fsdp", 0, 0, tiled=True),
        )
    dma = pltpu.SemaphoreType.DMA
    x_all, a = pl.pallas_call(
        start_kernel,
        out_shape=(
            jax.ShapeDtypeStruct((8,) + x.shape, x.dtype),
            jax.ShapeDtypeStruct(a.shape, a.dtype),
        ),
        in_specs=[ANY] * 2,
        out_specs=(ANY,) * 2,
        scratch_shapes=gather_scratch() + [dma((7,))] * 2 + [dma(())],
        compiler_params=pltpu.CompilerParams(collective_id=cid, has_side_effects=True),
        cost_estimate=LINKED,
        name="start_exchange",
    )(x, a)
    return x_all.reshape(-1, x.shape[1]), a


def same_or_later(seg_rows, seg_cols):
    rows = lax.broadcasted_iota(jnp.int32, (BLK, BLK), 0)
    cols = lax.broadcasted_iota(jnp.int32, (BLK, BLK), 1)
    return (seg_rows == seg_cols) & (cols <= rows)


def later_or_same(seg_keys, seg_queries):
    keys = lax.broadcasted_iota(jnp.int32, (BLK, BLK), 0)
    queries = lax.broadcasted_iota(jnp.int32, (BLK, BLK), 1)
    return (seg_keys == seg_queries) & (keys <= queries)


def spot(b):
    return pl.ds(b * BLK, BLK)


def moving(c):
    return pl.ds(pl.multiple_of(c * BLK, BLK), BLK)


def lanes_of(h, heads):
    lane = lax.broadcasted_iota(jnp.int32, (BLK, 128), 1)
    at = (heads + h) * FEAT
    return (lane >= at) & (lane < at + FEAT)


def lay_out(heads, wide, blocks, qkv_ref, edge_ref, qz, vx):
    first = (lax.broadcasted_iota(jnp.int32, (BLK, wide), 1) == 0).astype(F32)

    @pl.loop(0, blocks)
    def _(b):
        here = moving(b)
        tile = qkv_ref[here, heads * wide :].astype(F32)
        turned = pltpu.roll(tile, heads * FEAT, 1) * 0.25
        edge = edge_ref[here, :]
        for h in range(heads):
            qz[b, h * BLK : (h + 1) * BLK, :] = jnp.where(lanes_of(h, heads), turned, 0.0).astype(BF16)
            vx[h, here, :wide] = (qkv_ref[here, h * wide : (h + 1) * wide].astype(F32) * edge).astype(BF16)
            vx[h, here, wide:] = (first * edge).astype(BF16)


def attend_kernel(heads, wide, blocks, linked, *refs):
    x_ref, gain_ref, mats_ref, sc_ref, sr_ref, edge_ref = refs[:6]
    refs = refs[6:]
    if linked:
        dt_ref, cot_ref = refs[:2]
        qkv_ref, att_ref, full_ref, den_ref, act_ref, own_dt_ref, own_out_ref, cot_all_ref = refs[2:10]
        xs, act, w, load, save, load_w, qz, vx, dt_send, dt_recv, out_send, out_recv, stay = refs[10:23]
        me = lax.axis_index("fsdp")
        part = heads * wide

        def rows_for(to):
            return mats_ref.at[pl.ds(pl.multiple_of(to * part, part), part), qkv_ref.shape[1] :]

        here = own_out_ref.at[:, pl.ds(pl.multiple_of(me * part, part), part)]
        others = everyone()
        greet(others)
        gather = Gather(cot_ref, cot_all_ref, *refs[23:])
        gather.start()
        turns = {blocks - 3: gather.rest, blocks - 1: gather.across}
        moves = []
        for r, to in enumerate(others):
            moves.append(push(rows_for(to), here, out_send.at[r], out_recv.at[r], to))
            moves.append(push(dt_ref.at[to], own_dt_ref.at[me], dt_send.at[r], dt_recv.at[r], to))
        moves.append(pltpu.make_async_copy(rows_for(me), here, stay.at[0]))
        moves.append(pltpu.make_async_copy(dt_ref.at[me], own_dt_ref.at[me], stay.at[1]))
        for copy in moves:
            copy.start()
    else:
        qkv_ref, att_ref, full_ref, den_ref, act_ref, xs, act, w, load, save, load_w, qz, vx = refs
        moves, turns = [], {}
    width = x_ref.shape[1]
    weights = pltpu.make_async_copy(mats_ref.at[:, : qkv_ref.shape[1]], w, load_w)
    weights.start()

    def fetch(b):
        return pltpu.make_async_copy(x_ref.at[moving(b)], xs.at[lax.rem(b, 2)], load.at[lax.rem(b, 2)])

    def keep(b):
        return pltpu.make_async_copy(act.at[lax.rem(b, 2)], act_ref.at[moving(b)], save.at[lax.rem(b, 2)])

    fetch(0).start()
    weights.wait()

    @pl.loop(0, blocks)
    def _(b):
        slot = lax.rem(b, 2)

        @pl.when(b < blocks - 1)
        def _():
            fetch(b + 1).start()

        fetch(b).wait()

        @pl.when(b >= 2)
        def _():
            keep(b - 2).wait()

        @pl.loop(0, BLK // 64)
        def _(n):
            some = pl.ds(pl.multiple_of(n * 64, 64), 64)
            x = xs[slot, some, :].astype(F32)
            factor = lax.rsqrt(jnp.sum(x * x, 1, keepdims=True) * (1.0 / width) + EPS)
            act[slot, some, :] = (x * factor * gain_ref[...]).astype(BF16)

        keep(b).start()
        qkv_ref[moving(b), :] = dot(act[slot], w[...]).astype(BF16)

    keep(blocks - 2).wait()
    keep(blocks - 1).wait()

    lay_out(heads, wide, blocks, qkv_ref, edge_ref, qz, vx)
    if linked:
        gather.turn()
    one = (lax.broadcasted_iota(jnp.int32, (BLK, wide), 1) == 0).astype(BF16)
    for b in range(blocks):
        here = spot(b)

        def weigh(c):
            s = dot_nt(qz[b], qkv_ref[c, heads * wide :]) + 1.0
            return s * s + 1.0

        def step(c, sums):
            at = moving(c)
            w = weigh(at).astype(BF16)
            return tuple(
                sums[h] + dot(w[h * BLK : (h + 1) * BLK], vx[h, at, :]) for h in range(heads)
            )

        sums = lax.fori_loop(0, b, step, (jnp.zeros((BLK, 2 * wide), F32),) * heads)
        if b == blocks - 1:
            sums = tuple(s * edge_ref[here, :] for s in sums)
        mask = same_or_later(sc_ref[here, :], sr_ref[b])
        w = weigh(here)
        for h in range(heads):
            entry = slice(h * wide, (h + 1) * wide)
            near = jnp.where(mask, w[h * BLK : (h + 1) * BLK], 0.0).astype(BF16)
            value = jnp.concatenate([qkv_ref[here, entry], one], 1)
            total = sums[h] + dot(near, value)
            den = total[:, wide : wide + 1]
            att = total[:, :wide] / den
            att_ref[here, entry] = att.astype(BF16)
            full_ref[here, entry] = att
            den_ref[here, h : h + 1] = den
        if b in turns:
            turns[b]()
    for copy in moves:
        copy.wait()
    if linked:
        gather.finish()


def attend_back_kernel(heads, wide, blocks, with_sum, *refs):
    qkv_ref, sc_ref, sr_ref, edge_ref, da_ref, full_ref, den_ref = refs[:7]
    refs = refs[7:]
    if with_sum:
        part_ref, e_ref, c_ref, d_ref, o_ref, e_out_ref, c_out_ref = refs[:7]
        qz, vx, kt, near_dn, far_dn, qk_acc, v_acc = refs[7:14]
        mine, got, ex, ey, fx, fy, send, recv, local = refs[14:23]
        flip = neighbours()[5]
        greet(everyone())
        s = Sum(
            mine, got, lambda k: part_ref.at[neighbours()[(4, 2, 3, 0)[k]] + flip], ex, ey, fx, fy, o_ref, send, recv
        )
        loads = [pltpu.make_async_copy(part_ref.at[s.order[k]], mine.at[k], local.at[k]) for k in range(4)]
        for k in range(4):
            s.swaps[k].start()
            loads[k].start()
        moved = [Exchange(c_ref, c_out_ref, *refs[26:]), Exchange(e_ref, e_out_ref, *refs[23:26])]
        for one_move in moved:
            one_move.start()

        def first():
            loads[0].wait()
            s.over()

        def second():
            loads[1].wait()
            s.along_x()
            loads[2].wait()
            s.along_y()

        def fourth():
            loads[3].wait()
            s.own()

        turns = {blocks - 1: first, blocks - 2: second, blocks - 3: s.second, blocks - 4: fourth}
    else:
        d_ref, qz, vx, kt, near_dn, far_dn, qk_acc, v_acc = refs
        turns = {}
    lay_out(heads, wide, blocks, qkv_ref, edge_ref, qz, vx)

    @pl.loop(0, blocks)
    def _(b):
        kt[b] = qkv_ref[moving(b), heads * wide :].astype(F32).T.astype(BF16)

    qk_acc[...] = jnp.zeros_like(qk_acc)
    v_acc[...] = jnp.zeros_like(v_acc)
    one = (lax.broadcasted_iota(jnp.int32, (BLK, wide), 1) == 0).astype(F32)
    unit = one.astype(BF16)
    for b in reversed(range(blocks)):
        here = spot(b)
        for h in range(heads):
            entry = slice(h * wide, (h + 1) * wide)
            inv = 1.0 / den_ref[here, h : h + 1]
            da = da_ref[here, entry].astype(F32)
            dn = da * inv
            dd = -jnp.sum(dn * full_ref[here, entry], 1, keepdims=True)
            rows = slice(h * BLK, (h + 1) * BLK)
            near_dn[rows, :wide] = dn.astype(BF16)
            near_dn[rows, wide:] = (dd * one).astype(BF16)
            if b == blocks - 1:
                edge = edge_ref[here, :]
                far_dn[rows, :wide] = (dn * edge).astype(BF16)
                far_dn[rows, wide:] = (dd * edge * one).astype(BF16)

        far = far_dn if b == blocks - 1 else near_dn

        def pair(c, keys_t, grads, values, mask):
            t = dot_nt(qkv_ref[c, heads * wide :], qz[b]) + 1.0
            parts = []
            for h in range(heads):
                rows = slice(h * BLK, (h + 1) * BLK)
                t_h = t[:, rows]
                w = t_h * t_h + 1.0
                ds = dot_nt(values(h), grads[rows, :]) * t_h
                if mask is not None:
                    w = jnp.where(mask, w, 0.0)
                    ds = jnp.where(mask, ds, 0.0)
                parts.append(ds.astype(BF16))
                v_acc[c, h * wide : (h + 1) * wide] += dot(w.astype(BF16), grads[rows, :wide])
            ds = jnp.concatenate(parts, 1)
            qk_acc[c, :] += dot(ds, qz[b])
            return dot(keys_t, ds)

        def step(c, dq):
            at = moving(c)
            return dq + pair(at, kt[c], far, lambda h: vx[h, at, :], None)

        dq = lax.fori_loop(0, b, step, jnp.zeros((128, heads * BLK), F32))
        if b == 0:
            v_acc[here, :] = v_acc[here, :] * edge_ref[here, :]
        dq = dq + pair(
            here, kt[b], near_dn,
            lambda h: jnp.concatenate([qkv_ref[here, h * wide : (h + 1) * wide], unit], 1),
            later_or_same(sc_ref[here, :], sr_ref[b]),
        )
        row = lax.broadcasted_iota(jnp.int32, (128, BLK), 0)
        total = jnp.zeros((128, BLK), F32)
        for h in range(heads):
            at = (heads + h) * FEAT
            own = (row >= at) & (row < at + FEAT)
            total = jnp.where(own, dq[:, h * BLK : (h + 1) * BLK], total)
        total = total.T
        back = pltpu.roll(total, 128 - heads * FEAT, 1) * 0.5
        d_ref[here, heads * wide :] = back.astype(BF16)
        if b in turns:
            turns[b]()
    for b in range(blocks):
        here = spot(b)
        d_ref[here, : heads * wide] = v_acc[here, :].astype(BF16)
        queries = d_ref[here, heads * wide :].astype(F32)
        d_ref[here, heads * wide :] = (queries + 2.0 * qk_acc[here, :]).astype(BF16)
    if with_sum:
        s.finish()
        for one_move in moved:
            one_move.finish()


def marks(seg):
    length = seg.shape[0]
    edge = (seg == seg[BLK - 1]).astype(F32)
    return seg[:, None], seg.reshape(length // BLK, 1, BLK), edge[:, None]


def attend(x_all, gain, mats, seg, heads, wide, dt, cot, cid):
    length, width = x_all.shape
    blocks = length // BLK
    part = heads * wide
    columns = mats.shape[1] - part
    linked = lax.axis_size("fsdp") == 8
    dma = pltpu.SemaphoreType.DMA
    args = [x_all, gain[None, :], mats, *marks(seg)]
    specs = [ANY, WHOLE, ANY, WHOLE, WHOLE, WHOLE]
    outs = [
        jax.ShapeDtypeStruct((length, columns), BF16),
        jax.ShapeDtypeStruct((length, part), BF16),
        jax.ShapeDtypeStruct((length, part), F32),
        jax.ShapeDtypeStruct((length, heads), F32),
        jax.ShapeDtypeStruct((length, width), BF16),
    ]
    out_specs = [WHOLE] * 4 + [ANY]
    scratch = [
        VMEM((2, BLK, width), BF16), VMEM((2, BLK, width), BF16), VMEM((width, columns), BF16),
        dma((2,)), dma((2,)), dma(()),
        VMEM((blocks, heads * BLK, 128), BF16), VMEM((heads, length, 2 * wide), BF16),
    ]
    params = dict(vmem_limit_bytes=48 << 20)
    if linked:
        args += [dt, cot]
        specs += [ANY, ANY]
        outs += [
            jax.ShapeDtypeStruct(dt.shape, BF16),
            jax.ShapeDtypeStruct((part, width), BF16),
            jax.ShapeDtypeStruct((8,) + cot.shape, BF16),
        ]
        out_specs += [ANY] * 3
        scratch += [dma((7,))] * 4 + [dma((2,))] + gather_scratch()
        params.update(collective_id=cid, has_side_effects=True)
    got = pl.pallas_call(
        functools.partial(attend_kernel, heads, wide, blocks, linked),
        out_shape=outs,
        in_specs=specs,
        out_specs=out_specs,
        scratch_shapes=scratch,
        compiler_params=pltpu.CompilerParams(**params),
        cost_estimate=LINKED,
        name="attend",
    )(*args)
    if linked:
        return *got[:7], got[7].reshape(length, width)
    return (
        *got,
        lax.all_to_all(dt, "fsdp", 0, 0, tiled=True),
        lax.all_to_all(mats[:, columns:], "fsdp", 0, 1, tiled=True),
        lax.all_gather(cot, "fsdp", axis=0, tiled=True),
    )


def attend_back(qkv, seg, heads, wide, da, full, den, part, moved, across, cid):
    length, columns = qkv.shape
    blocks = length // BLK
    width = heads * wide
    with_sum = lax.axis_size("fsdp") == 8
    args = [qkv, *marks(seg), da, full, den]
    specs = [WHOLE] * 7
    outs = [jax.ShapeDtypeStruct((length, columns), BF16)]
    scratch = [
        VMEM((blocks, heads * BLK, 128), BF16), VMEM((heads, length, 2 * wide), BF16),
        VMEM((blocks, 128, BLK), BF16), VMEM((heads * BLK, 2 * wide), BF16), VMEM((heads * BLK, 2 * wide), BF16),
        VMEM((length, 128), F32), VMEM((length, width), F32),
    ]
    if with_sum:
        rows, cols = length // 8, part.shape[1]
        args += [part.reshape(8, rows, cols), moved, across]
        specs += [ANY] * 3
        outs += [
            jax.ShapeDtypeStruct((rows, cols), F32),
            jax.ShapeDtypeStruct(moved.shape, moved.dtype),
            jax.ShapeDtypeStruct((8, across.shape[0], across.shape[1] // 8), across.dtype),
        ]
        scratch += sum_scratch(rows, cols) + [pltpu.SemaphoreType.DMA((4,))] + 2 * exchange_scratch()
        params = pltpu.CompilerParams(
            vmem_limit_bytes=60 << 20, collective_id=cid, has_side_effects=True
        )
    else:
        params = pltpu.CompilerParams(vmem_limit_bytes=60 << 20)
    got = pl.pallas_call(
        functools.partial(attend_back_kernel, heads, wide, blocks, with_sum),
        out_shape=outs,
        in_specs=specs,
        out_specs=[WHOLE, WHOLE, ANY, ANY][: len(outs)],
        scratch_shapes=scratch,
        compiler_params=params,
        cost_estimate=LINKED,
        name="attend_back",
    )(*args)
    if with_sum:
        return *got[:3], got[3].reshape(-1, got[3].shape[2])
    return (
        got[0],
        lax.psum_scatter(part, "fsdp", scatter_dimension=0, tiled=True).astype(F32),
        lax.all_to_all(moved, "fsdp", 0, 0, tiled=True),
        lax.all_to_all(across, "fsdp", 1, 0, tiled=True),
    )


class Exchange:
    def __init__(self, x_ref, o_ref, send, recv, local):
        me = lax.axis_index("fsdp")
        cols = o_ref.shape[2]

        def block(to):
            if len(x_ref.shape) == 3:
                return x_ref.at[to]
            return x_ref.at[:, pl.ds(pl.multiple_of(to * cols, cols), cols)]

        self.copies = [
            push(block(to), o_ref.at[me], send.at[r], recv.at[r], to) for r, to in enumerate(everyone())
        ] + [pltpu.make_async_copy(block(me), o_ref.at[me], local)]

    def start(self):
        for copy in self.copies:
            copy.start()

    def finish(self):
        for copy in self.copies:
            copy.wait()


def exchange_scratch():
    dma = pltpu.SemaphoreType.DMA
    return [dma((7,)), dma((7,)), dma(())]


def everyone():
    me = lax.axis_index("fsdp")
    return [lax.rem(me + r, 8) for r in range(1, 8)]


def tiles(cols):
    return [pl.ds(at, min(256, cols - at)) for at in range(0, cols, 256)]


def gated(gate, up):
    return gate * jax.nn.sigmoid(gate) * up


def gated_back(grad, gate, up):
    sigma = jax.nn.sigmoid(gate)
    return grad * up * sigma * (1.0 + gate * (1.0 - sigma)), grad * gate * sigma


def lane_index(rows):
    return lax.broadcasted_iota(jnp.int32, (rows, 128), 1)


def feed_kernel(
    ff, cot_ref, act_ref, w_ref, act_all_ref, gu_ref, hid_ref, grad_ref,
    acts, gus, hid, cots, acc, load, save_gu, save_hid, save_act, send, recv, local,
):
    me, sib, xn, yn, dg, flip = neighbours()
    rows = act_ref.shape[0]
    main = ff // 128 * 128
    tail = ff - main
    order = [me, sib, xn, yn, xn + flip, yn + flip, dg, dg + flip]
    cot_load = pltpu.make_async_copy(cot_ref, cots, load)
    cot_load.start()
    greet([sib, xn, yn])
    g = Gather(act_ref, acts, send, recv, local)
    g.start()

    def keep_gu(k):
        at = pl.ds(pl.multiple_of(order[k] * rows, rows), rows)
        return pltpu.make_async_copy(gus.at[k % 2], gu_ref.at[at], save_gu.at[k % 2])

    def work(k):
        q = order[k]
        if k >= 2:
            keep_gu(k - 2).wait()
        gu = gus.at[k % 2]
        for tile in tiles(w_ref.shape[1]):
            gu[:, tile] = dot(acts[q], w_ref[:, tile])
        hid[q, :, :main] = gated(gu[:, :main], gu[:, main : 2 * main]).astype(BF16)
        last = gu[:, 2 * main :]
        value = gated(last, pltpu.roll(last, 128 - tail, 1))
        hid[q, :, main:] = jnp.where(lane_index(rows) < tail, value, 0.0).astype(BF16)
        keep_gu(k).start()

    def product(first, second, here):
        return dot_tn(cots[first, :, here], hid[first]) + dot_tn(cots[second, :, here], hid[second])

    def add(first, second, start):
        @pl.loop(0, acc.shape[0] // 256)
        def _(n):
            here = pl.ds(pl.multiple_of(n * 256, 256), 256)
            value = product(first, second, here)
            acc[here, :] = value if start else acc[here, :] + value

    g.keep.wait()
    work(0)
    g.whole.wait_recv()
    work(1)
    g.turn()
    cot_load.wait()
    add(me, sib, True)
    g.rest()
    work(2)
    work(3)
    for k in range(4):
        g.core[k].wait_recv()
    work(4)
    g.across()
    work(5)
    add(xn, xn + flip, False)
    add(yn, yn + flip, False)
    work(6)
    g.core[4].wait_recv()
    g.core[5].wait_recv()
    store_act = pltpu.make_async_copy(acts, act_all_ref, save_act)
    store_act.start()
    work(7)
    store = pltpu.make_async_copy(hid, hid_ref, save_hid)
    store.start()

    @pl.loop(0, acc.shape[0] // 256)
    def _(n):
        here = pl.ds(pl.multiple_of(n * 256, 256), 256)
        grad_ref[here, :] = (acc[here, :] + product(dg, dg + flip, here)).astype(BF16)

    keep_gu(6).wait()
    keep_gu(7).wait()
    g.sent()
    store.wait()
    store_act.wait()


def feed(cot_all, act, w_gu, ff, cid):
    main = ff // 128 * 128
    tail = ff - main
    hid_cols = main + -(-tail // 128) * 128
    if lax.axis_size("fsdp") != 8:
        act = lax.all_gather(act, "fsdp", axis=0, tiled=True)
        gu = dot(act, w_gu)
        gate = jnp.concatenate([gu[:, :main], gu[:, 2 * main : 2 * main + tail]], 1)
        up = jnp.concatenate([gu[:, main : 2 * main], gu[:, 2 * main + tail : 2 * ff]], 1)
        hidden = jnp.pad(gated(gate, up), ((0, 0), (0, hid_cols - ff))).astype(BF16)
        return act, gu, hidden, dot_tn(cot_all, hidden).astype(BF16)
    rows, width = act.shape
    gu_cols = w_gu.shape[1]
    dma = pltpu.SemaphoreType.DMA
    act_all, gu, hidden, grad = pl.pallas_call(
        functools.partial(feed_kernel, ff),
        out_shape=(
            jax.ShapeDtypeStruct((8, rows, width), BF16),
            jax.ShapeDtypeStruct((8 * rows, gu_cols), F32),
            jax.ShapeDtypeStruct((8, rows, hid_cols), BF16),
            jax.ShapeDtypeStruct((width, hid_cols), BF16),
        ),
        in_specs=[ANY, ANY, WHOLE],
        out_specs=(ANY, ANY, ANY, WHOLE),
        scratch_shapes=[
            VMEM((8, rows, width), BF16), VMEM((2, rows, gu_cols), F32), VMEM((8, rows, hid_cols), BF16),
            VMEM((8, rows, width), BF16), VMEM((width, hid_cols), F32),
            dma(()), dma((2,)), dma(()), dma(()),
        ] + gather_scratch(),
        compiler_params=pltpu.CompilerParams(
            collective_id=cid, has_side_effects=True, vmem_limit_bytes=56 << 20
        ),
        cost_estimate=LINKED,
        name="feed",
    )(cot_all.reshape(8, rows, width), act, w_gu)
    return act_all.reshape(-1, width), gu, hidden.reshape(-1, hid_cols), grad


def feed_back_kernel(
    ff, cot_ref, gu_ref, act_ref, w_ref, d_ref, o_ref, grad_ref,
    acts, cots, gus, dh, dgu, out, load_act, load_cot, load_gu, mine, got, ex, ey, fx, fy, send, recv,
):
    me, sib, xn, yn, dg, flip = neighbours()
    rows, cols = o_ref.shape
    main = ff // 128 * 128
    tail = ff - main
    order = [dg + flip, dg, xn + flip, xn, yn + flip, yn, me + flip, me]

    def fetch(k):
        q, slot = order[k], k % 2
        return [
            pltpu.make_async_copy(cot_ref.at[q], cots.at[slot], load_cot.at[slot]),
            pltpu.make_async_copy(gu_ref.at[q], gus.at[slot], load_gu.at[slot]),
        ]

    for copy in fetch(0):
        copy.start()
    whole = pltpu.make_async_copy(act_ref, acts, load_act)
    whole.start()
    greet([sib, xn, yn])
    s = Sum(mine, got, out.at.__getitem__, ex, ey, fx, fy, o_ref, send, recv)

    def block(k, to):
        if k < 7:
            for copy in fetch(k + 1):
                copy.start()
        for copy in fetch(k):
            copy.wait()
        slot, q = k % 2, order[k]
        gu = gus.at[slot]
        for tile in tiles(d_ref.shape[1]):
            dh[:, tile] = dot(cots[slot], d_ref[:, tile])
        here = pl.ds(pl.multiple_of(q * rows, rows), rows)
        d_gate, d_up = gated_back(dh[:, :main], gu[:, :main], gu[:, main : 2 * main])
        dgu[here, :main] = d_gate.astype(BF16)
        dgu[here, main : 2 * main] = d_up.astype(BF16)
        last = gu[:, 2 * main :]
        d_gate, d_up = gated_back(dh[:, main:], last, pltpu.roll(last, 128 - tail, 1))
        lane = lane_index(rows)
        both = jnp.where(lane < tail, d_gate, jnp.where(lane < 2 * tail, pltpu.roll(d_up, tail, 1), 0.0))
        dgu[here, 2 * main :] = both.astype(BF16)

        @pl.loop(0, cols // 256)
        def _(n):
            part = pl.ds(pl.multiple_of(n * 256, 256), 256)
            to[:, part] = dot_nt(dgu[here, :], w_ref[part, :]).astype(BF16)

    def away(k):
        block(2 * k, out.at[k])
        s.swaps[k].start()

    def home(k):
        block(2 * k + 1, mine.at[k])

    away(0)
    home(0)
    s.over()
    away(1)
    home(1)
    s.along_x()
    away(2)
    home(2)
    s.along_y()
    s.second()
    away(3)
    home(3)
    s.own()
    whole.wait()

    @pl.loop(0, cols // 256)
    def _(n):
        part = pl.ds(pl.multiple_of(n * 256, 256), 256)
        grad_ref[part, :] = dot_tn(acts[:, part], dgu[...]).astype(BF16)

    s.finish()


def feed_back(cot_all, gu, act, w_gu, w_dt, ff, cid):
    main = ff // 128 * 128
    tail = ff - main
    if lax.axis_size("fsdp") != 8:
        gate = jnp.concatenate([gu[:, :main], gu[:, 2 * main : 2 * main + tail]], 1)
        up = jnp.concatenate([gu[:, main : 2 * main], gu[:, 2 * main + tail : 2 * ff]], 1)
        d_gate, d_up = gated_back(dot(cot_all, w_dt)[:, :ff], gate, up)
        d_gu = jnp.concatenate(
            [d_gate[:, :main], d_up[:, :main], d_gate[:, main:], d_up[:, main:],
             jnp.zeros((gu.shape[0], gu.shape[1] - 2 * ff), F32)], 1
        ).astype(BF16)
        part = lax.psum_scatter(
            dot_nt(d_gu, w_gu).astype(BF16), "fsdp", scatter_dimension=0, tiled=True
        )
        return part.astype(F32), dot_tn(act, d_gu).astype(BF16)
    length, width = act.shape
    rows, gu_cols, hid_cols = length // 8, gu.shape[1], w_dt.shape[1]
    dma = pltpu.SemaphoreType.DMA
    return pl.pallas_call(
        functools.partial(feed_back_kernel, ff),
        out_shape=(
            jax.ShapeDtypeStruct((rows, width), F32),
            jax.ShapeDtypeStruct((width, gu_cols), BF16),
        ),
        in_specs=[ANY, ANY, ANY, WHOLE, WHOLE],
        out_specs=(WHOLE, WHOLE),
        scratch_shapes=[
            VMEM((length, width), BF16), VMEM((2, rows, width), BF16), VMEM((2, rows, gu_cols), F32),
            VMEM((rows, hid_cols), F32), VMEM((length, gu_cols), BF16), VMEM((4, rows, width), BF16),
            dma(()), dma((2,)), dma((2,)),
        ] + sum_scratch(rows, width),
        compiler_params=pltpu.CompilerParams(
            collective_id=cid, has_side_effects=True, vmem_limit_bytes=61 << 20
        ),
        cost_estimate=LINKED,
        name="feed_back",
    )(cot_all.reshape(8, rows, width), gu.reshape(8, rows, gu_cols), act, w_gu, w_dt)


def project_back_kernel(
    p_ref, hid_ref, d_ref, w_ref, mix_ref, att_ref, part_ref, grad_ref,
    rowed, parts, acc, save, send, recv, local,
):
    me, sib, xn, yn, dg, flip = neighbours()
    rows, cols = p_ref.shape
    greet([sib, xn, yn])
    g = Gather(p_ref, rowed, send, recv, local)
    g.start()

    def side(lo, hi):
        @pl.loop(lo, hi)
        def _(b):
            left = hid_ref[pl.ds(pl.multiple_of(b * rows, rows), rows), :]
            for tile in tiles(cols):
                parts[b, :, tile] = dot_nt(left, d_ref[tile, :]).astype(BF16)

    def use(q, start):
        at = pl.ds(pl.multiple_of(q * rows, rows), rows)
        att_ref[at, :] = dot_nt(rowed[q], w_ref[...]).astype(BF16)
        left = mix_ref[at, :]
        for tile in tiles(cols):
            value = dot_tn(left, rowed[q, :, tile])
            acc[:, tile] = value if start else acc[:, tile] + value

    side(0, 5)
    g.turn()
    side(5, 8)
    store = pltpu.make_async_copy(parts, part_ref, save)
    store.start()
    g.keep.wait()
    use(me, True)
    g.whole.wait_recv()
    use(sib, False)
    g.rest()
    use(xn, False)
    use(yn, False)
    g.across()
    use(dg, False)
    for k in range(4):
        g.core[k].wait_recv()
    use(xn + flip, False)
    use(yn + flip, False)
    g.core[4].wait_recv()
    g.core[5].wait_recv()
    use(dg + flip, False)
    grad_ref[...] = acc[...].astype(BF16)
    g.sent()
    store.wait()


def project_back(d_proj, hidden, w_dt, w_o, mixed, cid):
    if lax.axis_size("fsdp") != 8:
        d_proj = lax.all_gather(d_proj, "fsdp", axis=0, tiled=True)
        return (
            dot_nt(d_proj, w_o).astype(BF16),
            dot_nt(hidden, w_dt).astype(BF16),
            dot_tn(mixed, d_proj).astype(BF16),
        )
    rows, width = d_proj.shape
    own = w_o.shape[0]
    att, part, grad = pl.pallas_call(
        project_back_kernel,
        out_shape=(
            jax.ShapeDtypeStruct((8 * rows, own), BF16),
            jax.ShapeDtypeStruct((8, rows, width), BF16),
            jax.ShapeDtypeStruct((own, width), BF16),
        ),
        in_specs=[ANY] + [WHOLE] * 4,
        out_specs=(WHOLE, ANY, WHOLE),
        scratch_shapes=[
            VMEM((8, rows, width), BF16), VMEM((8, rows, width), BF16), VMEM((own, width), F32),
            pltpu.SemaphoreType.DMA(()),
        ] + gather_scratch(),
        compiler_params=pltpu.CompilerParams(
            collective_id=cid, has_side_effects=True, vmem_limit_bytes=50 << 20
        ),
        cost_estimate=LINKED,
        name="project_back",
    )(d_proj, hidden, w_dt, w_o, mixed)
    return att, part.reshape(8 * rows, width), grad


def group(arrays, groups):
    parts = jnp.concatenate([a.reshape(a.shape[0], groups, -1) for a in arrays], -1)
    return jnp.transpose(parts, (1, 0, 2))


def over_rows(own):
    return lax.all_gather(own.reshape(-1, own.shape[-1]), "dp", axis=0, tiled=True)


def sum_rows(array):
    return lax.psum_scatter(array, "dp", scatter_dimension=0, tiled=True)


def to_owners(part, groups):
    part = part.reshape(groups, part.shape[0] // groups, -1)
    return jnp.transpose(lax.all_to_all(part, "fsdp", 0, 0, tiled=True), (1, 0, 2)).astype(F32)


def columns(array, lo, hi):
    return array[:, :, lo:hi].reshape(array.shape[0], -1)


def after(value, *others):
    return lax.optimization_barrier((value,) + others)[0]


def on_device(
    layer_input, doc_starts, norm1_gain, w_query, w_key, w_value, w_out, norm2_gain,
    w_gate, w_up, w_down, cotangent,
):
    n_f = lax.axis_size("fsdp")
    x = layer_input[0]
    cot = cotangent[0]
    tokens, width = x.shape
    length = tokens * n_f
    kv = w_query.shape[1]
    rows = w_query.shape[0]
    ff = w_gate.shape[1]
    ff_own, qk_own, v_own = ff // n_f, kv // n_f, width // n_f
    heads = qk_own // FEAT
    wide = v_own // heads
    used = v_own + 2 * qk_own
    gain_at = used
    qkv_cols = v_own + 128
    att_cols = qkv_cols + v_own

    def blocked(a):
        return a.reshape(n_f, a.shape[0] // n_f, a.shape[1])

    def each(vec):
        return jnp.broadcast_to(vec[:, None, None], (rows, n_f, 1))

    attn = group(
        [w_value, w_query, w_key, each(norm1_gain), each(norm2_gain),
         jnp.zeros((rows, n_f, qkv_cols - used - 2), BF16), w_out],
        n_f,
    )
    attn = over_rows(lax.all_to_all(attn, "fsdp", 0, 0, tiled=True))
    main = ff_own // 128 * 128

    def halves(a):
        return a[:, : n_f * main].reshape(rows, n_f, main), a[:, n_f * main :].reshape(rows, n_f, -1)

    (gate_main, gate_tail), (up_main, up_tail) = halves(w_gate), halves(w_up)
    empty = jnp.zeros((rows, n_f, 128), BF16)
    gu = group(
        [gate_main, up_main, gate_tail, up_tail, empty[:, :, : -(2 * ff_own) % 128]], n_f
    )
    x_all, gu_part = start_exchange(x, gu, 0)
    w_gu = over_rows(gu_part)
    dt = group([*halves(w_down.T), empty[:, :, : -ff_own % 128]], n_f)
    gain_one = attn[:, gain_at].astype(F32)
    gain_two = attn[:, gain_at + 1].astype(F32)
    places = jnp.arange(length, dtype=jnp.int32)
    seg = jnp.sum((doc_starts[0][None, :] <= places[:, None]).astype(jnp.int32), 1)
    qkv, mixed, full, den, act_one, dt_part, w_o, cot_all = attend(
        x_all, gain_one, attn, seg, heads, wide, dt, cot, 3
    )
    w_dt = over_rows(dt_part)
    resid, act_two = product_sum(mixed, w_o, False, 2, x, gain_two)
    factor_two = lax.rsqrt(jnp.mean(resid * resid, -1, keepdims=True) + EPS)
    act_two, gate_up, hidden, g_dt = feed(cot_all, act_two, w_gu, ff_own, 1)
    d_act_two, g_gu = feed_back(cot_all, gate_up, act_two, w_gu, w_dt, ff_own, 4)
    g_dt = sum_rows(g_dt)
    g_gu = sum_rows(after(g_gu, g_dt))

    d_norm, _ = rms_back(d_act_two, resid, factor_two, gain_two)
    d_resid = cot.astype(F32) + d_norm
    d_att, out_part, g_out = project_back(d_resid.astype(BF16), hidden, w_dt, w_o, mixed, 5)
    d_qkv, out_sum, g_dt, g_out = attend_back(
        qkv, seg, heads, wide, d_att, full, den, out_part, blocked(g_dt), g_out, 7
    )
    g_qkv = dot_tn(act_one, d_qkv).astype(BF16)
    grad_input, moved_gu = product_sum(
        after(d_qkv, g_qkv), attn, True, 6, x, gain_one, d_resid, blocked(g_gu)
    )

    g_out = sum_rows(after(g_out, g_gu))
    g_qkv = sum_rows(after(g_qkv, g_gu))
    own_rows = lax.axis_index("dp") * (width // lax.axis_size("dp"))

    def gain_grad(weights, grads, gain):
        part = lax.dynamic_slice_in_dim(weights, own_rows, grads.shape[0], 0)
        inner = jnp.sum(part.astype(F32) * grads.astype(F32), 1)
        return inner / lax.dynamic_slice_in_dim(gain, own_rows, grads.shape[0], 0)

    gains = jnp.stack([gain_grad(attn[:, :qkv_cols], g_qkv, gain_one), gain_grad(w_gu, g_gu, gain_two)], 1)
    filler = jnp.zeros((g_qkv.shape[0], qkv_cols - used - 2), BF16)
    g_attn = jnp.concatenate([g_qkv[:, :used], gains.astype(BF16), filler, g_out], 1)
    moved_gu, g_dt, _ = lax.optimization_barrier((moved_gu, g_dt, g_attn))
    g_gu, g_dt = jnp.transpose(moved_gu, (1, 0, 2)), jnp.transpose(g_dt, (1, 0, 2))
    g_attn = to_owners(g_attn, n_f)

    def from_halves(grads, at, tail):
        parts = [grads[:, :, at : at + main], grads[:, :, tail : tail + ff_own - main]]
        return jnp.concatenate([columns(g, 0, g.shape[2]) for g in parts], 1).astype(F32)

    output = (resid + out_sum).astype(BF16)[None]
    return (
        output,
        grad_input[None],
        jnp.sum(g_attn[:, :, gain_at], 1),
        columns(g_attn, v_own, v_own + qk_own),
        columns(g_attn, v_own + qk_own, used),
        columns(g_attn, 0, v_own),
        columns(g_attn, qkv_cols, att_cols),
        jnp.sum(g_attn[:, :, gain_at + 1], 1),
        from_halves(g_gu, 0, 2 * main),
        from_halves(g_gu, main, main + ff_own),
        from_halves(g_dt, 0, main).T,
    )


def solution(mesh):
    rows, cols = P(ALL, None), P(None, ALL)
    toks = P("dp", "fsdp", None)
    return jax.shard_map(
        on_device,
        mesh=mesh,
        in_specs=(toks, P("dp", None), P(ALL), rows, rows, rows, rows, P(ALL), rows, rows, cols, toks),
        out_specs=(toks, toks, P(ALL), rows, rows, rows, rows, P(ALL), rows, rows, cols),
        check_vma=False,
    )
```

```python
import functools

import jax
import jax.numpy as jnp
from jax import lax
from jax.experimental import pallas as pl
from jax.experimental.pallas import tpu as pltpu
from jax.sharding import PartitionSpec as P

FEAT = 16
EPS = 1e-05
BLK = 256
F32 = jnp.float32
BF16 = jnp.bfloat16
NT = (((1,), (1,)), ((), ()))
TN = (((0,), (0,)), ((), ()))
VMEM = pltpu.VMEM
ALL = ("dp", "fsdp")
MESH = pl.DeviceIdType.MESH


def dot(a, b):
    return jnp.dot(a, b, preferred_element_type=F32)


def dot_nt(a, b):
    return lax.dot_general(a, b, NT, preferred_element_type=F32)


def dot_tn(a, b):
    return lax.dot_general(a, b, TN, preferred_element_type=F32)


def rms_apply(values, gain):
    factor = lax.rsqrt(jnp.mean(values * values, -1, keepdims=True) + EPS)
    return values * factor * gain, factor


def rms_back(grad, values, factor, gain):
    normed = values * factor
    grad_gain = jnp.sum(grad * normed, 0)
    inner = grad * gain
    grad_in = factor * (inner - normed * jnp.mean(inner * normed, -1, keepdims=True))
    return grad_in, grad_gain


def neighbours():
    me = lax.axis_index("fsdp")
    core, side, line = lax.rem(me, 2), lax.rem(me // 2, 2), me // 4

    def at(y, x, c):
        return 4 * y + 2 * x + c

    return (
        me,
        at(line, side, 1 - core),
        at(line, 1 - side, core),
        at(1 - line, side, core),
        at(1 - line, 1 - side, core),
        1 - 2 * core,
    )


def greet(others):
    barrier = pltpu.get_barrier_semaphore()
    for other in others:
        pl.semaphore_signal(barrier, inc=1, device_id={"fsdp": other}, device_id_type=MESH)
    pl.semaphore_wait(barrier, len(others))


def push(src, dst, send, recv, to):
    return pltpu.make_async_remote_copy(
        src_ref=src, dst_ref=dst, send_sem=send, recv_sem=recv,
        device_id={"fsdp": to}, device_id_type=MESH,
    )


class Gather:
    COPIES = 13

    def __init__(self, x_ref, o_ref, send, recv, local):
        me, sib, xn, yn, dg, _ = neighbours()
        half = x_ref.shape[0] // 2
        lo, hi = pl.ds(0, half), pl.ds(half, half)

        def own(part, to, k):
            return push(x_ref.at[part], o_ref.at[me, part], send.at[k], recv.at[k], to)

        def on(who, part, to, k):
            spot = o_ref.at[who, part]
            return push(spot, spot, send.at[k], recv.at[k], to)

        self.keep = pltpu.make_async_copy(x_ref, o_ref.at[me], local)
        self.x_hi, self.y_lo = own(hi, xn, 0), own(lo, yn, 1)
        self.x_lo, self.y_hi = own(lo, xn, 2), own(hi, yn, 3)
        self.whole = push(x_ref, o_ref.at[me], send.at[4], recv.at[4], sib)
        self.over_x, self.over_y = on(yn, lo, xn, 5), on(xn, hi, yn, 7)
        self.core = [
            on(yn, lo, sib, 6), on(xn, hi, sib, 8), on(xn, lo, sib, 9),
            on(yn, hi, sib, 10), on(dg, lo, sib, 11), on(dg, hi, sib, 12),
        ]

    def start(self):
        self.keep.start()
        for copy in (self.x_hi, self.y_lo, self.x_lo, self.y_hi, self.whole):
            copy.start()

    def turn(self):
        self.y_lo.wait_recv()
        self.over_x.start()
        self.core[0].start()
        self.x_hi.wait_recv()
        self.over_y.start()
        self.core[1].start()

    def rest(self):
        self.x_lo.wait_recv()
        self.core[2].start()
        self.y_hi.wait_recv()
        self.core[3].start()

    def across(self):
        self.over_x.wait_recv()
        self.core[4].start()
        self.over_y.wait_recv()
        self.core[5].start()

    def finish(self):
        self.whole.wait_recv()
        for copy in self.core:
            copy.wait_recv()
        self.sent()
        self.keep.wait()

    def sent(self):
        for copy in [self.x_hi, self.y_lo, self.x_lo, self.y_hi, self.whole, self.over_x, self.over_y] + self.core:
            copy.wait_send()


def gather_scratch():
    dma = pltpu.SemaphoreType.DMA
    return [dma((Gather.COPIES,)), dma((Gather.COPIES,)), dma(())]


ANY = pl.BlockSpec(memory_space=pl.ANY)
LINKED = pl.CostEstimate(flops=45 * 10**9, bytes_accessed=10**8, transcendentals=0)
WHOLE = pl.BlockSpec(memory_space=VMEM)


class Sum:
    COPIES = 10

    def __init__(self, mine, got, away, ex, ey, fx, fy, total, send, recv):
        me, sib, xn, yn, dg, self.flip = neighbours()
        half = fx.shape[0] // 2
        self.lo, self.hi = lo, hi = pl.ds(0, half), pl.ds(half, half)
        self.order = [dg, xn, yn, me]
        self.mine, self.got, self.ex, self.ey, self.fx, self.fy, self.total = mine, got, ex, ey, fx, fy, total
        self.swaps = [push(away(k), got.at[k], send.at[k], recv.at[k], sib) for k in range(4)]
        self.a = push(mine.at[0, lo], ey, send.at[4], recv.at[4], yn)
        self.b = push(mine.at[0, hi], ex, send.at[5], recv.at[5], xn)
        self.c = push(mine.at[1, hi], fx.at[hi], send.at[6], recv.at[6], xn)
        self.d = push(mine.at[2, lo], fy.at[lo], send.at[7], recv.at[7], yn)
        self.e = push(mine.at[1, lo], fx.at[lo], send.at[8], recv.at[8], xn)
        self.f = push(mine.at[2, hi], fy.at[hi], send.at[9], recv.at[9], yn)

    def add(self, k, part, more=None):
        value = self.mine[k, part].astype(F32) + self.got[k, part].astype(F32)
        if more is not None:
            value = value + more[...].astype(F32)
        self.mine[k, part] = value.astype(BF16)

    def over(self):
        self.swaps[0].wait_recv()
        self.add(0, self.lo)
        self.a.start()
        self.add(0, self.hi)
        self.b.start()

    def along_x(self):
        self.swaps[1].wait_recv()
        self.add(1, self.hi)
        self.c.start()

    def along_y(self):
        self.swaps[2].wait_recv()
        self.add(2, self.lo)
        self.d.start()

    def second(self):
        self.a.wait_recv()
        self.add(1, self.lo, self.ey)
        self.e.start()
        self.b.wait_recv()
        self.add(2, self.hi, self.ex)
        self.f.start()

    def own(self):
        self.swaps[3].wait_recv()
        self.total[...] = self.mine[3].astype(F32) + self.got[3].astype(F32)

    def finish(self):
        for copy in (self.c, self.d, self.e, self.f):
            copy.wait_recv()
        self.total[...] += self.fx[...].astype(F32) + self.fy[...].astype(F32)
        for copy in self.swaps + [self.a, self.b, self.c, self.d, self.e, self.f]:
            copy.wait_send()


def sum_scratch(rows, cols):
    dma = pltpu.SemaphoreType.DMA
    return [
        VMEM((4, rows, cols), BF16), VMEM((4, rows, cols), BF16), VMEM((rows // 2, cols), BF16),
        VMEM((rows // 2, cols), BF16), VMEM((rows, cols), BF16), VMEM((rows, cols), BF16),
        dma((Sum.COPIES,)), dma((Sum.COPIES,)),
    ]


def regroup(body, end, main, tail, o_ref):
    width = 8 * tail
    lane = lax.broadcasted_iota(jnp.int32, (o_ref.shape[0], width), 1)
    tails = jnp.zeros((o_ref.shape[0], width), F32)
    for j in range(8):
        o_ref[:, j * main : (j + 1) * main] = body(j).astype(F32)
        piece = jnp.concatenate([end(j), jnp.zeros((o_ref.shape[0], width - 128), F32)], 1)
        piece = pltpu.roll(piece, j * tail, 1) if j else piece
        tails = jnp.where((lane >= j * tail) & (lane < (j + 1) * tail), piece, tails)
    o_ref[:, 8 * main :] = tails


def product_sum_kernel(turned, normed, l_ref, r_ref, *refs):
    if normed:
        x_ref, gain_ref, o_ref, act, out, mine, got, ex, ey, fx, fy, send, recv = refs
        _, sib, xn, yn, _, _ = neighbours()
        greet([sib, xn, yn])
    else:
        x_ref, gain_ref, base_ref, e_ref, dt_ref, w_ref, o_ref, gate_ref, up_ref, down_ref, along_ref = refs[:11]
        out, mine, got, ex, ey, fx, fy, send, recv = refs[11:20]
        own_gu, gu, w, load_gu, load_w = refs[20:25]
        loads = [
            pltpu.make_async_copy(e_ref, gu, load_gu),
            pltpu.make_async_copy(w_ref.at[pl.ds(lax.axis_index("dp") * w.shape[0], w.shape[0])], w, load_w),
        ]
        for load in loads:
            load.start()
        greet(everyone())
        moved = Exchange(e_ref, own_gu, *refs[25:])
        moved.start()
    rows, cols = o_ref.shape
    depth = l_ref.shape[1]
    s = Sum(mine, got, out.at.__getitem__, ex, ey, fx, fy, o_ref, send, recv)

    def block(q, to):
        left = l_ref[pl.ds(pl.multiple_of(q * rows, rows), rows), :]

        @pl.loop(0, cols // 256)
        def _(n):
            here = pl.ds(pl.multiple_of(n * 256, 256), 256)
            part = dot_nt(left, r_ref[here, :depth]) if turned else dot(left, r_ref[:, here])
            to[:, here] = part.astype(BF16)

    def away(k):
        block(s.order[k] + s.flip, out.at[k])
        s.swaps[k].start()

    def home(k):
        block(s.order[k], mine.at[k])

    away(0)
    home(0)
    away(1)
    s.over()
    home(1)
    s.along_x()
    away(2)
    home(2)
    s.along_y()
    away(3)
    s.second()
    home(3)
    s.own()
    if not normed:
        for load in loads:
            load.wait()
        some_rows = gu.shape[1]
        for j in range(8):
            here = slice(j * some_rows, (j + 1) * some_rows)
            along_ref[here, :] = jnp.sum(w[here, :].astype(F32) * gu[j].astype(F32), 1, keepdims=True)
        main = down_ref.shape[1] // 8 // 128 * 128
        tail = down_ref.shape[1] // 8 - main
        regroup(lambda j: dt_ref[j, :, :main], lambda j: dt_ref[j, :, main:].astype(F32), main, tail, down_ref)
    s.finish()
    if not normed:
        @pl.loop(0, rows // 64)
        def _(n):
            some = pl.ds(pl.multiple_of(n * 64, 64), 64)
            value = x_ref[some, :].astype(F32)
            factor = lax.rsqrt(jnp.sum(value * value, 1, keepdims=True) * (1.0 / cols) + EPS)
            value = value * factor
            inner = o_ref[some, :] * gain_ref[...]
            along = jnp.sum(inner * value, 1, keepdims=True) * (1.0 / cols)
            o_ref[some, :] = base_ref[some, :] + factor * (inner - value * along)

        moved.finish()

        def turned_tail(j):
            return pltpu.roll(own_gu[j, :, 2 * main :].astype(F32), 128 - tail, 1)

        regroup(
            lambda j: own_gu[j, :, :main], lambda j: own_gu[j, :, 2 * main :].astype(F32), main, tail, gate_ref
        )
        regroup(lambda j: own_gu[j, :, main : 2 * main], turned_tail, main, tail, up_ref)
    else:
        @pl.loop(0, rows // 64)
        def _(n):
            some = pl.ds(pl.multiple_of(n * 64, 64), 64)
            value = x_ref[some, :].astype(F32) + o_ref[some, :]
            factor = lax.rsqrt(jnp.sum(value * value, 1, keepdims=True) * (1.0 / cols) + EPS)
            o_ref[some, :] = value
            act[some, :] = (value * factor * gain_ref[...]).astype(BF16)


def product_sum(left, right, turned, cid, x, gain, base=None, moved=None, down=None, w_gu=None, ff=0):
    depth = left.shape[1]
    if lax.axis_size("fsdp") != 8:
        part = (dot_nt(left, right[:, :depth]) if turned else dot(left, right)).astype(BF16)
        part = lax.psum_scatter(part, "fsdp", scatter_dimension=0, tiled=True).astype(F32)
        if base is not None:
            n_f, some, columns_own = moved.shape
            x = x.astype(F32)
            part, _ = rms_back(part, x, rms_apply(x, gain)[1], gain)
            at = lax.axis_index("dp") * n_f * some
            w = lax.dynamic_slice_in_dim(w_gu, at, n_f * some, 0).reshape(moved.shape)
            along = jnp.sum(w.astype(F32) * moved.astype(F32), 2).reshape(-1, 1)
            moved = lax.all_to_all(moved, "fsdp", 0, 0, tiled=True)
            main = ff // 128 * 128

            def owner(grads, at, end):
                parts = [grads[:, :, at : at + main], grads[:, :, end : end + ff - main]]
                parts = [jnp.transpose(p, (1, 0, 2)).reshape(some, -1) for p in parts]
                return jnp.concatenate(parts, 1).astype(F32)

            grads = owner(moved, 0, 2 * main), owner(moved, main, main + ff), owner(down, 0, main)
            return base + part, *grads, along
        part = part + x.astype(F32)
        act = rms_apply(part, gain)[0].astype(BF16)
        return part, act
    rows, cols = left.shape[0] // 8, right.shape[0 if turned else 1]
    args, specs = [left, right, x, gain[None, :]], [WHOLE] * 4
    outs, out_specs = [jax.ShapeDtypeStruct((rows, cols), F32)], [WHOLE]
    scratch = [VMEM((4, rows, cols), BF16)] + sum_scratch(rows, cols)
    if base is None:
        outs.append(jax.ShapeDtypeStruct((rows, cols), BF16))
        out_specs.append(WHOLE)
    else:
        args += [base, moved, down, w_gu]
        specs += [WHOLE, ANY, WHOLE, ANY]
        some = moved.shape[1]
        outs += [jax.ShapeDtypeStruct((some, 8 * ff), F32)] * 3 + [jax.ShapeDtypeStruct((8 * some, 1), F32)]
        out_specs += [WHOLE] * 4
        scratch += [
            VMEM(moved.shape, BF16), VMEM(moved.shape, BF16), VMEM((8 * some, moved.shape[2]), BF16),
            pltpu.SemaphoreType.DMA(()), pltpu.SemaphoreType.DMA(()),
        ] + exchange_scratch()
    got = pl.pallas_call(
        functools.partial(product_sum_kernel, turned, base is None),
        out_shape=outs,
        in_specs=specs,
        out_specs=out_specs,
        scratch_shapes=scratch,
        compiler_params=pltpu.CompilerParams(
            collective_id=cid, has_side_effects=True, vmem_limit_bytes=56 << 20
        ),
        cost_estimate=LINKED,
        name="product_sum",
    )(*args)
    return got


def start_kernel(x_ref, a_ref, ox_ref, oa_ref, send, recv, local, a_send, a_recv, keep):
    me = lax.axis_index("fsdp")
    others = [lax.rem(me + r, 8) for r in range(1, 8)]
    greet(others)
    g = Gather(x_ref, ox_ref, send, recv, local)
    g.start()
    moves = []
    for r, to in enumerate(others):
        moves.append(push(a_ref.at[to], oa_ref.at[me], a_send.at[r], a_recv.at[r], to))
    stay = [pltpu.make_async_copy(a_ref.at[me], oa_ref.at[me], keep)]
    for copy in moves + stay:
        copy.start()
    g.turn()
    g.rest()
    g.across()
    g.finish()
    for copy in moves + stay:
        copy.wait()


def start_exchange(x, a, cid):
    if lax.axis_size("fsdp") != 8:
        return (
            lax.all_gather(x, "fsdp", axis=0, tiled=True),
            lax.all_to_all(a, "fsdp", 0, 0, tiled=True),
        )
    dma = pltpu.SemaphoreType.DMA
    x_all, a = pl.pallas_call(
        start_kernel,
        out_shape=(
            jax.ShapeDtypeStruct((8,) + x.shape, x.dtype),
            jax.ShapeDtypeStruct(a.shape, a.dtype),
        ),
        in_specs=[ANY] * 2,
        out_specs=(ANY,) * 2,
        scratch_shapes=gather_scratch() + [dma((7,))] * 2 + [dma(())],
        compiler_params=pltpu.CompilerParams(collective_id=cid, has_side_effects=True),
        cost_estimate=LINKED,
        name="start_exchange",
    )(x, a)
    return x_all.reshape(-1, x.shape[1]), a


def same_or_later(seg_rows, seg_cols):
    rows = lax.broadcasted_iota(jnp.int32, (BLK, BLK), 0)
    cols = lax.broadcasted_iota(jnp.int32, (BLK, BLK), 1)
    return (seg_rows == seg_cols) & (cols <= rows)


def later_or_same(seg_keys, seg_queries):
    keys = lax.broadcasted_iota(jnp.int32, (BLK, BLK), 0)
    queries = lax.broadcasted_iota(jnp.int32, (BLK, BLK), 1)
    return (seg_keys == seg_queries) & (keys <= queries)


def spot(b):
    return pl.ds(b * BLK, BLK)


def moving(c):
    return pl.ds(pl.multiple_of(c * BLK, BLK), BLK)


def lanes_of(h, heads):
    lane = lax.broadcasted_iota(jnp.int32, (BLK, 128), 1)
    at = (heads + h) * FEAT
    return (lane >= at) & (lane < at + FEAT)


def lay_out(heads, wide, blocks, qkv_ref, edge_ref, qz, vx):
    first = (lax.broadcasted_iota(jnp.int32, (BLK, wide), 1) == 0).astype(F32)

    @pl.loop(0, blocks)
    def _(b):
        here = moving(b)
        tile = qkv_ref[here, heads * wide :].astype(F32)
        turned = pltpu.roll(tile, heads * FEAT, 1) * 0.25
        edge = edge_ref[here, :]
        for h in range(heads):
            qz[b, h * BLK : (h + 1) * BLK, :] = jnp.where(lanes_of(h, heads), turned, 0.0).astype(BF16)
            vx[h, here, :wide] = (qkv_ref[here, h * wide : (h + 1) * wide].astype(F32) * edge).astype(BF16)
            vx[h, here, wide:] = (first * edge).astype(BF16)


def attend_kernel(heads, wide, blocks, linked, *refs):
    x_ref, gain_ref, mats_ref, sc_ref, sr_ref, edge_ref = refs[:6]
    refs = refs[6:]
    if linked:
        dt_ref, cot_ref = refs[:2]
        qkv_ref, att_ref, full_ref, den_ref, act_ref, own_dt_ref, own_out_ref, cot_all_ref = refs[2:10]
        xs, act, w, load, save, load_w, qz, vx, dt_send, dt_recv, out_send, out_recv, stay = refs[10:23]
        me = lax.axis_index("fsdp")
        part = heads * wide

        def rows_for(to):
            return mats_ref.at[pl.ds(pl.multiple_of(to * part, part), part), qkv_ref.shape[1] :]

        here = own_out_ref.at[:, pl.ds(pl.multiple_of(me * part, part), part)]
        others = everyone()
        greet(others)
        gather = Gather(cot_ref, cot_all_ref, *refs[23:])
        gather.start()
        turns = {blocks - 3: gather.rest, blocks - 1: gather.across}
        moves = []
        for r, to in enumerate(others):
            moves.append(push(rows_for(to), here, out_send.at[r], out_recv.at[r], to))
            moves.append(push(dt_ref.at[to], own_dt_ref.at[me], dt_send.at[r], dt_recv.at[r], to))
        moves.append(pltpu.make_async_copy(rows_for(me), here, stay.at[0]))
        moves.append(pltpu.make_async_copy(dt_ref.at[me], own_dt_ref.at[me], stay.at[1]))
        for copy in moves:
            copy.start()
    else:
        qkv_ref, att_ref, full_ref, den_ref, act_ref, xs, act, w, load, save, load_w, qz, vx = refs
        moves, turns = [], {}
    width = x_ref.shape[1]
    weights = pltpu.make_async_copy(mats_ref.at[:, : qkv_ref.shape[1]], w, load_w)
    weights.start()

    def fetch(b):
        return pltpu.make_async_copy(x_ref.at[moving(b)], xs.at[lax.rem(b, 2)], load.at[lax.rem(b, 2)])

    def keep(b):
        return pltpu.make_async_copy(act.at[lax.rem(b, 2)], act_ref.at[moving(b)], save.at[lax.rem(b, 2)])

    fetch(0).start()
    weights.wait()

    @pl.loop(0, blocks)
    def _(b):
        slot = lax.rem(b, 2)

        @pl.when(b < blocks - 1)
        def _():
            fetch(b + 1).start()

        fetch(b).wait()

        @pl.when(b >= 2)
        def _():
            keep(b - 2).wait()

        @pl.loop(0, BLK // 64)
        def _(n):
            some = pl.ds(pl.multiple_of(n * 64, 64), 64)
            x = xs[slot, some, :].astype(F32)
            factor = lax.rsqrt(jnp.sum(x * x, 1, keepdims=True) * (1.0 / width) + EPS)
            act[slot, some, :] = (x * factor * gain_ref[...]).astype(BF16)

        keep(b).start()
        qkv_ref[moving(b), :] = dot(act[slot], w[...]).astype(BF16)

    keep(blocks - 2).wait()
    keep(blocks - 1).wait()

    lay_out(heads, wide, blocks, qkv_ref, edge_ref, qz, vx)
    if linked:
        gather.turn()
    one = (lax.broadcasted_iota(jnp.int32, (BLK, wide), 1) == 0).astype(BF16)
    for b in range(blocks):
        here = spot(b)

        def weigh(c):
            s = dot_nt(qz[b], qkv_ref[c, heads * wide :]) + 1.0
            return s * s + 1.0

        def step(c, sums):
            at = moving(c)
            w = weigh(at).astype(BF16)
            return tuple(
                sums[h] + dot(w[h * BLK : (h + 1) * BLK], vx[h, at, :]) for h in range(heads)
            )

        sums = lax.fori_loop(0, b, step, (jnp.zeros((BLK, 2 * wide), F32),) * heads)
        if b == blocks - 1:
            sums = tuple(s * edge_ref[here, :] for s in sums)
        mask = same_or_later(sc_ref[here, :], sr_ref[b])
        w = weigh(here)
        for h in range(heads):
            entry = slice(h * wide, (h + 1) * wide)
            near = jnp.where(mask, w[h * BLK : (h + 1) * BLK], 0.0).astype(BF16)
            value = jnp.concatenate([qkv_ref[here, entry], one], 1)
            total = sums[h] + dot(near, value)
            den = total[:, wide : wide + 1]
            att = total[:, :wide] / den
            att_ref[here, entry] = att.astype(BF16)
            full_ref[here, entry] = att
            den_ref[here, h : h + 1] = den
        if b in turns:
            turns[b]()
    for copy in moves:
        copy.wait()
    if linked:
        gather.finish()


def attend_back_kernel(heads, wide, blocks, with_sum, *refs):
    qkv_ref, sc_ref, sr_ref, edge_ref, da_ref, full_ref, den_ref = refs[:7]
    refs = refs[7:]
    if with_sum:
        part_ref, e_ref, c_ref, act_ref, d_ref, o_ref, e_out_ref, c_out_ref, grad_ref = refs[:9]
        qz, vx, kt, near_dn, far_dn, qk_acc, v_acc = refs[9:16]
        mine, got, ex, ey, fx, fy, send, recv, local = refs[16:25]
        acts, load_act = refs[31:]
        whole = pltpu.make_async_copy(act_ref, acts, load_act)
        whole.start()
        flip = neighbours()[5]
        greet(everyone())
        s = Sum(
            mine, got, lambda k: part_ref.at[neighbours()[(4, 2, 3, 0)[k]] + flip], ex, ey, fx, fy, o_ref, send, recv
        )
        loads = [pltpu.make_async_copy(part_ref.at[s.order[k]], mine.at[k], local.at[k]) for k in range(4)]
        for k in range(4):
            s.swaps[k].start()
            loads[k].start()
        moved = [Exchange(c_ref, c_out_ref, *refs[28:31]), Exchange(e_ref, e_out_ref, *refs[25:28])]
        for one_move in moved:
            one_move.start()

        def first():
            loads[0].wait()
            s.over()

        def second():
            loads[1].wait()
            s.along_x()
            loads[2].wait()
            s.along_y()

        def fourth():
            loads[3].wait()
            s.own()

        turns = {blocks - 1: first, blocks - 2: second, blocks - 3: s.second, blocks - 4: fourth}
    else:
        d_ref, qz, vx, kt, near_dn, far_dn, qk_acc, v_acc = refs
        turns = {}
    lay_out(heads, wide, blocks, qkv_ref, edge_ref, qz, vx)

    @pl.loop(0, blocks)
    def _(b):
        kt[b] = qkv_ref[moving(b), heads * wide :].astype(F32).T.astype(BF16)

    qk_acc[...] = jnp.zeros_like(qk_acc)
    v_acc[...] = jnp.zeros_like(v_acc)
    one = (lax.broadcasted_iota(jnp.int32, (BLK, wide), 1) == 0).astype(F32)
    unit = one.astype(BF16)
    for b in reversed(range(blocks)):
        here = spot(b)
        for h in range(heads):
            entry = slice(h * wide, (h + 1) * wide)
            inv = 1.0 / den_ref[here, h : h + 1]
            da = da_ref[here, entry].astype(F32)
            dn = da * inv
            dd = -jnp.sum(dn * full_ref[here, entry], 1, keepdims=True)
            rows = slice(h * BLK, (h + 1) * BLK)
            near_dn[rows, :wide] = dn.astype(BF16)
            near_dn[rows, wide:] = (dd * one).astype(BF16)
            if b == blocks - 1:
                edge = edge_ref[here, :]
                far_dn[rows, :wide] = (dn * edge).astype(BF16)
                far_dn[rows, wide:] = (dd * edge * one).astype(BF16)

        far = far_dn if b == blocks - 1 else near_dn

        def pair(c, keys_t, grads, values, mask):
            t = dot_nt(qkv_ref[c, heads * wide :], qz[b]) + 1.0
            parts = []
            for h in range(heads):
                rows = slice(h * BLK, (h + 1) * BLK)
                t_h = t[:, rows]
                w = t_h * t_h + 1.0
                ds = dot_nt(values(h), grads[rows, :]) * t_h
                if mask is not None:
                    w = jnp.where(mask, w, 0.0)
                    ds = jnp.where(mask, ds, 0.0)
                parts.append(ds.astype(BF16))
                v_acc[c, h * wide : (h + 1) * wide] += dot(w.astype(BF16), grads[rows, :wide])
            ds = jnp.concatenate(parts, 1)
            qk_acc[c, :] += dot(ds, qz[b])
            return dot(keys_t, ds)

        def step(c, dq):
            at = moving(c)
            return dq + pair(at, kt[c], far, lambda h: vx[h, at, :], None)

        dq = lax.fori_loop(0, b, step, jnp.zeros((128, heads * BLK), F32))
        if b == 0:
            v_acc[here, :] = v_acc[here, :] * edge_ref[here, :]
        dq = dq + pair(
            here, kt[b], near_dn,
            lambda h: jnp.concatenate([qkv_ref[here, h * wide : (h + 1) * wide], unit], 1),
            later_or_same(sc_ref[here, :], sr_ref[b]),
        )
        row = lax.broadcasted_iota(jnp.int32, (128, BLK), 0)
        total = jnp.zeros((128, BLK), F32)
        for h in range(heads):
            at = (heads + h) * FEAT
            own = (row >= at) & (row < at + FEAT)
            total = jnp.where(own, dq[:, h * BLK : (h + 1) * BLK], total)
        total = total.T
        back = pltpu.roll(total, 128 - heads * FEAT, 1) * 0.5
        d_ref[here, heads * wide :] = back.astype(BF16)
        if b in turns:
            turns[b]()
    for b in range(blocks):
        here = spot(b)
        d_ref[here, : heads * wide] = v_acc[here, :].astype(BF16)
        queries = d_ref[here, heads * wide :].astype(F32)
        d_ref[here, heads * wide :] = (queries + 2.0 * qk_acc[here, :]).astype(BF16)
    if with_sum:
        whole.wait()

        @pl.loop(0, acts.shape[1] // 256)
        def _(n):
            part = pl.ds(pl.multiple_of(n * 256, 256), 256)
            grad_ref[part, :] = dot_tn(acts[:, part], d_ref[...]).astype(BF16)

        s.finish()
        for one_move in moved:
            one_move.finish()


def marks(seg):
    length = seg.shape[0]
    edge = (seg == seg[BLK - 1]).astype(F32)
    return seg[:, None], seg.reshape(length // BLK, 1, BLK), edge[:, None]


def attend(x_all, gain, mats, seg, heads, wide, dt, cot, cid):
    length, width = x_all.shape
    blocks = length // BLK
    part = heads * wide
    columns = mats.shape[1] - part
    linked = lax.axis_size("fsdp") == 8
    dma = pltpu.SemaphoreType.DMA
    args = [x_all, gain[None, :], mats, *marks(seg)]
    specs = [ANY, WHOLE, ANY, WHOLE, WHOLE, WHOLE]
    outs = [
        jax.ShapeDtypeStruct((length, columns), BF16),
        jax.ShapeDtypeStruct((length, part), BF16),
        jax.ShapeDtypeStruct((length, part), F32),
        jax.ShapeDtypeStruct((length, heads), F32),
        jax.ShapeDtypeStruct((length, width), BF16),
    ]
    out_specs = [WHOLE] * 4 + [ANY]
    scratch = [
        VMEM((2, BLK, width), BF16), VMEM((2, BLK, width), BF16), VMEM((width, columns), BF16),
        dma((2,)), dma((2,)), dma(()),
        VMEM((blocks, heads * BLK, 128), BF16), VMEM((heads, length, 2 * wide), BF16),
    ]
    params = dict(vmem_limit_bytes=48 << 20)
    if linked:
        args += [dt, cot]
        specs += [ANY, ANY]
        outs += [
            jax.ShapeDtypeStruct(dt.shape, BF16),
            jax.ShapeDtypeStruct((part, width), BF16),
            jax.ShapeDtypeStruct((8,) + cot.shape, BF16),
        ]
        out_specs += [ANY] * 3
        scratch += [dma((7,))] * 4 + [dma((2,))] + gather_scratch()
        params.update(collective_id=cid, has_side_effects=True)
    got = pl.pallas_call(
        functools.partial(attend_kernel, heads, wide, blocks, linked),
        out_shape=outs,
        in_specs=specs,
        out_specs=out_specs,
        scratch_shapes=scratch,
        compiler_params=pltpu.CompilerParams(**params),
        cost_estimate=LINKED,
        name="attend",
    )(*args)
    if linked:
        return *got[:7], got[7].reshape(length, width)
    return (
        *got,
        lax.all_to_all(dt, "fsdp", 0, 0, tiled=True),
        lax.all_to_all(mats[:, columns:], "fsdp", 0, 1, tiled=True),
        lax.all_gather(cot, "fsdp", axis=0, tiled=True),
    )


def attend_back(qkv, seg, heads, wide, da, full, den, part, moved, across, act, cid):
    length, columns = qkv.shape
    blocks = length // BLK
    width = heads * wide
    with_sum = lax.axis_size("fsdp") == 8
    args = [qkv, *marks(seg), da, full, den]
    specs = [WHOLE] * 7
    outs = [jax.ShapeDtypeStruct((length, columns), BF16)]
    scratch = [
        VMEM((blocks, heads * BLK, 128), BF16), VMEM((heads, length, 2 * wide), BF16),
        VMEM((blocks, 128, BLK), BF16), VMEM((heads * BLK, 2 * wide), BF16), VMEM((heads * BLK, 2 * wide), BF16),
        VMEM((length, 128), F32), VMEM((length, width), F32),
    ]
    if with_sum:
        rows, cols = length // 8, part.shape[1]
        args += [part.reshape(8, rows, cols), moved, across, act]
        specs += [ANY] * 4
        outs += [
            jax.ShapeDtypeStruct((rows, cols), F32),
            jax.ShapeDtypeStruct(moved.shape, moved.dtype),
            jax.ShapeDtypeStruct((8, across.shape[0], across.shape[1] // 8), across.dtype),
            jax.ShapeDtypeStruct((act.shape[1], columns), BF16),
        ]
        scratch += sum_scratch(rows, cols) + [pltpu.SemaphoreType.DMA((4,))] + 2 * exchange_scratch()
        scratch += [VMEM(act.shape, BF16), pltpu.SemaphoreType.DMA(())]
        params = pltpu.CompilerParams(
            vmem_limit_bytes=60 << 20, collective_id=cid, has_side_effects=True
        )
    else:
        params = pltpu.CompilerParams(vmem_limit_bytes=60 << 20)
    got = pl.pallas_call(
        functools.partial(attend_back_kernel, heads, wide, blocks, with_sum),
        out_shape=outs,
        in_specs=specs,
        out_specs=[WHOLE, WHOLE, ANY, ANY, WHOLE][: len(outs)],
        scratch_shapes=scratch,
        compiler_params=params,
        cost_estimate=LINKED,
        name="attend_back",
    )(*args)
    if with_sum:
        return *got[:3], got[3].reshape(-1, got[3].shape[2]), got[4]
    return (
        got[0],
        lax.psum_scatter(part, "fsdp", scatter_dimension=0, tiled=True).astype(F32),
        lax.all_to_all(moved, "fsdp", 0, 0, tiled=True),
        lax.all_to_all(across, "fsdp", 1, 0, tiled=True),
        dot_tn(act, got[0]).astype(BF16),
    )


class Exchange:
    def __init__(self, x_ref, o_ref, send, recv, local):
        me = lax.axis_index("fsdp")
        cols = o_ref.shape[2]

        def block(to):
            if len(x_ref.shape) == 3:
                return x_ref.at[to]
            return x_ref.at[:, pl.ds(pl.multiple_of(to * cols, cols), cols)]

        self.copies = [
            push(block(to), o_ref.at[me], send.at[r], recv.at[r], to) for r, to in enumerate(everyone())
        ] + [pltpu.make_async_copy(block(me), o_ref.at[me], local)]

    def start(self):
        for copy in self.copies:
            copy.start()

    def finish(self):
        for copy in self.copies:
            copy.wait()


def exchange_scratch():
    dma = pltpu.SemaphoreType.DMA
    return [dma((7,)), dma((7,)), dma(())]


def everyone():
    me = lax.axis_index("fsdp")
    return [lax.rem(me + r, 8) for r in range(1, 8)]


def tiles(cols):
    return [pl.ds(at, min(256, cols - at)) for at in range(0, cols, 256)]


def gated(gate, up):
    return gate * jax.nn.sigmoid(gate) * up


def gated_back(grad, gate, up):
    sigma = jax.nn.sigmoid(gate)
    return grad * up * sigma * (1.0 + gate * (1.0 - sigma)), grad * gate * sigma


def lane_index(rows):
    return lax.broadcasted_iota(jnp.int32, (rows, 128), 1)


def feed_kernel(
    ff, cot_ref, act_ref, w_ref, act_all_ref, gu_ref, hid_ref, grad_ref,
    acts, gus, hid, cots, acc, load, save_gu, save_hid, save_act, send, recv, local,
):
    me, sib, xn, yn, dg, flip = neighbours()
    rows = act_ref.shape[0]
    main = ff // 128 * 128
    tail = ff - main
    order = [me, sib, xn, yn, xn + flip, yn + flip, dg, dg + flip]
    cot_load = pltpu.make_async_copy(cot_ref, cots, load)
    cot_load.start()
    greet([sib, xn, yn])
    g = Gather(act_ref, acts, send, recv, local)
    g.start()

    def keep_gu(k):
        at = pl.ds(pl.multiple_of(order[k] * rows, rows), rows)
        return pltpu.make_async_copy(gus.at[k % 2], gu_ref.at[at], save_gu.at[k % 2])

    def work(k):
        q = order[k]
        if k >= 2:
            keep_gu(k - 2).wait()
        gu = gus.at[k % 2]
        for tile in tiles(w_ref.shape[1]):
            gu[:, tile] = dot(acts[q], w_ref[:, tile])
        hid[q, :, :main] = gated(gu[:, :main], gu[:, main : 2 * main]).astype(BF16)
        last = gu[:, 2 * main :]
        value = gated(last, pltpu.roll(last, 128 - tail, 1))
        hid[q, :, main:] = jnp.where(lane_index(rows) < tail, value, 0.0).astype(BF16)
        keep_gu(k).start()

    def product(first, second, here):
        return dot_tn(cots[first, :, here], hid[first]) + dot_tn(cots[second, :, here], hid[second])

    def add(first, second, start):
        @pl.loop(0, acc.shape[0] // 256)
        def _(n):
            here = pl.ds(pl.multiple_of(n * 256, 256), 256)
            value = product(first, second, here)
            acc[here, :] = value if start else acc[here, :] + value

    g.keep.wait()
    work(0)
    g.whole.wait_recv()
    work(1)
    g.turn()
    cot_load.wait()
    add(me, sib, True)
    g.rest()
    work(2)
    work(3)
    for k in range(4):
        g.core[k].wait_recv()
    work(4)
    g.across()
    work(5)
    add(xn, xn + flip, False)
    add(yn, yn + flip, False)
    work(6)
    g.core[4].wait_recv()
    g.core[5].wait_recv()
    store_act = pltpu.make_async_copy(acts, act_all_ref, save_act)
    store_act.start()
    work(7)
    store = pltpu.make_async_copy(hid, hid_ref, save_hid)
    store.start()

    @pl.loop(0, acc.shape[0] // 256)
    def _(n):
        here = pl.ds(pl.multiple_of(n * 256, 256), 256)
        grad_ref[here, :] = (acc[here, :] + product(dg, dg + flip, here)).astype(BF16)

    keep_gu(6).wait()
    keep_gu(7).wait()
    g.sent()
    store.wait()
    store_act.wait()


def feed(cot_all, act, w_gu, ff, cid):
    main = ff // 128 * 128
    tail = ff - main
    hid_cols = main + -(-tail // 128) * 128
    if lax.axis_size("fsdp") != 8:
        act = lax.all_gather(act, "fsdp", axis=0, tiled=True)
        gu = dot(act, w_gu)
        gate = jnp.concatenate([gu[:, :main], gu[:, 2 * main : 2 * main + tail]], 1)
        up = jnp.concatenate([gu[:, main : 2 * main], gu[:, 2 * main + tail : 2 * ff]], 1)
        hidden = jnp.pad(gated(gate, up), ((0, 0), (0, hid_cols - ff))).astype(BF16)
        return act, gu, hidden, dot_tn(cot_all, hidden).astype(BF16)
    rows, width = act.shape
    gu_cols = w_gu.shape[1]
    dma = pltpu.SemaphoreType.DMA
    act_all, gu, hidden, grad = pl.pallas_call(
        functools.partial(feed_kernel, ff),
        out_shape=(
            jax.ShapeDtypeStruct((8, rows, width), BF16),
            jax.ShapeDtypeStruct((8 * rows, gu_cols), F32),
            jax.ShapeDtypeStruct((8, rows, hid_cols), BF16),
            jax.ShapeDtypeStruct((width, hid_cols), BF16),
        ),
        in_specs=[ANY, ANY, WHOLE],
        out_specs=(ANY, ANY, ANY, WHOLE),
        scratch_shapes=[
            VMEM((8, rows, width), BF16), VMEM((2, rows, gu_cols), F32), VMEM((8, rows, hid_cols), BF16),
            VMEM((8, rows, width), BF16), VMEM((width, hid_cols), F32),
            dma(()), dma((2,)), dma(()), dma(()),
        ] + gather_scratch(),
        compiler_params=pltpu.CompilerParams(
            collective_id=cid, has_side_effects=True, vmem_limit_bytes=56 << 20
        ),
        cost_estimate=LINKED,
        name="feed",
    )(cot_all.reshape(8, rows, width), act, w_gu)
    return act_all.reshape(-1, width), gu, hidden.reshape(-1, hid_cols), grad


def feed_back_kernel(
    ff, cot_ref, gu_ref, act_ref, w_ref, d_ref, o_ref, grad_ref,
    acts, cots, gus, dh, dgu, out, load_act, load_cot, load_gu, mine, got, ex, ey, fx, fy, send, recv,
):
    me, sib, xn, yn, dg, flip = neighbours()
    rows, cols = o_ref.shape
    main = ff // 128 * 128
    tail = ff - main
    order = [dg + flip, dg, xn + flip, xn, yn + flip, yn, me + flip, me]

    def fetch(k):
        q, slot = order[k], k % 2
        return [
            pltpu.make_async_copy(cot_ref.at[q], cots.at[slot], load_cot.at[slot]),
            pltpu.make_async_copy(gu_ref.at[q], gus.at[slot], load_gu.at[slot]),
        ]

    for copy in fetch(0):
        copy.start()
    whole = pltpu.make_async_copy(act_ref, acts, load_act)
    whole.start()
    greet([sib, xn, yn])
    s = Sum(mine, got, out.at.__getitem__, ex, ey, fx, fy, o_ref, send, recv)

    def block(k, to):
        if k < 7:
            for copy in fetch(k + 1):
                copy.start()
        for copy in fetch(k):
            copy.wait()
        slot, q = k % 2, order[k]
        gu = gus.at[slot]
        for tile in tiles(d_ref.shape[1]):
            dh[:, tile] = dot(cots[slot], d_ref[:, tile])
        here = pl.ds(pl.multiple_of(q * rows, rows), rows)
        d_gate, d_up = gated_back(dh[:, :main], gu[:, :main], gu[:, main : 2 * main])
        dgu[here, :main] = d_gate.astype(BF16)
        dgu[here, main : 2 * main] = d_up.astype(BF16)
        last = gu[:, 2 * main :]
        d_gate, d_up = gated_back(dh[:, main:], last, pltpu.roll(last, 128 - tail, 1))
        lane = lane_index(rows)
        both = jnp.where(lane < tail, d_gate, jnp.where(lane < 2 * tail, pltpu.roll(d_up, tail, 1), 0.0))
        dgu[here, 2 * main :] = both.astype(BF16)

        @pl.loop(0, cols // 256)
        def _(n):
            part = pl.ds(pl.multiple_of(n * 256, 256), 256)
            to[:, part] = dot_nt(dgu[here, :], w_ref[part, :]).astype(BF16)

    def away(k):
        block(2 * k, out.at[k])
        s.swaps[k].start()

    def home(k):
        block(2 * k + 1, mine.at[k])

    away(0)
    home(0)
    s.over()
    away(1)
    home(1)
    s.along_x()
    away(2)
    home(2)
    s.along_y()
    s.second()
    away(3)
    home(3)
    s.own()
    whole.wait()

    @pl.loop(0, cols // 256)
    def _(n):
        part = pl.ds(pl.multiple_of(n * 256, 256), 256)
        grad_ref[part, :] = dot_tn(acts[:, part], dgu[...]).astype(BF16)

    s.finish()


def feed_back(cot_all, gu, act, w_gu, w_dt, ff, cid):
    main = ff // 128 * 128
    tail = ff - main
    if lax.axis_size("fsdp") != 8:
        gate = jnp.concatenate([gu[:, :main], gu[:, 2 * main : 2 * main + tail]], 1)
        up = jnp.concatenate([gu[:, main : 2 * main], gu[:, 2 * main + tail : 2 * ff]], 1)
        d_gate, d_up = gated_back(dot(cot_all, w_dt)[:, :ff], gate, up)
        d_gu = jnp.concatenate(
            [d_gate[:, :main], d_up[:, :main], d_gate[:, main:], d_up[:, main:],
             jnp.zeros((gu.shape[0], gu.shape[1] - 2 * ff), F32)], 1
        ).astype(BF16)
        part = lax.psum_scatter(
            dot_nt(d_gu, w_gu).astype(BF16), "fsdp", scatter_dimension=0, tiled=True
        )
        return part.astype(F32), dot_tn(act, d_gu).astype(BF16)
    length, width = act.shape
    rows, gu_cols, hid_cols = length // 8, gu.shape[1], w_dt.shape[1]
    dma = pltpu.SemaphoreType.DMA
    return pl.pallas_call(
        functools.partial(feed_back_kernel, ff),
        out_shape=(
            jax.ShapeDtypeStruct((rows, width), F32),
            jax.ShapeDtypeStruct((width, gu_cols), BF16),
        ),
        in_specs=[ANY, ANY, ANY, WHOLE, WHOLE],
        out_specs=(WHOLE, WHOLE),
        scratch_shapes=[
            VMEM((length, width), BF16), VMEM((2, rows, width), BF16), VMEM((2, rows, gu_cols), F32),
            VMEM((rows, hid_cols), F32), VMEM((length, gu_cols), BF16), VMEM((4, rows, width), BF16),
            dma(()), dma((2,)), dma((2,)),
        ] + sum_scratch(rows, width),
        compiler_params=pltpu.CompilerParams(
            collective_id=cid, has_side_effects=True, vmem_limit_bytes=61 << 20
        ),
        cost_estimate=LINKED,
        name="feed_back",
    )(cot_all.reshape(8, rows, width), gu.reshape(8, rows, gu_cols), act, w_gu, w_dt)


def project_back_kernel(
    p_ref, hid_ref, d_ref, w_ref, mix_ref, att_ref, part_ref, grad_ref,
    rowed, parts, acc, save, send, recv, local,
):
    me, sib, xn, yn, dg, flip = neighbours()
    rows, cols = p_ref.shape
    greet([sib, xn, yn])
    g = Gather(p_ref, rowed, send, recv, local)
    g.start()

    def side(lo, hi):
        @pl.loop(lo, hi)
        def _(b):
            left = hid_ref[pl.ds(pl.multiple_of(b * rows, rows), rows), :]
            for tile in tiles(cols):
                parts[b, :, tile] = dot_nt(left, d_ref[tile, :]).astype(BF16)

    def use(q, start):
        at = pl.ds(pl.multiple_of(q * rows, rows), rows)
        att_ref[at, :] = dot_nt(rowed[q], w_ref[...]).astype(BF16)
        left = mix_ref[at, :]
        for tile in tiles(cols):
            value = dot_tn(left, rowed[q, :, tile])
            acc[:, tile] = value if start else acc[:, tile] + value

    side(0, 5)
    g.turn()
    side(5, 8)
    store = pltpu.make_async_copy(parts, part_ref, save)
    store.start()
    g.keep.wait()
    use(me, True)
    g.whole.wait_recv()
    use(sib, False)
    g.rest()
    use(xn, False)
    use(yn, False)
    g.across()
    use(dg, False)
    for k in range(4):
        g.core[k].wait_recv()
    use(xn + flip, False)
    use(yn + flip, False)
    g.core[4].wait_recv()
    g.core[5].wait_recv()
    use(dg + flip, False)
    grad_ref[...] = acc[...].astype(BF16)
    g.sent()
    store.wait()


def project_back(d_proj, hidden, w_dt, w_o, mixed, cid):
    if lax.axis_size("fsdp") != 8:
        d_proj = lax.all_gather(d_proj, "fsdp", axis=0, tiled=True)
        return (
            dot_nt(d_proj, w_o).astype(BF16),
            dot_nt(hidden, w_dt).astype(BF16),
            dot_tn(mixed, d_proj).astype(BF16),
        )
    rows, width = d_proj.shape
    own = w_o.shape[0]
    att, part, grad = pl.pallas_call(
        project_back_kernel,
        out_shape=(
            jax.ShapeDtypeStruct((8 * rows, own), BF16),
            jax.ShapeDtypeStruct((8, rows, width), BF16),
            jax.ShapeDtypeStruct((own, width), BF16),
        ),
        in_specs=[ANY] + [WHOLE] * 4,
        out_specs=(WHOLE, ANY, WHOLE),
        scratch_shapes=[
            VMEM((8, rows, width), BF16), VMEM((8, rows, width), BF16), VMEM((own, width), F32),
            pltpu.SemaphoreType.DMA(()),
        ] + gather_scratch(),
        compiler_params=pltpu.CompilerParams(
            collective_id=cid, has_side_effects=True, vmem_limit_bytes=50 << 20
        ),
        cost_estimate=LINKED,
        name="project_back",
    )(d_proj, hidden, w_dt, w_o, mixed)
    return att, part.reshape(8 * rows, width), grad


def group(arrays, groups):
    parts = jnp.concatenate([a.reshape(a.shape[0], groups, -1) for a in arrays], -1)
    return jnp.transpose(parts, (1, 0, 2))


def over_rows(own):
    return lax.all_gather(own.reshape(-1, own.shape[-1]), "dp", axis=0, tiled=True)


def sum_rows(array):
    return lax.psum_scatter(array, "dp", scatter_dimension=0, tiled=True)


def to_owners(part, groups):
    part = part.reshape(groups, part.shape[0] // groups, -1)
    return jnp.transpose(lax.all_to_all(part, "fsdp", 0, 0, tiled=True), (1, 0, 2)).astype(F32)


def columns(array, lo, hi):
    return array[:, :, lo:hi].reshape(array.shape[0], -1)


def after(value, *others):
    return lax.optimization_barrier((value,) + others)[0]


def on_device(
    layer_input, doc_starts, norm1_gain, w_query, w_key, w_value, w_out, norm2_gain,
    w_gate, w_up, w_down, cotangent,
):
    n_f = lax.axis_size("fsdp")
    x = layer_input[0]
    cot = cotangent[0]
    tokens, width = x.shape
    length = tokens * n_f
    kv = w_query.shape[1]
    rows = w_query.shape[0]
    ff = w_gate.shape[1]
    ff_own, qk_own, v_own = ff // n_f, kv // n_f, width // n_f
    heads = qk_own // FEAT
    wide = v_own // heads
    used = v_own + 2 * qk_own
    gain_at = used
    qkv_cols = v_own + 128
    att_cols = qkv_cols + v_own

    def blocked(a):
        return a.reshape(n_f, a.shape[0] // n_f, a.shape[1])

    def each(vec):
        return jnp.broadcast_to(vec[:, None, None], (rows, n_f, 1))

    attn = group(
        [w_value, w_query, w_key, each(norm1_gain), each(norm2_gain),
         jnp.zeros((rows, n_f, qkv_cols - used - 2), BF16), w_out],
        n_f,
    )
    attn = over_rows(lax.all_to_all(attn, "fsdp", 0, 0, tiled=True))
    main = ff_own // 128 * 128

    def halves(a):
        return a[:, : n_f * main].reshape(rows, n_f, main), a[:, n_f * main :].reshape(rows, n_f, -1)

    (gate_main, gate_tail), (up_main, up_tail) = halves(w_gate), halves(w_up)
    empty = jnp.zeros((rows, n_f, 128), BF16)
    gu = group(
        [gate_main, up_main, gate_tail, up_tail, empty[:, :, : -(2 * ff_own) % 128]], n_f
    )
    x_all, gu_part = start_exchange(x, gu, 0)
    w_gu = over_rows(gu_part)
    dt = group([*halves(w_down.T), empty[:, :, : -ff_own % 128]], n_f)
    gain_one = attn[:, gain_at].astype(F32)
    gain_two = attn[:, gain_at + 1].astype(F32)
    places = jnp.arange(length, dtype=jnp.int32)
    seg = jnp.sum((doc_starts[0][None, :] <= places[:, None]).astype(jnp.int32), 1)
    qkv, mixed, full, den, act_one, dt_part, w_o, cot_all = attend(
        x_all, gain_one, attn, seg, heads, wide, dt, cot, 3
    )
    w_dt = over_rows(dt_part)
    resid, act_two = product_sum(mixed, w_o, False, 2, x, gain_two)
    factor_two = lax.rsqrt(jnp.mean(resid * resid, -1, keepdims=True) + EPS)
    act_two, gate_up, hidden, g_dt = feed(cot_all, act_two, w_gu, ff_own, 1)
    d_act_two, g_gu = feed_back(cot_all, gate_up, act_two, w_gu, w_dt, ff_own, 4)
    g_dt = sum_rows(g_dt)
    g_gu = sum_rows(after(g_gu, g_dt))

    d_norm, _ = rms_back(d_act_two, resid, factor_two, gain_two)
    d_resid = cot.astype(F32) + d_norm
    d_att, out_part, g_out = project_back(d_resid.astype(BF16), hidden, w_dt, w_o, mixed, 5)
    d_qkv, out_sum, g_dt, g_out, g_qkv = attend_back(
        qkv, seg, heads, wide, d_att, full, den, out_part, blocked(g_dt), g_out, act_one, 7
    )
    grad_input, grad_gate, grad_up, grad_dt, along = product_sum(
        after(d_qkv, g_qkv), attn, True, 6, x, gain_one, d_resid, blocked(g_gu), g_dt, w_gu, ff_own
    )

    g_out = sum_rows(after(g_out, g_gu))
    g_qkv = sum_rows(after(g_qkv, g_gu))
    own_rows = lax.axis_index("dp") * (width // lax.axis_size("dp"))

    def mine(value):
        return lax.dynamic_slice_in_dim(value, own_rows, g_qkv.shape[0], 0)

    gains = jnp.stack(
        [
            jnp.sum(mine(attn)[:, :qkv_cols].astype(F32) * g_qkv.astype(F32), 1) / mine(gain_one),
            along[:, 0] / mine(gain_two),
        ],
        1,
    )
    filler = jnp.zeros((g_qkv.shape[0], qkv_cols - used - 2), BF16)
    g_attn = jnp.concatenate([g_qkv[:, :used], gains.astype(BF16), filler, g_out], 1)
    g_attn = to_owners(g_attn, n_f)

    output = (resid + out_sum).astype(BF16)[None]
    return (
        output,
        grad_input[None],
        jnp.sum(g_attn[:, :, gain_at], 1),
        columns(g_attn, v_own, v_own + qk_own),
        columns(g_attn, v_own + qk_own, used),
        columns(g_attn, 0, v_own),
        columns(g_attn, qkv_cols, att_cols),
        jnp.sum(g_attn[:, :, gain_at + 1], 1),
        grad_gate,
        grad_up,
        grad_dt.T,
    )


def solution(mesh):
    rows, cols = P(ALL, None), P(None, ALL)
    toks = P("dp", "fsdp", None)
    return jax.shard_map(
        on_device,
        mesh=mesh,
        in_specs=(toks, P("dp", None), P(ALL), rows, rows, rows, rows, P(ALL), rows, rows, cols, toks),
        out_specs=(toks, toks, P(ALL), rows, rows, rows, rows, P(ALL), rows, rows, cols),
        check_vma=False,
    )
```

```python
import functools

import jax
import jax.numpy as jnp
from jax import lax
from jax.experimental import pallas as pl
from jax.experimental.pallas import tpu as pltpu
from jax.sharding import PartitionSpec as P

FEAT = 16
EPS = 1e-05
BLK = 256
F32 = jnp.float32
BF16 = jnp.bfloat16
NT = (((1,), (1,)), ((), ()))
TN = (((0,), (0,)), ((), ()))
VMEM = pltpu.VMEM
ALL = ("dp", "fsdp")
MESH = pl.DeviceIdType.MESH


def dot(a, b):
    return jnp.dot(a, b, preferred_element_type=F32)


def dot_nt(a, b):
    return lax.dot_general(a, b, NT, preferred_element_type=F32)


def dot_tn(a, b):
    return lax.dot_general(a, b, TN, preferred_element_type=F32)


def rms_apply(values, gain):
    factor = lax.rsqrt(jnp.mean(values * values, -1, keepdims=True) + EPS)
    return values * factor * gain, factor


def rms_back(grad, values, factor, gain):
    normed = values * factor
    grad_gain = jnp.sum(grad * normed, 0)
    inner = grad * gain
    grad_in = factor * (inner - normed * jnp.mean(inner * normed, -1, keepdims=True))
    return grad_in, grad_gain


def neighbours():
    me = lax.axis_index("fsdp")
    core, side, line = lax.rem(me, 2), lax.rem(me // 2, 2), me // 4

    def at(y, x, c):
        return 4 * y + 2 * x + c

    return (
        me,
        at(line, side, 1 - core),
        at(line, 1 - side, core),
        at(1 - line, side, core),
        at(1 - line, 1 - side, core),
        1 - 2 * core,
    )


def greet(others):
    barrier = pltpu.get_barrier_semaphore()
    for other in others:
        pl.semaphore_signal(barrier, inc=1, device_id={"fsdp": other}, device_id_type=MESH)
    pl.semaphore_wait(barrier, len(others))


def push(src, dst, send, recv, to):
    return pltpu.make_async_remote_copy(
        src_ref=src, dst_ref=dst, send_sem=send, recv_sem=recv,
        device_id={"fsdp": to}, device_id_type=MESH,
    )


class Gather:
    COPIES = 13

    def __init__(self, x_ref, o_ref, send, recv, local):
        me, sib, xn, yn, dg, _ = neighbours()
        half = x_ref.shape[0] // 2
        lo, hi = pl.ds(0, half), pl.ds(half, half)

        def own(part, to, k):
            return push(x_ref.at[part], o_ref.at[me, part], send.at[k], recv.at[k], to)

        def on(who, part, to, k):
            spot = o_ref.at[who, part]
            return push(spot, spot, send.at[k], recv.at[k], to)

        self.keep = pltpu.make_async_copy(x_ref, o_ref.at[me], local)
        self.x_hi, self.y_lo = own(hi, xn, 0), own(lo, yn, 1)
        self.x_lo, self.y_hi = own(lo, xn, 2), own(hi, yn, 3)
        self.whole = push(x_ref, o_ref.at[me], send.at[4], recv.at[4], sib)
        self.over_x, self.over_y = on(yn, lo, xn, 5), on(xn, hi, yn, 7)
        self.core = [
            on(yn, lo, sib, 6), on(xn, hi, sib, 8), on(xn, lo, sib, 9),
            on(yn, hi, sib, 10), on(dg, lo, sib, 11), on(dg, hi, sib, 12),
        ]

    def start(self):
        self.keep.start()
        for copy in (self.x_hi, self.y_lo, self.x_lo, self.y_hi, self.whole):
            copy.start()

    def turn(self):
        self.y_lo.wait_recv()
        self.over_x.start()
        self.core[0].start()
        self.x_hi.wait_recv()
        self.over_y.start()
        self.core[1].start()

    def rest(self):
        self.x_lo.wait_recv()
        self.core[2].start()
        self.y_hi.wait_recv()
        self.core[3].start()

    def across(self):
        self.over_x.wait_recv()
        self.core[4].start()
        self.over_y.wait_recv()
        self.core[5].start()

    def finish(self):
        self.whole.wait_recv()
        for copy in self.core:
            copy.wait_recv()
        self.sent()
        self.keep.wait()

    def sent(self):
        for copy in [self.x_hi, self.y_lo, self.x_lo, self.y_hi, self.whole, self.over_x, self.over_y] + self.core:
            copy.wait_send()


def gather_scratch():
    dma = pltpu.SemaphoreType.DMA
    return [dma((Gather.COPIES,)), dma((Gather.COPIES,)), dma(())]


ANY = pl.BlockSpec(memory_space=pl.ANY)
LINKED = pl.CostEstimate(flops=45 * 10**9, bytes_accessed=10**8, transcendentals=0)
WHOLE = pl.BlockSpec(memory_space=VMEM)


class Sum:
    COPIES = 10

    def __init__(self, mine, got, away, ex, ey, fx, fy, total, send, recv):
        me, sib, xn, yn, dg, self.flip = neighbours()
        half = fx.shape[0] // 2
        self.lo, self.hi = lo, hi = pl.ds(0, half), pl.ds(half, half)
        self.order = [dg, xn, yn, me]
        self.mine, self.got, self.ex, self.ey, self.fx, self.fy, self.total = mine, got, ex, ey, fx, fy, total
        self.swaps = [push(away(k), got.at[k], send.at[k], recv.at[k], sib) for k in range(4)]
        self.a = push(mine.at[0, lo], ey, send.at[4], recv.at[4], yn)
        self.b = push(mine.at[0, hi], ex, send.at[5], recv.at[5], xn)
        self.c = push(mine.at[1, hi], fx.at[hi], send.at[6], recv.at[6], xn)
        self.d = push(mine.at[2, lo], fy.at[lo], send.at[7], recv.at[7], yn)
        self.e = push(mine.at[1, lo], fx.at[lo], send.at[8], recv.at[8], xn)
        self.f = push(mine.at[2, hi], fy.at[hi], send.at[9], recv.at[9], yn)

    def add(self, k, part, more=None):
        value = self.mine[k, part].astype(F32) + self.got[k, part].astype(F32)
        if more is not None:
            value = value + more[...].astype(F32)
        self.mine[k, part] = value.astype(BF16)

    def over(self):
        self.swaps[0].wait_recv()
        self.add(0, self.lo)
        self.a.start()
        self.add(0, self.hi)
        self.b.start()

    def along_x(self):
        self.swaps[1].wait_recv()
        self.add(1, self.hi)
        self.c.start()

    def along_y(self):
        self.swaps[2].wait_recv()
        self.add(2, self.lo)
        self.d.start()

    def second(self):
        self.a.wait_recv()
        self.add(1, self.lo, self.ey)
        self.e.start()
        self.b.wait_recv()
        self.add(2, self.hi, self.ex)
        self.f.start()

    def own(self):
        self.swaps[3].wait_recv()
        self.total[...] = self.mine[3].astype(F32) + self.got[3].astype(F32)

    def finish(self):
        for copy in (self.c, self.d, self.e, self.f):
            copy.wait_recv()
        self.total[...] += self.fx[...].astype(F32) + self.fy[...].astype(F32)
        for copy in self.swaps + [self.a, self.b, self.c, self.d, self.e, self.f]:
            copy.wait_send()


def sum_scratch(rows, cols):
    dma = pltpu.SemaphoreType.DMA
    return [
        VMEM((4, rows, cols), BF16), VMEM((4, rows, cols), BF16), VMEM((rows // 2, cols), BF16),
        VMEM((rows // 2, cols), BF16), VMEM((rows, cols), BF16), VMEM((rows, cols), BF16),
        dma((Sum.COPIES,)), dma((Sum.COPIES,)),
    ]


def regroup(body, end, main, tail, o_ref):
    width = 8 * tail
    lane = lax.broadcasted_iota(jnp.int32, (o_ref.shape[0], width), 1)
    tails = jnp.zeros((o_ref.shape[0], width), F32)
    for j in range(8):
        o_ref[:, j * main : (j + 1) * main] = body(j)
        piece = jnp.concatenate([end(j), jnp.zeros((o_ref.shape[0], width - 128), F32)], 1)
        piece = pltpu.roll(piece, j * tail, 1) if j else piece
        tails = jnp.where((lane >= j * tail) & (lane < (j + 1) * tail), piece, tails)
    o_ref[:, 8 * main :] = tails.astype(BF16)


def product_sum_kernel(turned, normed, l_ref, r_ref, *refs):
    if normed:
        x_ref, gain_ref, o_ref, act, out, mine, got, ex, ey, fx, fy, send, recv = refs
        _, sib, xn, yn, _, _ = neighbours()
        greet([sib, xn, yn])
    else:
        x_ref, gain_ref, e_ref, dt_ref, w_ref, o_ref, gate_ref, up_ref, down_ref, along_ref = refs[:10]
        out, mine, got, ex, ey, fx, fy, send, recv = refs[10:19]
        own_gu, gu, w, load_gu, load_w = refs[19:24]
        loads = [
            pltpu.make_async_copy(e_ref, gu, load_gu),
            pltpu.make_async_copy(w_ref.at[pl.ds(lax.axis_index("dp") * w.shape[0], w.shape[0])], w, load_w),
        ]
        for load in loads:
            load.start()
        greet(everyone())
        moved = Exchange(e_ref, own_gu, *refs[24:])
        moved.start()
    rows, cols = o_ref.shape
    depth = l_ref.shape[1]
    s = Sum(mine, got, out.at.__getitem__, ex, ey, fx, fy, o_ref, send, recv)

    def block(q, to):
        left = l_ref[pl.ds(pl.multiple_of(q * rows, rows), rows), :]

        @pl.loop(0, cols // 256)
        def _(n):
            here = pl.ds(pl.multiple_of(n * 256, 256), 256)
            part = dot_nt(left, r_ref[here, :depth]) if turned else dot(left, r_ref[:, here])
            to[:, here] = part.astype(BF16)

    def away(k):
        block(s.order[k] + s.flip, out.at[k])
        s.swaps[k].start()

    def home(k):
        block(s.order[k], mine.at[k])

    away(0)
    home(0)
    away(1)
    s.over()
    home(1)
    s.along_x()
    away(2)
    home(2)
    s.along_y()
    away(3)
    s.second()
    home(3)
    s.own()
    if not normed:
        for load in loads:
            load.wait()
        some_rows = gu.shape[1]
        for j in range(8):
            here = slice(j * some_rows, (j + 1) * some_rows)
            along_ref[here, :] = jnp.sum(w[here, :].astype(F32) * gu[j].astype(F32), 1, keepdims=True)
        main = down_ref.shape[1] // 8 // 128 * 128
        tail = down_ref.shape[1] // 8 - main
        regroup(lambda j: dt_ref[j, :, :main], lambda j: dt_ref[j, :, main:].astype(F32), main, tail, down_ref)
    s.finish()
    if not normed:
        @pl.loop(0, rows // 64)
        def _(n):
            some = pl.ds(pl.multiple_of(n * 64, 64), 64)
            value = x_ref[some, :].astype(F32)
            factor = lax.rsqrt(jnp.sum(value * value, 1, keepdims=True) * (1.0 / cols) + EPS)
            value = value * factor
            inner = o_ref[some, :] * gain_ref[...]
            along = jnp.sum(inner * value, 1, keepdims=True) * (1.0 / cols)
            o_ref[some, :] = factor * (inner - value * along)

        moved.finish()

        def turned_tail(j):
            return pltpu.roll(own_gu[j, :, 2 * main :].astype(F32), 128 - tail, 1)

        regroup(
            lambda j: own_gu[j, :, :main], lambda j: own_gu[j, :, 2 * main :].astype(F32), main, tail, gate_ref
        )
        regroup(lambda j: own_gu[j, :, main : 2 * main], turned_tail, main, tail, up_ref)
    else:
        @pl.loop(0, rows // 64)
        def _(n):
            some = pl.ds(pl.multiple_of(n * 64, 64), 64)
            value = x_ref[some, :].astype(F32) + o_ref[some, :]
            factor = lax.rsqrt(jnp.sum(value * value, 1, keepdims=True) * (1.0 / cols) + EPS)
            o_ref[some, :] = value
            act[some, :] = (value * factor * gain_ref[...]).astype(BF16)


def product_sum(left, right, turned, cid, x, gain, moved=None, down=None, w_gu=None, ff=0):
    depth = left.shape[1]
    if lax.axis_size("fsdp") != 8:
        part = (dot_nt(left, right[:, :depth]) if turned else dot(left, right)).astype(BF16)
        part = lax.psum_scatter(part, "fsdp", scatter_dimension=0, tiled=True).astype(F32)
        if moved is not None:
            n_f, some, columns_own = moved.shape
            x = x.astype(F32)
            part, _ = rms_back(part, x, rms_apply(x, gain)[1], gain)
            at = lax.axis_index("dp") * n_f * some
            w = lax.dynamic_slice_in_dim(w_gu, at, n_f * some, 0).reshape(moved.shape)
            along = jnp.sum(w.astype(F32) * moved.astype(F32), 2).reshape(-1, 1)
            moved = lax.all_to_all(moved, "fsdp", 0, 0, tiled=True)
            main = ff // 128 * 128

            def owner(grads, at, end):
                parts = [grads[:, :, at : at + main], grads[:, :, end : end + ff - main]]
                parts = [jnp.transpose(p, (1, 0, 2)).reshape(some, -1) for p in parts]
                return jnp.concatenate(parts, 1)

            grads = owner(moved, 0, 2 * main), owner(moved, main, main + ff), owner(down, 0, main)
            return part, *grads, along
        part = part + x.astype(F32)
        act = rms_apply(part, gain)[0].astype(BF16)
        return part, act
    rows, cols = left.shape[0] // 8, right.shape[0 if turned else 1]
    args, specs = [left, right, x, gain[None, :]], [WHOLE] * 4
    outs, out_specs = [jax.ShapeDtypeStruct((rows, cols), F32)], [WHOLE]
    scratch = [VMEM((4, rows, cols), BF16)] + sum_scratch(rows, cols)
    if moved is None:
        outs.append(jax.ShapeDtypeStruct((rows, cols), BF16))
        out_specs.append(WHOLE)
    else:
        args += [moved, down, w_gu]
        specs += [ANY, WHOLE, ANY]
        some = moved.shape[1]
        outs += [jax.ShapeDtypeStruct((some, 8 * ff), BF16)] * 3 + [jax.ShapeDtypeStruct((8 * some, 1), F32)]
        out_specs += [WHOLE] * 4
        scratch += [
            VMEM(moved.shape, BF16), VMEM(moved.shape, BF16), VMEM((8 * some, moved.shape[2]), BF16),
            pltpu.SemaphoreType.DMA(()), pltpu.SemaphoreType.DMA(()),
        ] + exchange_scratch()
    got = pl.pallas_call(
        functools.partial(product_sum_kernel, turned, moved is None),
        out_shape=outs,
        in_specs=specs,
        out_specs=out_specs,
        scratch_shapes=scratch,
        compiler_params=pltpu.CompilerParams(
            collective_id=cid, has_side_effects=True, vmem_limit_bytes=56 << 20
        ),
        cost_estimate=LINKED,
        name="product_sum",
    )(*args)
    return got


def start_kernel(x_ref, a_ref, ox_ref, oa_ref, send, recv, local, a_send, a_recv, keep):
    me = lax.axis_index("fsdp")
    others = [lax.rem(me + r, 8) for r in range(1, 8)]
    greet(others)
    g = Gather(x_ref, ox_ref, send, recv, local)
    g.start()
    moves = []
    for r, to in enumerate(others):
        moves.append(push(a_ref.at[to], oa_ref.at[me], a_send.at[r], a_recv.at[r], to))
    stay = [pltpu.make_async_copy(a_ref.at[me], oa_ref.at[me], keep)]
    for copy in moves + stay:
        copy.start()
    g.turn()
    g.rest()
    g.across()
    g.finish()
    for copy in moves + stay:
        copy.wait()


def start_exchange(x, a, cid):
    if lax.axis_size("fsdp") != 8:
        return (
            lax.all_gather(x, "fsdp", axis=0, tiled=True),
            lax.all_to_all(a, "fsdp", 0, 0, tiled=True),
        )
    dma = pltpu.SemaphoreType.DMA
    x_all, a = pl.pallas_call(
        start_kernel,
        out_shape=(
            jax.ShapeDtypeStruct((8,) + x.shape, x.dtype),
            jax.ShapeDtypeStruct(a.shape, a.dtype),
        ),
        in_specs=[ANY] * 2,
        out_specs=(ANY,) * 2,
        scratch_shapes=gather_scratch() + [dma((7,))] * 2 + [dma(())],
        compiler_params=pltpu.CompilerParams(collective_id=cid, has_side_effects=True),
        cost_estimate=LINKED,
        name="start_exchange",
    )(x, a)
    return x_all.reshape(-1, x.shape[1]), a


def same_or_later(seg_rows, seg_cols):
    rows = lax.broadcasted_iota(jnp.int32, (BLK, BLK), 0)
    cols = lax.broadcasted_iota(jnp.int32, (BLK, BLK), 1)
    return (seg_rows == seg_cols) & (cols <= rows)


def later_or_same(seg_keys, seg_queries):
    keys = lax.broadcasted_iota(jnp.int32, (BLK, BLK), 0)
    queries = lax.broadcasted_iota(jnp.int32, (BLK, BLK), 1)
    return (seg_keys == seg_queries) & (keys <= queries)


def spot(b):
    return pl.ds(b * BLK, BLK)


def moving(c):
    return pl.ds(pl.multiple_of(c * BLK, BLK), BLK)


def lanes_of(h, heads):
    lane = lax.broadcasted_iota(jnp.int32, (BLK, 128), 1)
    at = (heads + h) * FEAT
    return (lane >= at) & (lane < at + FEAT)


def lay_out(heads, wide, blocks, qkv_ref, edge_ref, qz, vx):
    first = (lax.broadcasted_iota(jnp.int32, (BLK, wide), 1) == 0).astype(F32)

    @pl.loop(0, blocks)
    def _(b):
        here = moving(b)
        tile = qkv_ref[here, heads * wide :].astype(F32)
        turned = pltpu.roll(tile, heads * FEAT, 1) * 0.25
        edge = edge_ref[here, :]
        for h in range(heads):
            qz[b, h * BLK : (h + 1) * BLK, :] = jnp.where(lanes_of(h, heads), turned, 0.0).astype(BF16)
            vx[h, here, :wide] = (qkv_ref[here, h * wide : (h + 1) * wide].astype(F32) * edge).astype(BF16)
            vx[h, here, wide:] = (first * edge).astype(BF16)


def attend_kernel(heads, wide, blocks, linked, *refs):
    x_ref, gain_ref, mats_ref, sc_ref, sr_ref, edge_ref = refs[:6]
    refs = refs[6:]
    if linked:
        dt_ref, cot_ref = refs[:2]
        qkv_ref, att_ref, full_ref, den_ref, act_ref, own_dt_ref, own_out_ref, cot_all_ref = refs[2:10]
        xs, act, w, load, save, load_w, qz, vx, dt_send, dt_recv, out_send, out_recv, stay = refs[10:23]
        me = lax.axis_index("fsdp")
        part = heads * wide

        def rows_for(to):
            return mats_ref.at[pl.ds(pl.multiple_of(to * part, part), part), qkv_ref.shape[1] :]

        here = own_out_ref.at[:, pl.ds(pl.multiple_of(me * part, part), part)]
        others = everyone()
        greet(others)
        gather = Gather(cot_ref, cot_all_ref, *refs[23:])
        gather.start()
        turns = {blocks - 3: gather.rest, blocks - 1: gather.across}
        moves = []
        for r, to in enumerate(others):
            moves.append(push(rows_for(to), here, out_send.at[r], out_recv.at[r], to))
            moves.append(push(dt_ref.at[to], own_dt_ref.at[me], dt_send.at[r], dt_recv.at[r], to))
        moves.append(pltpu.make_async_copy(rows_for(me), here, stay.at[0]))
        moves.append(pltpu.make_async_copy(dt_ref.at[me], own_dt_ref.at[me], stay.at[1]))
        for copy in moves:
            copy.start()
    else:
        qkv_ref, att_ref, full_ref, den_ref, act_ref, xs, act, w, load, save, load_w, qz, vx = refs
        moves, turns = [], {}
    width = x_ref.shape[1]
    weights = pltpu.make_async_copy(mats_ref.at[:, : qkv_ref.shape[1]], w, load_w)
    weights.start()

    def fetch(b):
        return pltpu.make_async_copy(x_ref.at[moving(b)], xs.at[lax.rem(b, 2)], load.at[lax.rem(b, 2)])

    def keep(b):
        return pltpu.make_async_copy(act.at[lax.rem(b, 2)], act_ref.at[moving(b)], save.at[lax.rem(b, 2)])

    fetch(0).start()
    weights.wait()

    @pl.loop(0, blocks)
    def _(b):
        slot = lax.rem(b, 2)

        @pl.when(b < blocks - 1)
        def _():
            fetch(b + 1).start()

        fetch(b).wait()

        @pl.when(b >= 2)
        def _():
            keep(b - 2).wait()

        @pl.loop(0, BLK // 64)
        def _(n):
            some = pl.ds(pl.multiple_of(n * 64, 64), 64)
            x = xs[slot, some, :].astype(F32)
            factor = lax.rsqrt(jnp.sum(x * x, 1, keepdims=True) * (1.0 / width) + EPS)
            act[slot, some, :] = (x * factor * gain_ref[...]).astype(BF16)

        keep(b).start()
        qkv_ref[moving(b), :] = dot(act[slot], w[...]).astype(BF16)

    keep(blocks - 2).wait()
    keep(blocks - 1).wait()

    lay_out(heads, wide, blocks, qkv_ref, edge_ref, qz, vx)
    if linked:
        gather.turn()
    one = (lax.broadcasted_iota(jnp.int32, (BLK, wide), 1) == 0).astype(BF16)
    for b in range(blocks):
        here = spot(b)

        def weigh(c):
            s = dot_nt(qz[b], qkv_ref[c, heads * wide :]) + 1.0
            return s * s + 1.0

        def step(c, sums):
            at = moving(c)
            w = weigh(at).astype(BF16)
            return tuple(
                sums[h] + dot(w[h * BLK : (h + 1) * BLK], vx[h, at, :]) for h in range(heads)
            )

        sums = lax.fori_loop(0, b, step, (jnp.zeros((BLK, 2 * wide), F32),) * heads)
        if b == blocks - 1:
            sums = tuple(s * edge_ref[here, :] for s in sums)
        mask = same_or_later(sc_ref[here, :], sr_ref[b])
        w = weigh(here)
        for h in range(heads):
            entry = slice(h * wide, (h + 1) * wide)
            near = jnp.where(mask, w[h * BLK : (h + 1) * BLK], 0.0).astype(BF16)
            value = jnp.concatenate([qkv_ref[here, entry], one], 1)
            total = sums[h] + dot(near, value)
            den = total[:, wide : wide + 1]
            att = total[:, :wide] / den
            att_ref[here, entry] = att.astype(BF16)
            full_ref[here, entry] = att
            den_ref[here, h : h + 1] = den
        if b in turns:
            turns[b]()
    for copy in moves:
        copy.wait()
    if linked:
        gather.finish()


def attend_back_kernel(heads, wide, blocks, with_sum, *refs):
    qkv_ref, sc_ref, sr_ref, edge_ref, da_ref, full_ref, den_ref = refs[:7]
    refs = refs[7:]
    if with_sum:
        part_ref, e_ref, c_ref, act_ref, d_ref, o_ref, e_out_ref, c_out_ref, grad_ref = refs[:9]
        qz, vx, kt, near_dn, far_dn, qk_acc, v_acc = refs[9:16]
        mine, got, ex, ey, fx, fy, send, recv, local = refs[16:25]
        acts, load_act = refs[31:]
        whole = pltpu.make_async_copy(act_ref, acts, load_act)
        whole.start()
        flip = neighbours()[5]
        greet(everyone())
        s = Sum(
            mine, got, lambda k: part_ref.at[neighbours()[(4, 2, 3, 0)[k]] + flip], ex, ey, fx, fy, o_ref, send, recv
        )
        loads = [pltpu.make_async_copy(part_ref.at[s.order[k]], mine.at[k], local.at[k]) for k in range(4)]
        for k in range(4):
            s.swaps[k].start()
            loads[k].start()
        moved = [Exchange(c_ref, c_out_ref, *refs[28:31]), Exchange(e_ref, e_out_ref, *refs[25:28])]
        for one_move in moved:
            one_move.start()

        def first():
            loads[0].wait()
            s.over()

        def second():
            loads[1].wait()
            s.along_x()
            loads[2].wait()
            s.along_y()

        def fourth():
            loads[3].wait()
            s.own()

        turns = {blocks - 1: first, blocks - 2: second, blocks - 3: s.second, blocks - 4: fourth}
    else:
        d_ref, qz, vx, kt, near_dn, far_dn, qk_acc, v_acc = refs
        turns = {}
    lay_out(heads, wide, blocks, qkv_ref, edge_ref, qz, vx)

    @pl.loop(0, blocks)
    def _(b):
        kt[b] = qkv_ref[moving(b), heads * wide :].astype(F32).T.astype(BF16)

    qk_acc[...] = jnp.zeros_like(qk_acc)
    v_acc[...] = jnp.zeros_like(v_acc)
    one = (lax.broadcasted_iota(jnp.int32, (BLK, wide), 1) == 0).astype(F32)
    unit = one.astype(BF16)
    for b in reversed(range(blocks)):
        here = spot(b)
        for h in range(heads):
            entry = slice(h * wide, (h + 1) * wide)
            inv = 1.0 / den_ref[here, h : h + 1]
            da = da_ref[here, entry].astype(F32)
            dn = da * inv
            dd = -jnp.sum(dn * full_ref[here, entry], 1, keepdims=True)
            rows = slice(h * BLK, (h + 1) * BLK)
            near_dn[rows, :wide] = dn.astype(BF16)
            near_dn[rows, wide:] = (dd * one).astype(BF16)
            if b == blocks - 1:
                edge = edge_ref[here, :]
                far_dn[rows, :wide] = (dn * edge).astype(BF16)
                far_dn[rows, wide:] = (dd * edge * one).astype(BF16)

        far = far_dn if b == blocks - 1 else near_dn

        def pair(c, keys_t, grads, values, mask):
            t = dot_nt(qkv_ref[c, heads * wide :], qz[b]) + 1.0
            parts = []
            for h in range(heads):
                rows = slice(h * BLK, (h + 1) * BLK)
                t_h = t[:, rows]
                w = t_h * t_h + 1.0
                ds = dot_nt(values(h), grads[rows, :]) * t_h
                if mask is not None:
                    w = jnp.where(mask, w, 0.0)
                    ds = jnp.where(mask, ds, 0.0)
                parts.append(ds.astype(BF16))
                v_acc[c, h * wide : (h + 1) * wide] += dot(w.astype(BF16), grads[rows, :wide])
            ds = jnp.concatenate(parts, 1)
            qk_acc[c, :] += dot(ds, qz[b])
            return dot(keys_t, ds)

        def step(c, dq):
            at = moving(c)
            return dq + pair(at, kt[c], far, lambda h: vx[h, at, :], None)

        dq = lax.fori_loop(0, b, step, jnp.zeros((128, heads * BLK), F32))
        if b == 0:
            v_acc[here, :] = v_acc[here, :] * edge_ref[here, :]
        dq = dq + pair(
            here, kt[b], near_dn,
            lambda h: jnp.concatenate([qkv_ref[here, h * wide : (h + 1) * wide], unit], 1),
            later_or_same(sc_ref[here, :], sr_ref[b]),
        )
        row = lax.broadcasted_iota(jnp.int32, (128, BLK), 0)
        total = jnp.zeros((128, BLK), F32)
        for h in range(heads):
            at = (heads + h) * FEAT
            own = (row >= at) & (row < at + FEAT)
            total = jnp.where(own, dq[:, h * BLK : (h + 1) * BLK], total)
        total = total.T
        back = pltpu.roll(total, 128 - heads * FEAT, 1) * 0.5
        d_ref[here, heads * wide :] = back.astype(BF16)
        if b in turns:
            turns[b]()
    for b in range(blocks):
        here = spot(b)
        d_ref[here, : heads * wide] = v_acc[here, :].astype(BF16)
        queries = d_ref[here, heads * wide :].astype(F32)
        d_ref[here, heads * wide :] = (queries + 2.0 * qk_acc[here, :]).astype(BF16)
    if with_sum:
        whole.wait()

        @pl.loop(0, acts.shape[1] // 256)
        def _(n):
            part = pl.ds(pl.multiple_of(n * 256, 256), 256)
            grad_ref[part, :] = dot_tn(acts[:, part], d_ref[...]).astype(BF16)

        s.finish()
        for one_move in moved:
            one_move.finish()


def marks(seg):
    length = seg.shape[0]
    edge = (seg == seg[BLK - 1]).astype(F32)
    return seg[:, None], seg.reshape(length // BLK, 1, BLK), edge[:, None]


def attend(x_all, gain, mats, seg, heads, wide, dt, cot, cid):
    length, width = x_all.shape
    blocks = length // BLK
    part = heads * wide
    columns = mats.shape[1] - part
    linked = lax.axis_size("fsdp") == 8
    dma = pltpu.SemaphoreType.DMA
    args = [x_all, gain[None, :], mats, *marks(seg)]
    specs = [ANY, WHOLE, ANY, WHOLE, WHOLE, WHOLE]
    outs = [
        jax.ShapeDtypeStruct((length, columns), BF16),
        jax.ShapeDtypeStruct((length, part), BF16),
        jax.ShapeDtypeStruct((length, part), F32),
        jax.ShapeDtypeStruct((length, heads), F32),
        jax.ShapeDtypeStruct((length, width), BF16),
    ]
    out_specs = [WHOLE] * 4 + [ANY]
    scratch = [
        VMEM((2, BLK, width), BF16), VMEM((2, BLK, width), BF16), VMEM((width, columns), BF16),
        dma((2,)), dma((2,)), dma(()),
        VMEM((blocks, heads * BLK, 128), BF16), VMEM((heads, length, 2 * wide), BF16),
    ]
    params = dict(vmem_limit_bytes=48 << 20)
    if linked:
        args += [dt, cot]
        specs += [ANY, ANY]
        outs += [
            jax.ShapeDtypeStruct(dt.shape, BF16),
            jax.ShapeDtypeStruct((part, width), BF16),
            jax.ShapeDtypeStruct((8,) + cot.shape, BF16),
        ]
        out_specs += [ANY] * 3
        scratch += [dma((7,))] * 4 + [dma((2,))] + gather_scratch()
        params.update(collective_id=cid, has_side_effects=True)
    got = pl.pallas_call(
        functools.partial(attend_kernel, heads, wide, blocks, linked),
        out_shape=outs,
        in_specs=specs,
        out_specs=out_specs,
        scratch_shapes=scratch,
        compiler_params=pltpu.CompilerParams(**params),
        cost_estimate=LINKED,
        name="attend",
    )(*args)
    if linked:
        return *got[:7], got[7].reshape(length, width)
    return (
        *got,
        lax.all_to_all(dt, "fsdp", 0, 0, tiled=True),
        lax.all_to_all(mats[:, columns:], "fsdp", 0, 1, tiled=True),
        lax.all_gather(cot, "fsdp", axis=0, tiled=True),
    )


def attend_back(qkv, seg, heads, wide, da, full, den, part, moved, across, act, cid):
    length, columns = qkv.shape
    blocks = length // BLK
    width = heads * wide
    with_sum = lax.axis_size("fsdp") == 8
    args = [qkv, *marks(seg), da, full, den]
    specs = [WHOLE] * 7
    outs = [jax.ShapeDtypeStruct((length, columns), BF16)]
    scratch = [
        VMEM((blocks, heads * BLK, 128), BF16), VMEM((heads, length, 2 * wide), BF16),
        VMEM((blocks, 128, BLK), BF16), VMEM((heads * BLK, 2 * wide), BF16), VMEM((heads * BLK, 2 * wide), BF16),
        VMEM((length, 128), F32), VMEM((length, width), F32),
    ]
    if with_sum:
        rows, cols = length // 8, part.shape[1]
        args += [part.reshape(8, rows, cols), moved, across, act]
        specs += [ANY] * 4
        outs += [
            jax.ShapeDtypeStruct((rows, cols), F32),
            jax.ShapeDtypeStruct(moved.shape, moved.dtype),
            jax.ShapeDtypeStruct((8, across.shape[0], across.shape[1] // 8), across.dtype),
            jax.ShapeDtypeStruct((act.shape[1], columns), BF16),
        ]
        scratch += sum_scratch(rows, cols) + [pltpu.SemaphoreType.DMA((4,))] + 2 * exchange_scratch()
        scratch += [VMEM(act.shape, BF16), pltpu.SemaphoreType.DMA(())]
        params = pltpu.CompilerParams(
            vmem_limit_bytes=60 << 20, collective_id=cid, has_side_effects=True
        )
    else:
        params = pltpu.CompilerParams(vmem_limit_bytes=60 << 20)
    got = pl.pallas_call(
        functools.partial(attend_back_kernel, heads, wide, blocks, with_sum),
        out_shape=outs,
        in_specs=specs,
        out_specs=[WHOLE, WHOLE, ANY, ANY, WHOLE][: len(outs)],
        scratch_shapes=scratch,
        compiler_params=params,
        cost_estimate=LINKED,
        name="attend_back",
    )(*args)
    if with_sum:
        return *got[:3], got[3].reshape(-1, got[3].shape[2]), got[4]
    return (
        got[0],
        lax.psum_scatter(part, "fsdp", scatter_dimension=0, tiled=True).astype(F32),
        lax.all_to_all(moved, "fsdp", 0, 0, tiled=True),
        lax.all_to_all(across, "fsdp", 1, 0, tiled=True),
        dot_tn(act, got[0]).astype(BF16),
    )


class Exchange:
    def __init__(self, x_ref, o_ref, send, recv, local):
        me = lax.axis_index("fsdp")
        cols = o_ref.shape[2]

        def block(to):
            if len(x_ref.shape) == 3:
                return x_ref.at[to]
            return x_ref.at[:, pl.ds(pl.multiple_of(to * cols, cols), cols)]

        self.copies = [
            push(block(to), o_ref.at[me], send.at[r], recv.at[r], to) for r, to in enumerate(everyone())
        ] + [pltpu.make_async_copy(block(me), o_ref.at[me], local)]

    def start(self):
        for copy in self.copies:
            copy.start()

    def finish(self):
        for copy in self.copies:
            copy.wait()


def exchange_scratch():
    dma = pltpu.SemaphoreType.DMA
    return [dma((7,)), dma((7,)), dma(())]


def everyone():
    me = lax.axis_index("fsdp")
    return [lax.rem(me + r, 8) for r in range(1, 8)]


def tiles(cols):
    return [pl.ds(at, min(256, cols - at)) for at in range(0, cols, 256)]


def gated(gate, up):
    return gate * jax.nn.sigmoid(gate) * up


def gated_back(grad, gate, up):
    sigma = jax.nn.sigmoid(gate)
    return grad * up * sigma * (1.0 + gate * (1.0 - sigma)), grad * gate * sigma


def lane_index(rows):
    return lax.broadcasted_iota(jnp.int32, (rows, 128), 1)


def feed_kernel(
    ff, cot_ref, act_ref, w_ref, act_all_ref, gu_ref, hid_ref, grad_ref,
    acts, gus, hid, cots, acc, load, save_gu, save_hid, save_act, send, recv, local,
):
    me, sib, xn, yn, dg, flip = neighbours()
    rows = act_ref.shape[0]
    main = ff // 128 * 128
    tail = ff - main
    order = [me, sib, xn, yn, xn + flip, yn + flip, dg, dg + flip]
    cot_load = pltpu.make_async_copy(cot_ref, cots, load)
    cot_load.start()
    greet([sib, xn, yn])
    g = Gather(act_ref, acts, send, recv, local)
    g.start()

    def keep_gu(k):
        at = pl.ds(pl.multiple_of(order[k] * rows, rows), rows)
        return pltpu.make_async_copy(gus.at[k % 2], gu_ref.at[at], save_gu.at[k % 2])

    def work(k):
        q = order[k]
        if k >= 2:
            keep_gu(k - 2).wait()
        gu = gus.at[k % 2]
        for tile in tiles(w_ref.shape[1]):
            gu[:, tile] = dot(acts[q], w_ref[:, tile])
        hid[q, :, :main] = gated(gu[:, :main], gu[:, main : 2 * main]).astype(BF16)
        last = gu[:, 2 * main :]
        value = gated(last, pltpu.roll(last, 128 - tail, 1))
        hid[q, :, main:] = jnp.where(lane_index(rows) < tail, value, 0.0).astype(BF16)
        keep_gu(k).start()

    def product(first, second, here):
        return dot_tn(cots[first, :, here], hid[first]) + dot_tn(cots[second, :, here], hid[second])

    def add(first, second, start):
        @pl.loop(0, acc.shape[0] // 256)
        def _(n):
            here = pl.ds(pl.multiple_of(n * 256, 256), 256)
            value = product(first, second, here)
            acc[here, :] = value if start else acc[here, :] + value

    g.keep.wait()
    work(0)
    g.whole.wait_recv()
    work(1)
    g.turn()
    cot_load.wait()
    add(me, sib, True)
    g.rest()
    work(2)
    work(3)
    for k in range(4):
        g.core[k].wait_recv()
    work(4)
    g.across()
    work(5)
    add(xn, xn + flip, False)
    add(yn, yn + flip, False)
    work(6)
    g.core[4].wait_recv()
    g.core[5].wait_recv()
    store_act = pltpu.make_async_copy(acts, act_all_ref, save_act)
    store_act.start()
    work(7)
    store = pltpu.make_async_copy(hid, hid_ref, save_hid)
    store.start()

    @pl.loop(0, acc.shape[0] // 256)
    def _(n):
        here = pl.ds(pl.multiple_of(n * 256, 256), 256)
        grad_ref[here, :] = (acc[here, :] + product(dg, dg + flip, here)).astype(BF16)

    keep_gu(6).wait()
    keep_gu(7).wait()
    g.sent()
    store.wait()
    store_act.wait()


def feed(cot_all, act, w_gu, ff, cid):
    main = ff // 128 * 128
    tail = ff - main
    hid_cols = main + -(-tail // 128) * 128
    if lax.axis_size("fsdp") != 8:
        act = lax.all_gather(act, "fsdp", axis=0, tiled=True)
        gu = dot(act, w_gu)
        gate = jnp.concatenate([gu[:, :main], gu[:, 2 * main : 2 * main + tail]], 1)
        up = jnp.concatenate([gu[:, main : 2 * main], gu[:, 2 * main + tail : 2 * ff]], 1)
        hidden = jnp.pad(gated(gate, up), ((0, 0), (0, hid_cols - ff))).astype(BF16)
        return act, gu, hidden, dot_tn(cot_all, hidden).astype(BF16)
    rows, width = act.shape
    gu_cols = w_gu.shape[1]
    dma = pltpu.SemaphoreType.DMA
    act_all, gu, hidden, grad = pl.pallas_call(
        functools.partial(feed_kernel, ff),
        out_shape=(
            jax.ShapeDtypeStruct((8, rows, width), BF16),
            jax.ShapeDtypeStruct((8 * rows, gu_cols), F32),
            jax.ShapeDtypeStruct((8, rows, hid_cols), BF16),
            jax.ShapeDtypeStruct((width, hid_cols), BF16),
        ),
        in_specs=[ANY, ANY, WHOLE],
        out_specs=(ANY, ANY, ANY, WHOLE),
        scratch_shapes=[
            VMEM((8, rows, width), BF16), VMEM((2, rows, gu_cols), F32), VMEM((8, rows, hid_cols), BF16),
            VMEM((8, rows, width), BF16), VMEM((width, hid_cols), F32),
            dma(()), dma((2,)), dma(()), dma(()),
        ] + gather_scratch(),
        compiler_params=pltpu.CompilerParams(
            collective_id=cid, has_side_effects=True, vmem_limit_bytes=56 << 20
        ),
        cost_estimate=LINKED,
        name="feed",
    )(cot_all.reshape(8, rows, width), act, w_gu)
    return act_all.reshape(-1, width), gu, hidden.reshape(-1, hid_cols), grad


def feed_back_kernel(
    ff, cot_ref, gu_ref, act_ref, w_ref, d_ref, o_ref, grad_ref,
    acts, cots, gus, dh, dgu, out, load_act, load_cot, load_gu, mine, got, ex, ey, fx, fy, send, recv,
):
    me, sib, xn, yn, dg, flip = neighbours()
    rows, cols = o_ref.shape
    main = ff // 128 * 128
    tail = ff - main
    order = [dg + flip, dg, xn + flip, xn, yn + flip, yn, me + flip, me]

    def fetch(k):
        q, slot = order[k], k % 2
        return [
            pltpu.make_async_copy(cot_ref.at[q], cots.at[slot], load_cot.at[slot]),
            pltpu.make_async_copy(gu_ref.at[q], gus.at[slot], load_gu.at[slot]),
        ]

    for copy in fetch(0):
        copy.start()
    whole = pltpu.make_async_copy(act_ref, acts, load_act)
    whole.start()
    greet([sib, xn, yn])
    s = Sum(mine, got, out.at.__getitem__, ex, ey, fx, fy, o_ref, send, recv)

    def block(k, to):
        if k < 7:
            for copy in fetch(k + 1):
                copy.start()
        for copy in fetch(k):
            copy.wait()
        slot, q = k % 2, order[k]
        gu = gus.at[slot]
        for tile in tiles(d_ref.shape[1]):
            dh[:, tile] = dot(cots[slot], d_ref[:, tile])
        here = pl.ds(pl.multiple_of(q * rows, rows), rows)
        d_gate, d_up = gated_back(dh[:, :main], gu[:, :main], gu[:, main : 2 * main])
        dgu[here, :main] = d_gate.astype(BF16)
        dgu[here, main : 2 * main] = d_up.astype(BF16)
        last = gu[:, 2 * main :]
        d_gate, d_up = gated_back(dh[:, main:], last, pltpu.roll(last, 128 - tail, 1))
        lane = lane_index(rows)
        both = jnp.where(lane < tail, d_gate, jnp.where(lane < 2 * tail, pltpu.roll(d_up, tail, 1), 0.0))
        dgu[here, 2 * main :] = both.astype(BF16)

        @pl.loop(0, cols // 256)
        def _(n):
            part = pl.ds(pl.multiple_of(n * 256, 256), 256)
            to[:, part] = dot_nt(dgu[here, :], w_ref[part, :]).astype(BF16)

    def away(k):
        block(2 * k, out.at[k])
        s.swaps[k].start()

    def home(k):
        block(2 * k + 1, mine.at[k])

    away(0)
    home(0)
    s.over()
    away(1)
    home(1)
    s.along_x()
    away(2)
    home(2)
    s.along_y()
    s.second()
    away(3)
    home(3)
    s.own()
    whole.wait()

    @pl.loop(0, cols // 256)
    def _(n):
        part = pl.ds(pl.multiple_of(n * 256, 256), 256)
        grad_ref[part, :] = dot_tn(acts[:, part], dgu[...]).astype(BF16)

    s.finish()


def feed_back(cot_all, gu, act, w_gu, w_dt, ff, cid):
    main = ff // 128 * 128
    tail = ff - main
    if lax.axis_size("fsdp") != 8:
        gate = jnp.concatenate([gu[:, :main], gu[:, 2 * main : 2 * main + tail]], 1)
        up = jnp.concatenate([gu[:, main : 2 * main], gu[:, 2 * main + tail : 2 * ff]], 1)
        d_gate, d_up = gated_back(dot(cot_all, w_dt)[:, :ff], gate, up)
        d_gu = jnp.concatenate(
            [d_gate[:, :main], d_up[:, :main], d_gate[:, main:], d_up[:, main:],
             jnp.zeros((gu.shape[0], gu.shape[1] - 2 * ff), F32)], 1
        ).astype(BF16)
        part = lax.psum_scatter(
            dot_nt(d_gu, w_gu).astype(BF16), "fsdp", scatter_dimension=0, tiled=True
        )
        return part.astype(F32), dot_tn(act, d_gu).astype(BF16)
    length, width = act.shape
    rows, gu_cols, hid_cols = length // 8, gu.shape[1], w_dt.shape[1]
    dma = pltpu.SemaphoreType.DMA
    return pl.pallas_call(
        functools.partial(feed_back_kernel, ff),
        out_shape=(
            jax.ShapeDtypeStruct((rows, width), F32),
            jax.ShapeDtypeStruct((width, gu_cols), BF16),
        ),
        in_specs=[ANY, ANY, ANY, WHOLE, WHOLE],
        out_specs=(WHOLE, WHOLE),
        scratch_shapes=[
            VMEM((length, width), BF16), VMEM((2, rows, width), BF16), VMEM((2, rows, gu_cols), F32),
            VMEM((rows, hid_cols), F32), VMEM((length, gu_cols), BF16), VMEM((4, rows, width), BF16),
            dma(()), dma((2,)), dma((2,)),
        ] + sum_scratch(rows, width),
        compiler_params=pltpu.CompilerParams(
            collective_id=cid, has_side_effects=True, vmem_limit_bytes=61 << 20
        ),
        cost_estimate=LINKED,
        name="feed_back",
    )(cot_all.reshape(8, rows, width), gu.reshape(8, rows, gu_cols), act, w_gu, w_dt)


def project_back_kernel(
    p_ref, hid_ref, d_ref, w_ref, mix_ref, att_ref, part_ref, grad_ref,
    rowed, parts, acc, save, send, recv, local,
):
    me, sib, xn, yn, dg, flip = neighbours()
    rows, cols = p_ref.shape
    greet([sib, xn, yn])
    g = Gather(p_ref, rowed, send, recv, local)
    g.start()

    def side(lo, hi):
        @pl.loop(lo, hi)
        def _(b):
            left = hid_ref[pl.ds(pl.multiple_of(b * rows, rows), rows), :]
            for tile in tiles(cols):
                parts[b, :, tile] = dot_nt(left, d_ref[tile, :]).astype(BF16)

    def use(q, start):
        at = pl.ds(pl.multiple_of(q * rows, rows), rows)
        att_ref[at, :] = dot_nt(rowed[q], w_ref[...]).astype(BF16)
        left = mix_ref[at, :]
        for tile in tiles(cols):
            value = dot_tn(left, rowed[q, :, tile])
            acc[:, tile] = value if start else acc[:, tile] + value

    side(0, 5)
    g.turn()
    side(5, 8)
    store = pltpu.make_async_copy(parts, part_ref, save)
    store.start()
    g.keep.wait()
    use(me, True)
    g.whole.wait_recv()
    use(sib, False)
    g.rest()
    use(xn, False)
    use(yn, False)
    g.across()
    use(dg, False)
    for k in range(4):
        g.core[k].wait_recv()
    use(xn + flip, False)
    use(yn + flip, False)
    g.core[4].wait_recv()
    g.core[5].wait_recv()
    use(dg + flip, False)
    grad_ref[...] = acc[...].astype(BF16)
    g.sent()
    store.wait()


def project_back(d_proj, hidden, w_dt, w_o, mixed, cid):
    if lax.axis_size("fsdp") != 8:
        d_proj = lax.all_gather(d_proj, "fsdp", axis=0, tiled=True)
        return (
            dot_nt(d_proj, w_o).astype(BF16),
            dot_nt(hidden, w_dt).astype(BF16),
            dot_tn(mixed, d_proj).astype(BF16),
        )
    rows, width = d_proj.shape
    own = w_o.shape[0]
    att, part, grad = pl.pallas_call(
        project_back_kernel,
        out_shape=(
            jax.ShapeDtypeStruct((8 * rows, own), BF16),
            jax.ShapeDtypeStruct((8, rows, width), BF16),
            jax.ShapeDtypeStruct((own, width), BF16),
        ),
        in_specs=[ANY] + [WHOLE] * 4,
        out_specs=(WHOLE, ANY, WHOLE),
        scratch_shapes=[
            VMEM((8, rows, width), BF16), VMEM((8, rows, width), BF16), VMEM((own, width), F32),
            pltpu.SemaphoreType.DMA(()),
        ] + gather_scratch(),
        compiler_params=pltpu.CompilerParams(
            collective_id=cid, has_side_effects=True, vmem_limit_bytes=50 << 20
        ),
        cost_estimate=LINKED,
        name="project_back",
    )(d_proj, hidden, w_dt, w_o, mixed)
    return att, part.reshape(8 * rows, width), grad


def group(arrays, groups):
    parts = jnp.concatenate([a.reshape(a.shape[0], groups, -1) for a in arrays], -1)
    return jnp.transpose(parts, (1, 0, 2))


def over_rows(own):
    return lax.all_gather(own.reshape(-1, own.shape[-1]), "dp", axis=0, tiled=True)


def sum_rows(array):
    return lax.psum_scatter(array, "dp", scatter_dimension=0, tiled=True)


def to_owners(part, groups):
    part = part.reshape(groups, part.shape[0] // groups, -1)
    return jnp.transpose(lax.all_to_all(part, "fsdp", 0, 0, tiled=True), (1, 0, 2)).astype(F32)


def columns(array, lo, hi):
    return array[:, :, lo:hi].reshape(array.shape[0], -1)


def after(value, *others):
    return lax.optimization_barrier((value,) + others)[0]


def on_device(
    layer_input, doc_starts, norm1_gain, w_query, w_key, w_value, w_out, norm2_gain,
    w_gate, w_up, w_down, cotangent,
):
    n_f = lax.axis_size("fsdp")
    x = layer_input[0]
    cot = cotangent[0]
    tokens, width = x.shape
    length = tokens * n_f
    kv = w_query.shape[1]
    rows = w_query.shape[0]
    ff = w_gate.shape[1]
    ff_own, qk_own, v_own = ff // n_f, kv // n_f, width // n_f
    heads = qk_own // FEAT
    wide = v_own // heads
    used = v_own + 2 * qk_own
    gain_at = used
    qkv_cols = v_own + 128
    att_cols = qkv_cols + v_own

    def blocked(a):
        return a.reshape(n_f, a.shape[0] // n_f, a.shape[1])

    def each(vec):
        return jnp.broadcast_to(vec[:, None, None], (rows, n_f, 1))

    attn = group(
        [w_value, w_query, w_key, each(norm1_gain), each(norm2_gain),
         jnp.zeros((rows, n_f, qkv_cols - used - 2), BF16), w_out],
        n_f,
    )
    attn = over_rows(lax.all_to_all(attn, "fsdp", 0, 0, tiled=True))
    main = ff_own // 128 * 128

    def halves(a):
        return a[:, : n_f * main].reshape(rows, n_f, main), a[:, n_f * main :].reshape(rows, n_f, -1)

    (gate_main, gate_tail), (up_main, up_tail) = halves(w_gate), halves(w_up)
    empty = jnp.zeros((rows, n_f, 128), BF16)
    gu = group(
        [gate_main, up_main, gate_tail, up_tail, empty[:, :, : -(2 * ff_own) % 128]], n_f
    )
    x_all, gu_part = start_exchange(x, gu, 0)
    w_gu = over_rows(gu_part)
    dt = group([*halves(w_down.T), empty[:, :, : -ff_own % 128]], n_f)
    gain_one = attn[:, gain_at].astype(F32)
    gain_two = attn[:, gain_at + 1].astype(F32)
    places = jnp.arange(length, dtype=jnp.int32)
    seg = jnp.sum((doc_starts[0][None, :] <= places[:, None]).astype(jnp.int32), 1)
    qkv, mixed, full, den, act_one, dt_part, w_o, cot_all = attend(
        x_all, gain_one, attn, seg, heads, wide, dt, cot, 3
    )
    w_dt = over_rows(dt_part)
    resid, act_two = product_sum(mixed, w_o, False, 2, x, gain_two)
    factor_two = lax.rsqrt(jnp.mean(resid * resid, -1, keepdims=True) + EPS)
    act_two, gate_up, hidden, g_dt = feed(cot_all, act_two, w_gu, ff_own, 1)
    d_act_two, g_gu = feed_back(cot_all, gate_up, act_two, w_gu, w_dt, ff_own, 4)
    g_dt = sum_rows(g_dt)
    g_gu = sum_rows(after(g_gu, g_dt))

    d_norm, _ = rms_back(d_act_two, resid, factor_two, gain_two)
    d_resid = cot.astype(F32) + d_norm
    d_att, out_part, g_out = project_back(d_resid.astype(BF16), hidden, w_dt, w_o, mixed, 5)
    d_qkv, out_sum, g_dt, g_out, g_qkv = attend_back(
        qkv, seg, heads, wide, d_att, full, den, out_part, blocked(g_dt), g_out, act_one, 7
    )
    grad_input, grad_gate, grad_up, grad_dt, along = product_sum(
        after(d_qkv, g_qkv), attn, True, 6, x, gain_one, blocked(g_gu), g_dt, w_gu, ff_own
    )

    g_out = sum_rows(after(g_out, g_gu))
    g_qkv = sum_rows(after(g_qkv, g_gu))
    own_rows = lax.axis_index("dp") * (width // lax.axis_size("dp"))

    def mine(value):
        return lax.dynamic_slice_in_dim(value, own_rows, g_qkv.shape[0], 0)

    gains = jnp.stack(
        [
            jnp.sum(mine(attn)[:, :qkv_cols].astype(F32) * g_qkv.astype(F32), 1) / mine(gain_one),
            along[:, 0] / mine(gain_two),
        ],
        1,
    )
    filler = jnp.zeros((g_qkv.shape[0], qkv_cols - used - 2), BF16)
    g_attn = jnp.concatenate([g_qkv[:, :used], gains.astype(BF16), filler, g_out], 1)
    grad_input, grad_gate, grad_up, grad_dt, _ = lax.optimization_barrier(
        (grad_input, grad_gate, grad_up, grad_dt, g_attn)
    )
    g_attn = to_owners(g_attn, n_f)

    output = (resid + out_sum).astype(BF16)[None]
    return (
        output,
        (d_resid + grad_input)[None],
        jnp.sum(g_attn[:, :, gain_at], 1),
        columns(g_attn, v_own, v_own + qk_own),
        columns(g_attn, v_own + qk_own, used),
        columns(g_attn, 0, v_own),
        columns(g_attn, qkv_cols, att_cols),
        jnp.sum(g_attn[:, :, gain_at + 1], 1),
        grad_gate.astype(F32),
        grad_up.astype(F32),
        grad_dt.T.astype(F32),
    )


def solution(mesh):
    rows, cols = P(ALL, None), P(None, ALL)
    toks = P("dp", "fsdp", None)
    return jax.shard_map(
        on_device,
        mesh=mesh,
        in_specs=(toks, P("dp", None), P(ALL), rows, rows, rows, rows, P(ALL), rows, rows, cols, toks),
        out_specs=(toks, toks, P(ALL), rows, rows, rows, rows, P(ALL), rows, rows, cols),
        check_vma=False,
    )
```
